32 devices in a mesh: groups: 2 (over x), orb: 8 (over z, y), aux: 2 (over core).
Axes of the slice: x: 2, y: 2, z: 4, core: 2. Of those that a mesh axis runs over, the one named last changes fastest.
Arguments:
- blocks: bfloat16 [64, 576, 1024], P(('groups', 'orb'), None, 'aux'), parts along dimension 0, may hold values from -1.25 to 1.25
- virt_energy: bfloat16 [64, 576], P(('groups', 'orb')), parts along dimension 0, may hold values from 0.19921875 to 4
- occ_energy: float32 [64], P('groups'), parts along dimension 0, may hold values from -2 to -0.3
- owner_slot: int32 [64], P('groups'), parts along dimension 0, may hold values from 0 to 31, as said below
- pairs: int32 [512, 2], P(('groups', 'orb')), parts along dimension 0, may hold values from 0 to 31, as said below
- domains: int32 [512, 2, 512], P(('groups', 'orb')), parts along dimension 0, may hold values from 0 to 575, as said below
Outputs:
- amplitudes: bfloat16 [512, 512, 512], P(('groups', 'orb', 'aux')), parts along dimension 0
The draws below stay inside these ranges and needn't reach their ends.
There are 2 independent parts, one for each index of `groups`. The reference program is written for one: setup_inputs(seed, part) draws one part's arguments, and reference() takes and returns one part's arrays. A program takes and returns all parts, laid end to end along the dimension named above; each array names one. Nothing has to cross between parts.
Inputs may be any that keep to these rules, and one draw needn't show every extreme that they name: A permutation: orbital o is stored in slot owner_slot[o] of blocks and virt_energy. `pairs`: rows 8 * k to 8 * k + 7 share their first orbital, the one in slot k, so each aligned block of 32 rows has first orbitals stored in that block's 4 slots. The second orbital differs from the first and no pair repeats. Within one aligned block of 32 rows, at most 2 distinct second orbitals lie in any one block of 4 slots, and in every aligned block exactly 2 lie in some block of slots. `domains`: each row of 512 positions is strictly increasing.
All inputs are finite; a program needn't handle non-finite values.
Results may differ from the reference program's by a relative error of at most 0.001.
Values may be sent and summed in bfloat16 or wider, within the bound.
No kernel may reach another device: no remote copies, remote signals or barrier semaphores. Data moves between devices by JAX's collectives and lax.ppermute only.
A program may use at most 192 MiB of HBM per device.

```python
import math
import jax
import jax.numpy as jnp
from jax import lax

QF = 1024
VO = 576
DOM = 512
CAP = 2
PAIRS_PER = 8
OCC_DEV = 4
OCCUPIED_COUNT = 32
PAIRS = 256


def pair_layout(key):
    key_slot, key_order, key_count, key_local, key_score, key_center = jax.random.split(key, 6)
    orb_count = OCCUPIED_COUNT // OCC_DEV
    owner_slot = jax.random.permutation(key_slot, OCCUPIED_COUNT).astype(jnp.int32)
    orbital_of_slot = jnp.argsort(owner_slot).astype(jnp.int32)
    sure_count = -(-(PAIRS_PER + 1) // CAP)
    device_ids = jnp.arange(orb_count, dtype=jnp.int32)
    order_noise = jax.random.randint(key_order, (orb_count, orb_count), 0, 2 ** 20)
    order_noise = jnp.where(device_ids[:, None] == device_ids[None, :], 2 ** 21, order_noise)
    source_order = jnp.argsort(order_noise * orb_count + device_ids[None, :], axis=1)
    source_place = jnp.argsort(source_order, axis=1)
    random_count = jax.random.randint(key_count, (orb_count, orb_count), 0, CAP + 1)
    counts = jnp.where(source_place < sure_count, CAP, random_count)
    local_noise = jax.random.randint(key_local, (orb_count, orb_count, OCC_DEV), 0, 2 ** 20)
    local_pick = jnp.argsort(local_noise * OCC_DEV + jnp.arange(OCC_DEV, dtype=jnp.int32), axis=2)[:, :, :CAP]
    is_valid = jnp.arange(CAP)[None, None, :] < counts[:, :, None]
    companion_slot = device_ids[None, :, None] * OCC_DEV + local_pick
    forced_flag = (source_place == 0)[:, :, None] & is_valid
    width_all = orb_count * CAP
    companion_slot = companion_slot.reshape(orb_count, width_all)
    is_valid = is_valid.reshape(orb_count, width_all)
    forced_flag = forced_flag.reshape(orb_count, width_all)
    own_slot = device_ids[:, None] * OCC_DEV + jnp.arange(OCC_DEV, dtype=jnp.int32)[None, :]
    center_extra_score = jnp.where(jax.random.randint(key_center, (OCCUPIED_COUNT,), 0, 6) == 0, 2 ** 16, 0)
    unadjusted_score = jax.random.randint(key_score, (orb_count, OCC_DEV, width_all), 0, 2 ** 16)
    leading_local_slot = (jnp.arange(OCC_DEV) == 0)[None, :, None]
    pair_score = unadjusted_score + center_extra_score[companion_slot][:, None, :] + jnp.where(forced_flag[:, None, :] & leading_local_slot, 2 ** 18, 0)
    is_bad = ~is_valid[:, None, :] | (companion_slot[:, None, :] == own_slot[:, :, None])
    pair_score = jnp.where(is_bad, -1, pair_score)
    pair_score = pair_score * width_all + jnp.arange(width_all, dtype=jnp.int32)[None, None, :]
    chosen = jnp.argsort(-pair_score, axis=2)[:, :, :PAIRS_PER]
    every_partner = jnp.broadcast_to(companion_slot[:, None, :], (orb_count, OCC_DEV, width_all))
    second_slot = jnp.take_along_axis(every_partner, chosen, axis=2)
    first_slot = jnp.broadcast_to(own_slot[:, :, None], (orb_count, OCC_DEV, PAIRS_PER))
    pair_list = jnp.stack([orbital_of_slot[first_slot], orbital_of_slot[second_slot]], axis=-1)
    return (owner_slot, pair_list.reshape(PAIRS, 2).astype(jnp.int32))


def draw_owner_slot(key, part):
    return pair_layout(key)[0]


def draw_pairs(key, part):
    return pair_layout(key)[1]


def draw_domains(key, part):
    key = jax.random.fold_in(key, 7)
    noise = jax.random.randint(key, (PAIRS, 2, VO), 0, 2 ** 16)
    picked = jnp.argsort(noise * VO + jnp.arange(VO, dtype=jnp.int32), axis=2)[:, :, :DOM]
    return jnp.sort(picked, axis=2).astype(jnp.int32)


def block_scale(rng, extent, cuts, low, largest):
    level, own = 1.0, jax.random.fold_in(rng, 6)
    for position, parts in cuts:
        draws = jnp.exp(jax.random.uniform(jax.random.fold_in(own, position), (parts,), jnp.float32, low / len(cuts), largest / len(cuts)))
        level = level * jnp.repeat(draws, extent[position] // parts).reshape([-1 if axis == position else 1 for axis in range(len(extent))])
    return level


def centred(key, extent, spread, limit, cuts=(), held_as=jnp.bfloat16):
    array = jax.random.normal(key, extent, jnp.float32) * spread
    if len(cuts) > 0:
        array = block_scale(key, extent, cuts, -0.22, 0.18) * array
    return jnp.clip(array, min=-limit, max=limit).astype(held_as)


def setup_inputs(seed: int = 0, part: int = 0) -> dict:
    key_list = jax.random.split(jax.random.key(seed), 7)
    part_splits = jax.random.split(jax.random.fold_in(key_list[6], part), 7)
    blocks = centred(part_splits[0], (OCCUPIED_COUNT, VO, QF), 0.2, 1.25, ((0, 8), (2, 2)))
    virt_energy = jnp.clip(jnp.exp(math.log(4.0) - 2.9996462 * jax.random.uniform(part_splits[1], (OCCUPIED_COUNT, VO), jnp.float32) ** block_scale(part_splits[1], (OCCUPIED_COUNT, VO), ((0, 8),), -0.2, 0.2)), 0.19921875, 4.0).astype(jnp.bfloat16)
    occ_energy = jnp.clip(jax.random.uniform(part_splits[2], (OCCUPIED_COUNT,), jnp.float32, -2.0, -0.3), -2.0, -0.3)
    owner_slot = draw_owner_slot(jax.random.fold_in(jax.random.fold_in(key_list[6], part), 71), part)
    pairs = draw_pairs(jax.random.fold_in(jax.random.fold_in(key_list[6], part), 71), part)
    domains = draw_domains(jax.random.fold_in(jax.random.fold_in(key_list[6], part), 71), part)
    return {"blocks": blocks, "virt_energy": virt_energy, "occ_energy": occ_energy, "owner_slot": owner_slot, "pairs": pairs, "domains": domains}


def reference(blocks, virt_energy, occ_energy, owner_slot, pairs, domains):
    first_slot = owner_slot[pairs[:, 0]]
    second_slot = owner_slot[pairs[:, 1]]
    occ_shift = occ_energy[pairs[:, 0]] + occ_energy[pairs[:, 1]]

    def one_pair(pair_items):
        slot_one, slot_two, cols_one, cols_two, shift_value = pair_items
        chosen_one = jnp.take(blocks[slot_one], cols_one, axis=0)
        chosen_two = jnp.take(blocks[slot_two], cols_two, axis=0)
        integral = jnp.dot(chosen_one, chosen_two.T, preferred_element_type=jnp.float32)
        energy_one = jnp.take(virt_energy[slot_one], cols_one).astype(jnp.float32)
        energy_two = jnp.take(virt_energy[slot_two], cols_two).astype(jnp.float32)
        denominator = energy_one[:, None] + energy_two[None, :] - shift_value
        return (-integral / denominator).astype(jnp.bfloat16)

    return lax.map(one_pair, (first_slot, second_slot, domains[:, 0, :], domains[:, 1, :], occ_shift))
```

```python
import functools

import jax
import jax.numpy as jnp
from jax import lax
from jax.experimental import pallas as pl
from jax.experimental.pallas import tpu as pltpu
from jax.sharding import PartitionSpec as P

NT = (((1,), (1,)), ((), ()))


def windows(full, kept):
    slack = full - kept
    tile = 256 - slack if 0 <= slack <= 128 else kept
    found = []
    base = 0
    while base < kept:
        rows = min(tile, kept - base)
        found.append((base, rows, rows + slack))
        base += rows
    return found


def pair_kernel(
    call, wins, has_prev,
    meta_ref, shift_ref, dom_ref, ve1_ref, ve2_ref,
    own_ref, other_ref, a_own, a_other, b_own, b_other, *rest,
):
    if has_prev:
        rest = rest[1:]
    out_ref, first, second, side_a, side_b, e1_buf, out_buf, first_sem, second_sem, out_sem = rest
    pairs_here = out_ref.shape[0]
    kept = out_ref.shape[1]
    half = own_ref.shape[2]
    n_first = first.shape[0]
    lo = meta_ref[0, call]
    hi = meta_ref[0, call + 1]
    base_first = meta_ref[1, 0]

    def first_copies():
        out = []
        for k in range(n_first):
            out.append(pltpu.make_async_copy(
                own_ref.at[base_first + k], first.at[k, :, pl.ds(0, half)], first_sem.at[2 * k]))
            out.append(pltpu.make_async_copy(
                other_ref.at[base_first + k], first.at[k, :, pl.ds(half, half)], first_sem.at[2 * k + 1]))
        return out

    def fetch(i, slot):
        p = meta_ref[2, i]
        which = meta_ref[3, p]
        idx = meta_ref[4, p]

        def go(x_own, x_other):
            pltpu.make_async_copy(
                x_own.at[idx], second.at[slot, :, pl.ds(0, half)], second_sem.at[slot, 0]).start()
            pltpu.make_async_copy(
                x_other.at[idx], second.at[slot, :, pl.ds(half, half)], second_sem.at[slot, 1]).start()

        @pl.when(which == 0)
        def _():
            go(a_own, a_other)

        @pl.when(which == 1)
        def _():
            go(b_own, b_other)

    def await_fetch(slot):
        for k in range(2):
            pltpu.make_async_copy(
                a_own.at[0], second.at[slot, :, pl.ds(k * half, half)], second_sem.at[slot, k]).wait()

    def out_copy(p, slot):
        return pltpu.make_async_copy(out_buf.at[slot], out_ref.at[p], out_sem.at[slot])

    @pl.when(hi > lo)
    def _():
        for c in first_copies():
            c.start()
        fetch(lo, lax.rem(lo, 2))
        for c in first_copies():
            c.wait()

    lanes = lax.broadcasted_iota(jnp.int32, (kept, 128), 1)

    def step(i, carry):
        slot = lax.rem(i, 2)
        p = meta_ref[2, i]
        f = p // (pairs_here // n_first)

        @pl.when(i + 1 < hi)
        def _():
            fetch(i + 1, 1 - slot)

        def chosen(side):
            wanted = jnp.where(lanes == 2 * p + side, dom_ref[...], 0.0)
            return jnp.sum(wanted, axis=1, keepdims=True)

        cols1 = chosen(0)
        cols2 = chosen(1)
        for base, rows, span in wins:
            kk = lax.broadcasted_iota(jnp.int32, (rows, span), 1).astype(jnp.float32) + float(base)
            hit = cols1[base:base + rows] == kk
            ve = ve1_ref[p, :, base:base + span]
            e1 = jnp.sum(jnp.where(hit, ve, 0.0), axis=1, keepdims=True)
            e1_buf[base:base + rows, :] = jnp.broadcast_to(e1, (rows, 128))
            pick = jnp.where(hit, 1.0, 0.0).astype(jnp.bfloat16)
            got = jnp.dot(pick, first[f, base:base + span, :], preferred_element_type=jnp.float32)
            side_a[base:base + rows, :] = got.astype(jnp.bfloat16)
        await_fetch(slot)
        e2_parts = []
        for base, rows, span in wins:
            kk = lax.broadcasted_iota(jnp.int32, (rows, span), 1).astype(jnp.float32) + float(base)
            hit = cols2[base:base + rows] == kk
            pick = jnp.where(hit, 1.0, 0.0).astype(jnp.bfloat16)
            got = jnp.dot(pick, second[slot, base:base + span, :], preferred_element_type=jnp.float32)
            side_b[base:base + rows, :] = got.astype(jnp.bfloat16)
            ve = jnp.broadcast_to(ve2_ref[p, :, base:base + span], (8, span)).astype(jnp.bfloat16)
            e2_parts.append(
                lax.dot_general(ve, pick, NT, preferred_element_type=jnp.float32)[0:1])
        e2 = jnp.concatenate(e2_parts, axis=1)

        @pl.when(i >= lo + 2)
        def _():
            out_copy(p, slot).wait()

        shift = shift_ref[p]
        chunk = 256
        for r in range(0, kept, chunk):
            c = lax.dot_general(
                side_a[r:r + chunk, :], side_b[...], NT, preferred_element_type=jnp.float32)
            for col in range(0, kept, 128):
                den = e1_buf[r:r + chunk, :] + e2[:, col:col + 128] - shift
                inv = pl.reciprocal(den, approx=True)
                neg = inv * (den * inv - 2.0)
                out_buf[slot, r:r + chunk, col:col + 128] = (
                    c[:, col:col + 128] * neg).astype(jnp.bfloat16)
        out_copy(p, slot).start()
        return carry

    lax.fori_loop(lo, hi, step, 0)

    @pl.when(hi - lo >= 2)
    def _():
        out_copy(0, lax.rem(hi, 2)).wait()

    @pl.when(hi > lo)
    def _():
        out_copy(0, lax.rem(hi + 1, 2)).wait()


def run_pairs(call, expected, meta, shift, dom, ve1, ve2, own, other, col_arrays, opp_arrays, prev, n_first):
    pairs_here = ve1.shape[0]
    full, half = own.shape[1], own.shape[2]
    kept = dom.shape[0]
    wins = windows(full, kept)
    any_spec = pl.BlockSpec(memory_space=pl.ANY)
    smem = pl.BlockSpec(memory_space=pltpu.SMEM)
    vmem = pl.BlockSpec(memory_space=pltpu.VMEM)
    operands = [meta, shift, dom, ve1, ve2, own, other, *col_arrays, *opp_arrays]
    in_specs = [smem, smem, vmem, vmem, vmem] + [any_spec] * 6
    aliases = {}
    if prev is not None:
        aliases = {len(operands): 0}
        operands.append(prev)
        in_specs.append(any_spec)
    bf = jnp.bfloat16
    return pl.pallas_call(
        functools.partial(pair_kernel, call, wins, prev is not None),
        out_shape=jax.ShapeDtypeStruct((pairs_here, kept, kept), bf),
        in_specs=in_specs,
        out_specs=any_spec,
        scratch_shapes=[
            pltpu.VMEM((n_first, full, 2 * half), bf),
            pltpu.VMEM((2, full, 2 * half), bf),
            pltpu.VMEM((kept, 2 * half), bf),
            pltpu.VMEM((kept, 2 * half), bf),
            pltpu.VMEM((kept, 128), jnp.float32),
            pltpu.VMEM((2, kept, kept), bf),
            pltpu.SemaphoreType.DMA((2 * n_first,)),
            pltpu.SemaphoreType.DMA((2, 2)),
            pltpu.SemaphoreType.DMA((2,)),
        ],
        input_output_aliases=aliases,
        compiler_params=pltpu.CompilerParams(vmem_limit_bytes=40 * 1024 * 1024),
        cost_estimate=pl.CostEstimate(
            flops=int(expected * 4 * kept * kept * 2 * half * 2),
            bytes_accessed=int(expected * (full * half * 4 + kept * kept * 2)),
            transcendentals=0),
        name=f"pairs_{call}",
    )(*operands)


def picks(source, i0, i1):
    return [lax.dynamic_slice_in_dim(source, i0, 1, 0), lax.dynamic_slice_in_dim(source, i1, 1, 0)]


def per_device(blocks, virt_energy, occ_energy, owner_slot, pairs, domains):
    orb_count = lax.axis_size("orb")
    aux_count = lax.axis_size("aux")
    occ_dev, full, half = blocks.shape
    pair_dev = pairs.shape[0]
    kept = domains.shape[2]
    own_rows = pair_dev // aux_count
    n_first = occ_dev // aux_count
    core = lax.axis_index("aux")
    o = lax.axis_index("orb")
    z, y = o // 2, o % 2
    chain = orb_count // 2
    n_slots = orb_count * occ_dev

    def over(axis, perm, *arrays):
        got = [lax.ppermute(a, axis, perm) for a in arrays]
        return got if len(got) > 1 else got[0]

    swap_aux = [(0, 1), (1, 0)]
    swap_y = [(k, k ^ 1) for k in range(orb_count)]

    def down_perm(d):
        return [(k, k - 2) for k in range(2, orb_count) if k // 2 <= chain - d]

    def up_perm(d):
        return [(k, k + 2) for k in range(orb_count - 2) if k // 2 >= d - 1]

    downs, ups = [], []
    down, up = blocks, blocks
    for d in range(1, chain):
        down = over("orb", down_perm(d), down)
        up = over("orb", up_perm(d), up)
        downs.append(down)
        ups.append(up)
    local_other = over("aux", swap_aux, blocks)
    ve_all = lax.all_gather(virt_energy, "orb", axis=0, tiled=True)

    orbitals = jnp.arange(owner_slot.shape[0], dtype=jnp.int32)
    hit_second = pairs[:, 1][:, None] == orbitals[None, :]
    slot_second = jnp.sum(jnp.where(hit_second, owner_slot[None, :], 0), axis=1)
    slots = jnp.arange(n_slots, dtype=jnp.int32)
    wanted = jnp.any(slot_second[:, None] == slots[None, :], axis=0).reshape(orb_count, occ_dev)
    local = jnp.arange(occ_dev, dtype=jnp.int32)[None, :]
    want_lo = jnp.min(jnp.where(wanted, local, occ_dev - 1), axis=1)
    want_hi = jnp.max(jnp.where(wanted, local, 0), axis=1)
    want = jnp.stack([want_lo, want_hi])
    want_opp = over("orb", swap_y, want)

    first_row = core * own_rows
    own_second = lax.dynamic_slice_in_dim(slot_second, first_row, own_rows, 0)
    own_pairs = lax.dynamic_slice_in_dim(pairs, first_row, own_rows, 0)
    src = own_second // occ_dev
    part = own_second % occ_dev
    rank = jnp.any(
        (slot_second[None, :] // occ_dev == src[:, None]) & (slot_second[None, :] < own_second[:, None]),
        axis=1).astype(jnp.int32)
    src_z, src_y = src // 2, src % 2
    dist = jnp.abs(src_z - z)
    is_opp = (src_y != y).astype(jnp.int32)
    from_up = src_z < z
    both = 2 * dist <= chain - 1
    idx = jnp.where(
        dist == 0,
        jnp.where(is_opp == 1, rank, part),
        rank + jnp.where(both & from_up, 2, 0))
    rows = jnp.arange(own_rows, dtype=jnp.int32)
    before = (dist[None, :] < dist[:, None]) | ((dist[None, :] == dist[:, None]) & (rows[None, :] < rows[:, None]))
    place = jnp.sum(before.astype(jnp.int32), axis=1)
    order = jnp.sum(jnp.where(place[None, :] == rows[:, None], rows[None, :], 0), axis=1)
    bounds = jnp.sum((dist[None, :] < jnp.arange(chain + 1, dtype=jnp.int32)[:, None]).astype(jnp.int32), axis=1)
    width = max(own_rows, chain + 1)

    def padded(v):
        v = v.reshape(-1)
        return jnp.pad(v, (0, width - v.shape[0]))

    meta = jnp.stack([padded(bounds), padded(core * n_first), padded(order), padded(is_opp), padded(idx)])

    def occ(col):
        hit = own_pairs[:, col][:, None] == orbitals[None, :]
        return jnp.sum(jnp.where(hit, occ_energy[None, :], 0.0), axis=1)

    shift = occ(0) + occ(1)
    first_slot = o * occ_dev + core * n_first + rows // (own_rows // n_first)

    def energies(slot):
        hit = (slot[:, None] == slots[None, :]).astype(jnp.bfloat16)
        rows_of = jnp.dot(hit, ve_all, preferred_element_type=jnp.float32)
        return rows_of.reshape(own_rows, 1, full)

    ve1, ve2 = energies(first_slot), energies(own_second)
    dom = lax.dynamic_slice_in_dim(domains, first_row, own_rows, 0)
    dom = dom.reshape(2 * own_rows, kept).T.astype(jnp.float32)
    dom = jnp.pad(dom, ((0, 0), (0, 128 - 2 * own_rows)))

    def idx_of(table, row, source):
        return lax.dynamic_index_in_dim(table[row], jnp.clip(source, 0, orb_count - 1), 0, keepdims=False)

    def chosen(arrays, table, sources):
        got = []
        for a, s in zip(arrays, sources):
            got += picks(a, idx_of(table, 0, s), idx_of(table, 1, s))
        return jnp.concatenate(got, axis=0)

    y_own = over("orb", swap_y, chosen([blocks], want_opp, [o]))
    y_other = over("aux", swap_aux, y_own)
    out = run_pairs(
        0, own_rows / 4, meta, shift, dom, ve1, ve2, blocks, local_other,
        (blocks, local_other), (y_own, y_other), None, n_first)
    for d in range(1, chain):
        down, up = downs[d - 1], ups[d - 1]
        s_down, s_up = o + 2 * d, o - 2 * d
        if 2 * d <= chain - 1:
            mine = chosen([down, up], want, [s_down, s_up])
            theirs = chosen([down, up], want_opp, [s_down, s_up])
        else:
            is_down = z + d <= chain - 1
            s = jnp.where(is_down, s_down, s_up)
            mine = jnp.where(is_down, chosen([down], want, [s]), chosen([up], want, [s]))
            theirs = jnp.where(is_down, chosen([down], want_opp, [s]), chosen([up], want_opp, [s]))
        mine_other = over("aux", swap_aux, mine)
        opp_own = over("orb", swap_y, theirs)
        opp_other = over("aux", swap_aux, opp_own)
        out = run_pairs(
            d, own_rows / 4, meta, shift, dom, ve1, ve2, blocks, local_other,
            (mine, mine_other), (opp_own, opp_other), out, n_first)
    return out


def solution(mesh):
    in_specs = (
        P(("groups", "orb"), None, "aux"),
        P(("groups", "orb"), None),
        P("groups"),
        P("groups"),
        P(("groups", "orb"), None),
        P(("groups", "orb"), None, None),
    )
    out_specs = P(("groups", "orb", "aux"), None, None)
    return jax.shard_map(
        per_device, mesh=mesh, in_specs=in_specs, out_specs=out_specs, check_vma=False
    )
```

```python
import functools

import jax
import jax.numpy as jnp
from jax import lax
from jax.experimental import pallas as pl
from jax.experimental.pallas import tpu as pltpu
from jax.sharding import PartitionSpec as P

NT = (((1,), (1,)), ((), ()))


def windows(full, kept):
    slack = full - kept
    tile = 256 - slack if 0 <= slack <= 128 else kept
    found = []
    base = 0
    while base < kept:
        rows = min(tile, kept - base)
        found.append((base, rows, rows + slack))
        base += rows
    return found


def pair_kernel(call, wins, n_sets, has_prev, meta_ref, shift_ref, ve1_ref, ve2_ref, pick_ref, own_ref, other_ref, *rest):
    sets = [(rest[2 * k], rest[2 * k + 1]) for k in range(n_sets)]
    rest = rest[2 * n_sets + (1 if has_prev else 0):]
    (out_ref, first, second, pick, side_a, side_b, e1_buf, out_buf,
     first_sem, second_sem, pick_sem, out_sem) = rest
    pairs_here = out_ref.shape[0]
    kept = out_ref.shape[1]
    half = own_ref.shape[2]
    n_first = first.shape[0]
    lo = meta_ref[0, call]
    hi = meta_ref[0, call + 1]
    base_first = meta_ref[1, 0]

    def first_copies():
        out = []
        for k in range(n_first):
            out.append(pltpu.make_async_copy(
                own_ref.at[base_first + k], first.at[k, :, pl.ds(0, half)], first_sem.at[2 * k]))
            out.append(pltpu.make_async_copy(
                other_ref.at[base_first + k], first.at[k, :, pl.ds(half, half)], first_sem.at[2 * k + 1]))
        return out

    def fetch(i, slot):
        p = meta_ref[2, i]
        which = meta_ref[3, p]
        idx = meta_ref[4, p]
        pltpu.make_async_copy(pick_ref.at[p], pick.at[slot], pick_sem.at[slot]).start()
        for k, (x_own, x_other) in enumerate(sets):
            @pl.when(which == k)
            def _():
                pltpu.make_async_copy(
                    x_own.at[idx], second.at[slot, :, pl.ds(0, half)], second_sem.at[slot, 0]).start()
                pltpu.make_async_copy(
                    x_other.at[idx], second.at[slot, :, pl.ds(half, half)], second_sem.at[slot, 1]).start()

    def await_fetch(slot):
        pltpu.make_async_copy(pick_ref.at[0], pick.at[slot], pick_sem.at[slot]).wait()
        for k in range(2):
            pltpu.make_async_copy(
                sets[0][0].at[0], second.at[slot, :, pl.ds(k * half, half)], second_sem.at[slot, k]).wait()

    def out_copy(p, slot):
        return pltpu.make_async_copy(out_buf.at[slot], out_ref.at[p], out_sem.at[slot])

    @pl.when(hi > lo)
    def _():
        for c in first_copies():
            c.start()
        fetch(lo, lax.rem(lo, 2))
        for c in first_copies():
            c.wait()

    def step(i, carry):
        slot = lax.rem(i, 2)
        p = meta_ref[2, i]
        f = p // (pairs_here // n_first)

        @pl.when(i + 1 < hi)
        def _():
            fetch(i + 1, 1 - slot)

        await_fetch(slot)

        @pl.when(i >= lo + 2)
        def _():
            out_copy(p, slot).wait()

        e2_parts = []
        for base, rows, span in wins:
            one = pick[slot, 0, base:base + rows, 0:span]
            got = jnp.dot(one, first[f, base:base + span, :], preferred_element_type=jnp.float32)
            side_a[base:base + rows, :] = got.astype(jnp.bfloat16)
            e1_buf[base:base + rows, :] = jnp.dot(
                one, ve1_ref[f, base:base + span, :], preferred_element_type=jnp.float32)
            two = pick[slot, 1, base:base + rows, 0:span]
            got = jnp.dot(two, second[slot, base:base + span, :], preferred_element_type=jnp.float32)
            side_b[base:base + rows, :] = got.astype(jnp.bfloat16)
            ve = jnp.broadcast_to(ve2_ref[p, :, base:base + span], (8, span)).astype(jnp.bfloat16)
            e2_parts.append(
                lax.dot_general(ve, two, NT, preferred_element_type=jnp.float32)[0:1])
        e2 = jnp.concatenate(e2_parts, axis=1)
        shift = shift_ref[p]
        c = lax.dot_general(side_a[...], side_b[...], NT, preferred_element_type=jnp.float32)
        for col in range(0, kept, 128):
            den = e1_buf[...] + e2[:, col:col + 128] - shift
            inv = pl.reciprocal(den, approx=True)
            neg = inv * (den * inv - 2.0)
            out_buf[slot, :, col:col + 128] = (c[:, col:col + 128] * neg).astype(jnp.bfloat16)
        out_copy(p, slot).start()
        return carry

    lax.fori_loop(lo, hi, step, 0)

    @pl.when(hi - lo >= 2)
    def _():
        out_copy(0, lax.rem(hi, 2)).wait()

    @pl.when(hi > lo)
    def _():
        out_copy(0, lax.rem(hi + 1, 2)).wait()


def run_pairs(call, expected, wins, meta, shift, ve1, ve2, pick, own, other, sets, prev):
    pairs_here, _, kept, span = pick.shape
    n_first = ve1.shape[0]
    full, half = own.shape[1], own.shape[2]
    any_spec = pl.BlockSpec(memory_space=pl.ANY)
    smem = pl.BlockSpec(memory_space=pltpu.SMEM)
    vmem = pl.BlockSpec(memory_space=pltpu.VMEM)
    operands = [meta, shift, ve1, ve2, pick, own, other]
    for pair in sets:
        operands += list(pair)
    in_specs = [smem, smem, vmem, vmem] + [any_spec] * (len(operands) - 4)
    aliases = {}
    if prev is not None:
        aliases = {len(operands): 0}
        operands.append(prev)
        in_specs.append(any_spec)
    bf = jnp.bfloat16
    return pl.pallas_call(
        functools.partial(pair_kernel, call, wins, len(sets), prev is not None),
        out_shape=jax.ShapeDtypeStruct((pairs_here, kept, kept), bf),
        in_specs=in_specs,
        out_specs=any_spec,
        scratch_shapes=[
            pltpu.VMEM((n_first, full, 2 * half), bf),
            pltpu.VMEM((2, full, 2 * half), bf),
            pltpu.VMEM((2, 2, kept, span), bf),
            pltpu.VMEM((kept, 2 * half), bf),
            pltpu.VMEM((kept, 2 * half), bf),
            pltpu.VMEM((kept, 128), jnp.float32),
            pltpu.VMEM((2, kept, kept), bf),
            pltpu.SemaphoreType.DMA((2 * n_first,)),
            pltpu.SemaphoreType.DMA((2, 2)),
            pltpu.SemaphoreType.DMA((2,)),
            pltpu.SemaphoreType.DMA((2,)),
        ],
        input_output_aliases=aliases,
        compiler_params=pltpu.CompilerParams(vmem_limit_bytes=40 * 1024 * 1024),
        cost_estimate=pl.CostEstimate(
            flops=int(expected * 4 * kept * kept * 2 * half * 2),
            bytes_accessed=int(expected * (full * half * 4 + kept * kept * 2)),
            transcendentals=0),
        name=f"pairs_{call}",
    )(*operands)


def picks(source, i0, i1):
    return [lax.dynamic_slice_in_dim(source, i0, 1, 0), lax.dynamic_slice_in_dim(source, i1, 1, 0)]


def per_device(blocks, virt_energy, occ_energy, owner_slot, pairs, domains):
    orb_count = lax.axis_size("orb")
    aux_count = lax.axis_size("aux")
    occ_dev, full, half = blocks.shape
    pair_dev = pairs.shape[0]
    kept = domains.shape[2]
    own_rows = pair_dev // aux_count
    n_first = occ_dev // aux_count
    core = lax.axis_index("aux")
    o = lax.axis_index("orb")
    z, y = o // 2, o % 2
    chain = orb_count // 2
    last = chain - 1
    n_slots = orb_count * occ_dev
    i32 = jnp.int32
    wins = windows(full, kept)

    swap_aux = [(0, 1), (1, 0)]
    swap_y = [(k, k ^ 1) for k in range(orb_count)]

    def across_y(a):
        return lax.ppermute(a, "orb", swap_y)

    def across_aux(a):
        return lax.ppermute(a, "aux", swap_aux)

    def hop_down(a, d):
        return lax.ppermute(a, "orb", [(k, k - 2) for k in range(2, orb_count) if k // 2 <= chain - d])

    def hop_up(a, d):
        return lax.ppermute(a, "orb", [(k, k + 2) for k in range(orb_count - 2) if k // 2 >= d - 1])

    downs, ups = [blocks], [blocks]
    for d in range(1, last):
        downs.append(hop_down(downs[-1], d))
        ups.append(hop_up(ups[-1], d))
    local_other = across_aux(blocks)

    orbitals = jnp.arange(owner_slot.shape[0], dtype=i32)
    hit_second = pairs[:, 1][:, None] == orbitals[None, :]
    slot_second = jnp.sum(jnp.where(hit_second, owner_slot[None, :], 0), axis=1)
    slots = jnp.arange(n_slots, dtype=i32)
    wanted_flat = jnp.any(slot_second[:, None] == slots[None, :], axis=0)
    wanted = wanted_flat.reshape(orb_count, occ_dev)
    info = jnp.concatenate(
        [virt_energy, jnp.pad(wanted_flat.astype(jnp.bfloat16), (0, full - n_slots))[None, :]], axis=0)
    info = jnp.concatenate([info, across_y(info)], axis=0)
    per_info = occ_dev + 1
    info_down, info_up = [info], [info]
    for d in range(1, chain):
        info_down.append(hop_down(info_down[-1], d))
        info_up.append(hop_up(info_up[-1], d))

    def wanted_by_opposite(table):
        return (table[2 * per_info - 1, :n_slots] > 0.5).reshape(orb_count, occ_dev)

    wanted_opp = wanted_by_opposite(info)
    local = jnp.arange(occ_dev, dtype=i32)[None, :]

    def two_of(table):
        return jnp.min(jnp.where(table, local, occ_dev - 1), axis=1), jnp.max(jnp.where(table, local, 0), axis=1)

    want, want_opp = two_of(wanted), two_of(wanted_opp)

    def far_place(rows):
        w = rows.astype(i32)
        earlier = (jnp.arange(occ_dev)[:, None] < jnp.arange(occ_dev)[None, :]).astype(i32)
        ahead = jnp.sum(w[:, :, None] * earlier[None], axis=1)
        ahead_not = jnp.sum((1 - w)[:, :, None] * earlier[None], axis=1)
        return jnp.where(rows, ahead, jnp.sum(w, axis=1, keepdims=True) + ahead_not)

    first_row = core * own_rows
    own_second = lax.dynamic_slice_in_dim(slot_second, first_row, own_rows, 0)
    own_pairs = lax.dynamic_slice_in_dim(pairs, first_row, own_rows, 0)
    src = own_second // occ_dev
    part = own_second % occ_dev
    rank = jnp.any(
        (slot_second[None, :] // occ_dev == src[:, None]) & (slot_second[None, :] < own_second[:, None]),
        axis=1).astype(i32)
    src_z, src_y = src // 2, src % 2
    dist = jnp.abs(src_z - z)
    is_opp = (src_y != y).astype(i32)
    from_up = src_z < z
    place_table = far_place(wanted_opp).reshape(-1)
    far = jnp.sum(jnp.where(own_second[:, None] == slots[None, :], place_table[None, :], 0), axis=1)
    both = 2 * dist <= chain - 1
    is_far = (dist == last) & (is_opp == 0)
    idx = jnp.where(
        dist == 0,
        jnp.where(is_opp == 1, rank, part),
        rank + jnp.where(both & from_up, 2, 0))
    idx = jnp.where(is_far, far % 2, idx)
    which = jnp.where(is_far & (far >= 2), 2, is_opp)
    rows = jnp.arange(own_rows, dtype=i32)
    before = (dist[None, :] < dist[:, None]) | ((dist[None, :] == dist[:, None]) & (rows[None, :] < rows[:, None]))
    place = jnp.sum(before.astype(i32), axis=1)
    order = jnp.sum(jnp.where(place[None, :] == rows[:, None], rows[None, :], 0), axis=1)
    bounds = jnp.sum((dist[None, :] < jnp.arange(chain + 1, dtype=i32)[:, None]).astype(i32), axis=1)
    width = max(own_rows, chain + 1)

    def padded(v):
        v = v.reshape(-1)
        return jnp.pad(v, (0, width - v.shape[0]))

    meta = jnp.stack([padded(bounds), padded(core * n_first), padded(order), padded(which), padded(idx)])

    def occ(col):
        hit = own_pairs[:, col][:, None] == orbitals[None, :]
        return jnp.sum(jnp.where(hit, occ_energy[None, :], 0.0), axis=1)

    shift = occ(0) + occ(1)
    ve1 = lax.dynamic_slice_in_dim(virt_energy, core * n_first, n_first, 0)
    ve1 = jnp.broadcast_to(ve1[:, :, None], (n_first, full, 128))

    def energies(tables, row):
        stacked = jnp.concatenate(tables, axis=0)
        hit = (row[:, None] == jnp.arange(stacked.shape[0], dtype=i32)[None, :]).astype(jnp.bfloat16)
        return jnp.dot(hit, stacked, preferred_element_type=jnp.float32).reshape(own_rows, 1, full)

    row_here = is_opp * per_info + part
    row_away = row_here + jnp.where(from_up, 2 * per_info, 0)

    dom = lax.dynamic_slice_in_dim(domains, first_row, own_rows, 0)
    base = jnp.concatenate([jnp.full((r,), b, i32) for b, r, _ in wins])
    span = max(sp for _, _, sp in wins)
    pick = ((dom - base)[..., None] == jnp.arange(span, dtype=i32)).astype(jnp.bfloat16)

    def idx_of(table, source):
        return lax.dynamic_index_in_dim(table, jnp.clip(source, 0, orb_count - 1), 0, keepdims=False)

    def chosen(arrays, table, sources):
        got = []
        for a, s in zip(arrays, sources):
            got += picks(a, idx_of(table[0], s), idx_of(table[1], s))
        return jnp.concatenate(got, axis=0)

    y_own = across_y(chosen([blocks], want_opp, [o]))
    sets = [(blocks, local_other), (y_own, across_aux(y_own))]
    out = run_pairs(
        0, own_rows / 4, wins, meta, shift, ve1, energies([info], row_here), pick, blocks, local_other, sets, None)
    for d in range(1, chain):
        s_down, s_up = o + 2 * d, o - 2 * d
        if d == last:
            sends_down = z == 1
            w = jnp.where(sends_down, wanted_by_opposite(info_up[1]), wanted_by_opposite(info_down[1]))
            w = idx_of(far_place(w), jnp.where(sends_down, 2 * last + y, y))
            turn = [jnp.sum(jnp.where(w == j, local[0], 0)) for j in range(occ_dev)]
            perm = [(2, 0), (3, 1), (2 * (last - 1), 2 * last), (2 * (last - 1) + 1, 2 * last + 1)]
            sets = []
            for j in range(0, occ_dev, 2):
                load = jnp.where(
                    sends_down,
                    jnp.concatenate(picks(downs[-1], turn[j], turn[j + 1]), axis=0),
                    jnp.concatenate(picks(ups[-1], turn[j], turn[j + 1]), axis=0))
                got = lax.ppermute(load, "orb", perm)
                sets.append((got, across_aux(got)))
                if j == 0:
                    opp_own = across_y(got)
                    sets.append((opp_own, across_aux(opp_own)))
        elif 2 * d <= last:
            mine = chosen([downs[d], ups[d]], want, [s_down, s_up])
            opp_own = across_y(chosen([downs[d], ups[d]], want_opp, [s_down, s_up]))
            sets = [(mine, across_aux(mine)), (opp_own, across_aux(opp_own))]
        else:
            is_down = z + d <= last
            s = jnp.where(is_down, s_down, s_up)
            mine = jnp.where(is_down, chosen([downs[d]], want, [s]), chosen([ups[d]], want, [s]))
            theirs = jnp.where(is_down, chosen([downs[d]], want_opp, [s]), chosen([ups[d]], want_opp, [s]))
            opp_own = across_y(theirs)
            sets = [(mine, across_aux(mine)), (opp_own, across_aux(opp_own))]
        ve2 = energies([info_down[d], info_up[d]], row_away)
        out = run_pairs(d, own_rows / 4, wins, meta, shift, ve1, ve2, pick, blocks, local_other, sets, out)
    return out


def solution(mesh):
    in_specs = (
        P(("groups", "orb"), None, "aux"),
        P(("groups", "orb"), None),
        P("groups"),
        P("groups"),
        P(("groups", "orb"), None),
        P(("groups", "orb"), None, None),
    )
    out_specs = P(("groups", "orb", "aux"), None, None)
    return jax.shard_map(
        per_device, mesh=mesh, in_specs=in_specs, out_specs=out_specs, check_vma=False
    )
```

```python
import functools

import jax
import jax.numpy as jnp
from jax import lax
from jax.experimental import pallas as pl
from jax.experimental.pallas import tpu as pltpu
from jax.sharding import PartitionSpec as P

NT = (((1,), (1,)), ((), ()))
EXTRA = 16


def windows(full, kept):
    slack = full - kept
    tile = 256 - slack if 0 <= slack <= 128 else kept
    found = []
    base = 0
    while base < kept:
        rows = min(tile, kept - base)
        found.append((base, rows, rows + slack))
        base += rows
    return found


def pair_kernel(call, wins, n_sets, n_skip, meta_ref, shift_ref, ve1_ref, pick_ref, own_ref, other_ref, *rest):
    sets = [(rest[2 * k], rest[2 * k + 1]) for k in range(n_sets)]
    rest = rest[2 * n_sets + n_skip:]
    (out_ref, first, second, pick, side_a, side_b, e1_buf, out_buf,
     first_sem, second_sem, pick_sem, out_sem) = rest
    pairs_here = out_ref.shape[0]
    kept = out_ref.shape[1]
    half = own_ref.shape[2]
    n_first = first.shape[0]
    lo = meta_ref[0, call]
    hi = meta_ref[0, call + 1]
    base_first = meta_ref[1, 0]

    def first_copies():
        out = []
        for k in range(n_first):
            out.append(pltpu.make_async_copy(
                own_ref.at[base_first + k], first.at[k, :, pl.ds(0, half)], first_sem.at[2 * k]))
            out.append(pltpu.make_async_copy(
                other_ref.at[base_first + k], first.at[k, :, pl.ds(half, half)], first_sem.at[2 * k + 1]))
        return out

    def fetch(i, slot):
        p = meta_ref[2, i]
        which = meta_ref[3, p]
        idx = meta_ref[4, p]
        pltpu.make_async_copy(pick_ref.at[p], pick.at[slot], pick_sem.at[slot]).start()
        for k, (x_own, x_other) in enumerate(sets):
            @pl.when(which == k)
            def _():
                pltpu.make_async_copy(
                    x_own.at[idx], second.at[slot, :, pl.ds(0, half)], second_sem.at[slot, 0]).start()
                pltpu.make_async_copy(
                    x_other.at[idx], second.at[slot, :, pl.ds(half, half)], second_sem.at[slot, 1]).start()

    def await_fetch(slot):
        pltpu.make_async_copy(pick_ref.at[0], pick.at[slot], pick_sem.at[slot]).wait()
        for k in range(2):
            pltpu.make_async_copy(
                sets[0][0].at[0], second.at[slot, :, pl.ds(k * half, half)], second_sem.at[slot, k]).wait()

    def out_copy(p, slot):
        return pltpu.make_async_copy(out_buf.at[slot], out_ref.at[p], out_sem.at[slot])

    @pl.when(hi > lo)
    def _():
        for c in first_copies():
            c.start()
        fetch(lo, lax.rem(lo, 2))
        for c in first_copies():
            c.wait()

    def step(i, carry):
        slot = lax.rem(i, 2)
        p = meta_ref[2, i]
        f = p // (pairs_here // n_first)

        @pl.when(i + 1 < hi)
        def _():
            fetch(i + 1, 1 - slot)

        await_fetch(slot)

        @pl.when(i >= lo + 2)
        def _():
            out_copy(p, slot).wait()

        e2_parts = []
        full = ve1_ref.shape[1]
        for t, (base, rows, span) in enumerate(wins):
            one = pick[slot, 0, base:base + rows, 0:span]
            got = jnp.dot(one, first[f, base:base + span, :], preferred_element_type=jnp.float32)
            side_a[base:base + rows, :] = got.astype(jnp.bfloat16)
            e1_buf[base:base + rows, :] = jnp.dot(
                one, ve1_ref[f, base:base + span, :], preferred_element_type=jnp.float32)
            two = pick[slot, 1, base:base + rows, 0:span]
            got = jnp.dot(two, second[slot, base:base + span, :], preferred_element_type=jnp.float32)
            side_b[base:base + rows, :] = got.astype(jnp.bfloat16)
            ve = second[slot, full:full + EXTRA, 0:span]
            e2_parts.append(
                lax.dot_general(ve, two, NT, preferred_element_type=jnp.float32)[t:t + 1])
        e2 = jnp.concatenate(e2_parts, axis=1)
        shift = shift_ref[p]
        c = lax.dot_general(side_a[...], side_b[...], NT, preferred_element_type=jnp.float32)
        for col in range(0, kept, 128):
            den = e1_buf[...] + e2[:, col:col + 128] - shift
            inv = pl.reciprocal(den, approx=True)
            neg = inv * (den * inv - 2.0)
            out_buf[slot, :, col:col + 128] = (c[:, col:col + 128] * neg).astype(jnp.bfloat16)
        out_copy(p, slot).start()
        return carry

    lax.fori_loop(lo, hi, step, 0)

    @pl.when(hi - lo >= 2)
    def _():
        out_copy(0, lax.rem(hi, 2)).wait()

    @pl.when(hi > lo)
    def _():
        out_copy(0, lax.rem(hi + 1, 2)).wait()


def run_pairs(call, expected, wins, meta, shift, ve1, pick, own, other, sets, after, prev):
    pairs_here, _, kept, span = pick.shape
    n_first = ve1.shape[0]
    full, half = own.shape[1], own.shape[2]
    any_spec = pl.BlockSpec(memory_space=pl.ANY)
    smem = pl.BlockSpec(memory_space=pltpu.SMEM)
    vmem = pl.BlockSpec(memory_space=pltpu.VMEM)
    operands = [meta, shift, ve1, pick, own, other]
    for pair in sets:
        operands += list(pair)
    operands += after
    in_specs = [smem, smem, vmem] + [any_spec] * (len(operands) - 3)
    aliases = {}
    if prev is not None:
        aliases = {len(operands): 0}
        operands.append(prev)
        in_specs.append(any_spec)
    bf = jnp.bfloat16
    return pl.pallas_call(
        functools.partial(pair_kernel, call, wins, len(sets), len(after) + (prev is not None)),
        out_shape=jax.ShapeDtypeStruct((pairs_here, kept, kept), bf),
        in_specs=in_specs,
        out_specs=any_spec,
        scratch_shapes=[
            pltpu.VMEM((n_first, full, 2 * half), bf),
            pltpu.VMEM((2, full, 2 * half), bf),
            pltpu.VMEM((2, 2, kept, span), bf),
            pltpu.VMEM((kept, 2 * half), bf),
            pltpu.VMEM((kept, 2 * half), bf),
            pltpu.VMEM((kept, 128), jnp.float32),
            pltpu.VMEM((2, kept, kept), bf),
            pltpu.SemaphoreType.DMA((2 * n_first,)),
            pltpu.SemaphoreType.DMA((2, 2)),
            pltpu.SemaphoreType.DMA((2,)),
            pltpu.SemaphoreType.DMA((2,)),
        ],
        input_output_aliases=aliases,
        compiler_params=pltpu.CompilerParams(vmem_limit_bytes=40 * 1024 * 1024),
        cost_estimate=pl.CostEstimate(
            flops=int(expected * 4 * kept * kept * 2 * half * 2),
            bytes_accessed=int(expected * (full * half * 4 + kept * kept * 2)),
            transcendentals=0),
        name=f"pairs_{call}",
    )(*operands)


def set_kernel(n_arrays, table_ref, *rest):
    arrays = rest[:n_arrays]
    out_ref, sems = rest[n_arrays:]
    for j in range(out_ref.shape[0]):
        for k, a in enumerate(arrays):
            @pl.when(table_ref[0, j] == k)
            def _():
                pltpu.make_async_copy(a.at[table_ref[1, j]], out_ref.at[j], sems.at[j]).start()
    for j in range(out_ref.shape[0]):
        pltpu.make_async_copy(arrays[0].at[0], out_ref.at[j], sems.at[j]).wait()


def copy_sets(which, index, arrays):
    n = len(index)
    table = jnp.stack([jnp.stack([jnp.asarray(w, jnp.int32) for w in which]), jnp.stack(index)])
    block = arrays[0].shape[1:]
    any_spec = pl.BlockSpec(memory_space=pl.ANY)
    size = 2 * n * block[0] * block[1] * 2
    return pl.pallas_call(
        functools.partial(set_kernel, len(arrays)),
        out_shape=jax.ShapeDtypeStruct((n,) + block, arrays[0].dtype),
        in_specs=[pl.BlockSpec(memory_space=pltpu.SMEM)] + [any_spec] * len(arrays),
        out_specs=any_spec,
        scratch_shapes=[pltpu.SemaphoreType.DMA((n,))],
        cost_estimate=pl.CostEstimate(flops=0, bytes_accessed=size, transcendentals=0),
        name="copy_sets",
    )(table, *arrays)


def per_device(blocks, virt_energy, occ_energy, owner_slot, pairs, domains):
    orb_count = lax.axis_size("orb")
    aux_count = lax.axis_size("aux")
    occ_dev, full, half = blocks.shape
    pair_dev = pairs.shape[0]
    kept = domains.shape[2]
    own_rows = pair_dev // aux_count
    n_first = occ_dev // aux_count
    core = lax.axis_index("aux")
    o = lax.axis_index("orb")
    z, y = o // 2, o % 2
    chain = orb_count // 2
    last = chain - 1
    n_slots = orb_count * occ_dev
    i32 = jnp.int32
    wins = windows(full, kept)

    swap_aux = [(0, 1), (1, 0)]
    swap_y = [(k, k ^ 1) for k in range(orb_count)]

    def across_y(a):
        return lax.ppermute(a, "orb", swap_y)

    def across_aux(a):
        return lax.ppermute(a, "aux", swap_aux)

    def hop_down(a, d):
        return lax.ppermute(a, "orb", [(k, k - 2) for k in range(2, orb_count) if k // 2 <= chain - d])

    def hop_up(a, d):
        return lax.ppermute(a, "orb", [(k, k + 2) for k in range(orb_count - 2) if k // 2 >= d - 1])

    extra = [
        jnp.pad(virt_energy[:, None, b:b + sp], ((0, 0), (0, 0), (0, half - sp))) for b, _, sp in wins]
    extra.append(jnp.zeros((occ_dev, EXTRA - len(wins), half), blocks.dtype))
    stored = jnp.concatenate([blocks] + extra, axis=1)

    downs, ups = [stored], [stored]
    for d in range(1, last):
        downs.append(hop_down(downs[-1], d))
        ups.append(hop_up(ups[-1], d))
    local_other = across_aux(stored)

    orbitals = jnp.arange(owner_slot.shape[0], dtype=i32)
    hit_second = pairs[:, 1][:, None] == orbitals[None, :]
    slot_second = jnp.sum(jnp.where(hit_second, owner_slot[None, :], 0), axis=1)
    slots = jnp.arange(n_slots, dtype=i32)
    wanted_flat = jnp.any(slot_second[:, None] == slots[None, :], axis=0).astype(i32)
    wanted = wanted_flat.reshape(orb_count, occ_dev) > 0
    wanted_opp = across_y(wanted_flat).reshape(orb_count, occ_dev) > 0
    top = orb_count - 1
    tell = [(0, 3), (1, 2), (top, top - 3), (top - 1, top - 2)]
    wanted_far = lax.ppermute(wanted_flat, "orb", tell).reshape(orb_count, occ_dev) > 0
    local = jnp.arange(occ_dev, dtype=i32)[None, :]

    def two_of(table):
        return jnp.min(jnp.where(table, local, occ_dev - 1), axis=1), jnp.max(jnp.where(table, local, 0), axis=1)

    want_opp = two_of(wanted_opp)

    def far_place(rows):
        w = rows.astype(i32)
        earlier = (jnp.arange(occ_dev)[:, None] < jnp.arange(occ_dev)[None, :]).astype(i32)
        ahead = jnp.sum(w[:, :, None] * earlier[None], axis=1)
        ahead_not = jnp.sum((1 - w)[:, :, None] * earlier[None], axis=1)
        return jnp.where(rows, ahead, jnp.sum(w, axis=1, keepdims=True) + ahead_not)

    first_row = core * own_rows
    own_second = lax.dynamic_slice_in_dim(slot_second, first_row, own_rows, 0)
    own_pairs = lax.dynamic_slice_in_dim(pairs, first_row, own_rows, 0)
    src = own_second // occ_dev
    part = own_second % occ_dev
    rank = jnp.any(
        (slot_second[None, :] // occ_dev == src[:, None]) & (slot_second[None, :] < own_second[:, None]),
        axis=1).astype(i32)
    src_z, src_y = src // 2, src % 2
    dist = jnp.abs(src_z - z)
    is_opp = (src_y != y).astype(i32)
    from_up = src_z < z
    place_table = far_place(wanted_opp).reshape(-1)
    far = jnp.sum(jnp.where(own_second[:, None] == slots[None, :], place_table[None, :], 0), axis=1)
    both = 2 * dist <= chain - 1
    is_far = (dist == last) & (is_opp == 0)
    idx = jnp.where(is_opp == 1, rank + jnp.where(both & from_up, 2, 0), part)
    idx = jnp.where(is_far, far % 2, idx)
    which_away = jnp.where(is_opp == 1, 2, jnp.where(is_far, far // 2, from_up.astype(i32)))
    which = jnp.where(dist == 0, is_opp, which_away)
    rows = jnp.arange(own_rows, dtype=i32)
    before = (dist[None, :] < dist[:, None]) | ((dist[None, :] == dist[:, None]) & (rows[None, :] < rows[:, None]))
    place = jnp.sum(before.astype(i32), axis=1)
    order = jnp.sum(jnp.where(place[None, :] == rows[:, None], rows[None, :], 0), axis=1)
    bounds = jnp.sum((dist[None, :] < jnp.arange(chain + 1, dtype=i32)[:, None]).astype(i32), axis=1)
    width = max(own_rows, chain + 1)

    def padded(v):
        v = v.reshape(-1)
        return jnp.pad(v, (0, width - v.shape[0]))

    meta = jnp.stack([padded(bounds), padded(core * n_first), padded(order), padded(which), padded(idx)])

    def occ(col):
        hit = own_pairs[:, col][:, None] == orbitals[None, :]
        return jnp.sum(jnp.where(hit, occ_energy[None, :], 0.0), axis=1)

    shift = occ(0) + occ(1)
    ve1 = lax.dynamic_slice_in_dim(virt_energy, core * n_first, n_first, 0)
    ve1 = jnp.broadcast_to(ve1[:, :, None], (n_first, full, 128))

    dom = lax.dynamic_slice_in_dim(domains, first_row, own_rows, 0)
    base = jnp.concatenate([jnp.full((r,), b, i32) for b, r, _ in wins])
    span = max(sp for _, _, sp in wins)
    pick = ((dom - base)[..., None] == jnp.arange(span, dtype=i32)).astype(jnp.bfloat16)

    def idx_of(table, source):
        return lax.dynamic_index_in_dim(table, jnp.clip(source, 0, orb_count - 1), 0, keepdims=False)

    def two_for_opposite(source):
        return [idx_of(want_opp[0], source), idx_of(want_opp[1], source)]

    y_own = across_y(copy_sets([0, 0], two_for_opposite(o), [stored]))
    sets = {0: [(stored, local_other), (y_own, across_aux(y_own))]}
    after = {0: [downs[1], ups[1]]}
    for d in range(1, last):
        s_down, s_up = o + 2 * d, o - 2 * d
        if 2 * d <= last:
            theirs = copy_sets([0, 0, 1, 1], two_for_opposite(s_down) + two_for_opposite(s_up), [downs[d], ups[d]])
        else:
            is_up = (z + d > last).astype(i32)
            s = jnp.where(is_up == 1, s_up, s_down)
            theirs = copy_sets([is_up, is_up], two_for_opposite(s), [downs[d], ups[d]])
        opp_own = across_y(theirs)
        sets[d] = [
            (downs[d], across_aux(downs[d])), (ups[d], across_aux(ups[d])), (opp_own, across_aux(opp_own))]
        after[d] = [] if d == last - 1 else [downs[d + 1], ups[d + 1]]
    sends_down = z == 1
    turn_of = idx_of(far_place(wanted_far), jnp.where(sends_down, 2 * last + y, y))
    turn = [jnp.sum(jnp.where(turn_of == j, local[0], 0)) for j in range(occ_dev)]
    perm = [(2, 0), (3, 1), (2 * (last - 1), 2 * last), (2 * (last - 1) + 1, 2 * last + 1)]
    is_up = 1 - sends_down.astype(i32)
    loads = [copy_sets([is_up, is_up], turn[j:j + 2], [downs[-1], ups[-1]]) for j in range(0, occ_dev, 2)]
    got_a, got_b = [lax.ppermute(load, "orb", perm) for load in loads]
    opp_own = across_y(got_a)
    sets[last] = [(got_a, across_aux(got_a)), (got_b, across_aux(got_b)), (opp_own, across_aux(opp_own))]
    for d in range(1, last):
        after[d] = after[d] + (loads if d == last - 2 else [got_a] if d == last - 1 else [])
    after[last] = []
    out = None
    for d in range(chain):
        out = run_pairs(
            d, own_rows / chain, wins, meta, shift, ve1, pick, stored, local_other, sets[d], after[d], out)
    return out


def solution(mesh):
    in_specs = (
        P(("groups", "orb"), None, "aux"),
        P(("groups", "orb"), None),
        P("groups"),
        P("groups"),
        P(("groups", "orb"), None),
        P(("groups", "orb"), None, None),
    )
    out_specs = P(("groups", "orb", "aux"), None, None)
    return jax.shard_map(
        per_device, mesh=mesh, in_specs=in_specs, out_specs=out_specs, check_vma=False
    )
```

```python
import functools

import jax
import jax.numpy as jnp
from jax import lax
from jax.experimental import pallas as pl
from jax.experimental.pallas import tpu as pltpu
from jax.sharding import PartitionSpec as P

NT = (((1,), (1,)), ((), ()))
VMEM_LIMIT = 56 * 1024 * 1024
EXTRA = 16


def windows(full, kept):
    slack = full - kept
    tile = 256 - slack if 0 <= slack <= 128 else kept
    found = []
    base = 0
    while base < kept:
        rows = min(tile, kept - base)
        found.append((base, rows, rows + slack))
        base += rows
    return found


def pair_kernel(call, wins, n_sets, n_skip, meta_ref, shift_ref, ve1_ref, pick_ref, own_ref, other_ref, *rest):
    sets = [(rest[2 * k], rest[2 * k + 1]) for k in range(n_sets)]
    rest = rest[2 * n_sets + n_skip:]
    (out_ref, first, second, pick, side_a, side_b, e1_buf, out_buf,
     first_sem, second_sem, pick_sem, out_sem) = rest
    pairs_here = out_ref.shape[0]
    kept = out_ref.shape[1]
    half = own_ref.shape[2]
    n_first = first.shape[0]
    lo = meta_ref[0, call]
    hi = meta_ref[0, call + 1]
    base_first = meta_ref[1, 0]

    def first_copies():
        out = []
        for k in range(n_first):
            out.append(pltpu.make_async_copy(
                own_ref.at[base_first + k], first.at[k, :, pl.ds(0, half)], first_sem.at[2 * k]))
            out.append(pltpu.make_async_copy(
                other_ref.at[base_first + k], first.at[k, :, pl.ds(half, half)], first_sem.at[2 * k + 1]))
        return out

    def fetch(i, slot):
        p = meta_ref[2, i]
        which = meta_ref[3, p]
        idx = meta_ref[4, p]
        pltpu.make_async_copy(pick_ref.at[p], pick.at[slot], pick_sem.at[slot]).start()
        for k, (x_own, x_other) in enumerate(sets):
            @pl.when(which == k)
            def _():
                pltpu.make_async_copy(
                    x_own.at[idx], second.at[slot, :, pl.ds(0, half)], second_sem.at[slot, 0]).start()
                pltpu.make_async_copy(
                    x_other.at[idx], second.at[slot, :, pl.ds(half, half)], second_sem.at[slot, 1]).start()

    def await_fetch(slot):
        pltpu.make_async_copy(pick_ref.at[0], pick.at[slot], pick_sem.at[slot]).wait()
        for k in range(2):
            pltpu.make_async_copy(
                sets[0][0].at[0], second.at[slot, :, pl.ds(k * half, half)], second_sem.at[slot, k]).wait()

    def out_copy(p, slot):
        return pltpu.make_async_copy(out_buf.at[slot], out_ref.at[p], out_sem.at[slot])

    @pl.when(hi > lo)
    def _():
        for c in first_copies():
            c.start()
        fetch(lo, lax.rem(lo, 2))
        for c in first_copies():
            c.wait()

    def step(i, carry):
        slot = lax.rem(i, 2)
        p = meta_ref[2, i]
        f = p // (pairs_here // n_first)

        @pl.when(i + 1 < hi)
        def _():
            fetch(i + 1, 1 - slot)

        await_fetch(slot)

        @pl.when(i >= lo + 2)
        def _():
            out_copy(p, slot).wait()

        e2_parts = []
        full = ve1_ref.shape[1]
        for t, (base, rows, span) in enumerate(wins):
            one = pick[slot, 0, base:base + rows, 0:span]
            got = jnp.dot(one, first[f, base:base + span, :], preferred_element_type=jnp.float32)
            side_a[base:base + rows, :] = got.astype(jnp.bfloat16)
            e1_buf[base:base + rows, :] = jnp.dot(
                one, ve1_ref[f, base:base + span, :], preferred_element_type=jnp.float32)
            two = pick[slot, 1, base:base + rows, 0:span]
            got = jnp.dot(two, second[slot, base:base + span, :], preferred_element_type=jnp.float32)
            side_b[base:base + rows, :] = got.astype(jnp.bfloat16)
            ve = second[slot, full:full + EXTRA, 0:span]
            e2_parts.append(
                lax.dot_general(ve, two, NT, preferred_element_type=jnp.float32)[t:t + 1])
        e2 = jnp.concatenate(e2_parts, axis=1)
        shift = shift_ref[p]
        c = lax.dot_general(side_a[...], side_b[...], NT, preferred_element_type=jnp.float32)
        for col in range(0, kept, 128):
            den = e1_buf[...] + e2[:, col:col + 128] - shift
            inv = pl.reciprocal(den, approx=True)
            neg = inv * (den * inv - 2.0)
            out_buf[slot, :, col:col + 128] = (c[:, col:col + 128] * neg).astype(jnp.bfloat16)
        out_copy(p, slot).start()
        return carry

    lax.fori_loop(lo, hi, step, 0)

    @pl.when(hi - lo >= 2)
    def _():
        out_copy(0, lax.rem(hi, 2)).wait()

    @pl.when(hi > lo)
    def _():
        out_copy(0, lax.rem(hi + 1, 2)).wait()


def run_pairs(call, expected, wins, meta, shift, ve1, pick, own, other, sets, after, prev):
    pairs_here, _, kept, span = pick.shape
    n_first = ve1.shape[0]
    full, half = own.shape[1], own.shape[2]
    any_spec = ANY_SPEC
    smem = pl.BlockSpec(memory_space=pltpu.SMEM)
    vmem = pl.BlockSpec(memory_space=pltpu.VMEM)
    operands = [meta, shift, ve1, pick, own, other]
    for pair in sets:
        operands += list(pair)
    operands += after
    in_specs = [smem, smem, vmem] + [any_spec] * (len(operands) - 3)
    aliases = {}
    if prev is not None:
        aliases = {len(operands): 0}
        operands.append(prev)
        in_specs.append(any_spec)
    bf = jnp.bfloat16
    return pl.pallas_call(
        functools.partial(pair_kernel, call, wins, len(sets), len(after) + (prev is not None)),
        out_shape=jax.ShapeDtypeStruct((pairs_here, kept, kept), bf),
        in_specs=in_specs,
        out_specs=any_spec,
        scratch_shapes=[
            pltpu.VMEM((n_first, full, 2 * half), bf),
            pltpu.VMEM((2, full, 2 * half), bf),
            pltpu.VMEM((2, 2, kept, span), bf),
            pltpu.VMEM((kept, 2 * half), bf),
            pltpu.VMEM((kept, 2 * half), bf),
            pltpu.VMEM((kept, 128), jnp.float32),
            pltpu.VMEM((2, kept, kept), bf),
            pltpu.SemaphoreType.DMA((2 * n_first,)),
            pltpu.SemaphoreType.DMA((2, 2)),
            pltpu.SemaphoreType.DMA((2,)),
            pltpu.SemaphoreType.DMA((2,)),
        ],
        input_output_aliases=aliases,
        compiler_params=pltpu.CompilerParams(vmem_limit_bytes=VMEM_LIMIT),
        cost_estimate=pl.CostEstimate(
            flops=int(expected * 4 * kept * kept * 2 * half * 2),
            bytes_accessed=int(expected * (full * half * 4 + kept * kept * 2)),
            transcendentals=0),
        name=f"pairs_{call}",
    )(*operands)


def set_kernel(n_arrays, n_skip, table_ref, *rest):
    arrays = rest[:n_arrays]
    out_ref, held, in_sems, out_sems = rest[n_arrays + n_skip:]
    count = out_ref.shape[0]
    for j in range(count):
        for k, a in enumerate(arrays):
            @pl.when(table_ref[0, j] == k)
            def _():
                pltpu.make_async_copy(a.at[table_ref[1, j]], held.at[j], in_sems.at[j]).start()
    for j in range(count):
        pltpu.make_async_copy(arrays[0].at[0], held.at[j], in_sems.at[j]).wait()
        pltpu.make_async_copy(held.at[j], out_ref.at[j], out_sems.at[j]).start()
    for j in range(count):
        pltpu.make_async_copy(held.at[j], out_ref.at[j], out_sems.at[j]).wait()


ANY_SPEC = pl.BlockSpec(memory_space=pl.ANY)


def copy_sets(which, index, arrays, after=()):
    n = len(index)
    table = jnp.stack([jnp.stack([jnp.asarray(w, jnp.int32) for w in which]), jnp.stack(index)])
    block = arrays[0].shape[1:]
    size = 2 * n * block[0] * block[1] * 2
    return pl.pallas_call(
        functools.partial(set_kernel, len(arrays), len(after)),
        out_shape=jax.ShapeDtypeStruct((n,) + block, arrays[0].dtype),
        in_specs=[pl.BlockSpec(memory_space=pltpu.SMEM)] + [ANY_SPEC] * (len(arrays) + len(after)),
        out_specs=ANY_SPEC,
        scratch_shapes=[
            pltpu.VMEM((n,) + block, arrays[0].dtype),
            pltpu.SemaphoreType.DMA((n,)),
            pltpu.SemaphoreType.DMA((n,))],
        cost_estimate=pl.CostEstimate(flops=0, bytes_accessed=size, transcendentals=0),
        compiler_params=pltpu.CompilerParams(vmem_limit_bytes=VMEM_LIMIT),
        name="copy_sets",
    )(table, *arrays, *after)


def extend_kernel(blocks_ref, extra_ref, out_ref, held, in_sems, out_sems):
    count, full, _ = blocks_ref.shape
    for k in range(count):
        pltpu.make_async_copy(blocks_ref.at[k], held.at[k, 0:full], in_sems.at[k]).start()
    for k in range(count):
        held[k, full:, :] = extra_ref[k]
    for k in range(count):
        pltpu.make_async_copy(blocks_ref.at[k], held.at[k, 0:full], in_sems.at[k]).wait()
        pltpu.make_async_copy(held.at[k], out_ref.at[k], out_sems.at[k]).start()
    for k in range(count):
        pltpu.make_async_copy(held.at[k], out_ref.at[k], out_sems.at[k]).wait()


def extend(blocks, extra):
    count, full, half = blocks.shape
    shape = (count, full + extra.shape[1], half)
    return pl.pallas_call(
        extend_kernel,
        out_shape=jax.ShapeDtypeStruct(shape, blocks.dtype),
        in_specs=[ANY_SPEC, pl.BlockSpec(memory_space=pltpu.VMEM)],
        out_specs=ANY_SPEC,
        scratch_shapes=[
            pltpu.VMEM(shape, blocks.dtype), pltpu.SemaphoreType.DMA((count,)), pltpu.SemaphoreType.DMA((count,))],
        compiler_params=pltpu.CompilerParams(vmem_limit_bytes=VMEM_LIMIT),
        name="extend",
    )(blocks, extra)


def tie(x, deps):
    return pl.pallas_call(
        lambda *refs: None,
        out_shape=jax.ShapeDtypeStruct(x.shape, x.dtype),
        in_specs=[ANY_SPEC] * (1 + len(deps)),
        out_specs=ANY_SPEC,
        input_output_aliases={0: 0},
        compiler_params=pltpu.CompilerParams(vmem_limit_bytes=VMEM_LIMIT),
        cost_estimate=pl.CostEstimate(flops=0, bytes_accessed=0, transcendentals=0),
        name="tie",
    )(x, *deps)


def per_device(blocks, virt_energy, occ_energy, owner_slot, pairs, domains):
    orb_count = lax.axis_size("orb")
    aux_count = lax.axis_size("aux")
    occ_dev, full, half = blocks.shape
    pair_dev = pairs.shape[0]
    kept = domains.shape[2]
    own_rows = pair_dev // aux_count
    n_first = occ_dev // aux_count
    core = lax.axis_index("aux")
    o = lax.axis_index("orb")
    z, y = o // 2, o % 2
    chain = orb_count // 2
    last = chain - 1
    n_slots = orb_count * occ_dev
    i32 = jnp.int32
    wins = windows(full, kept)

    swap_aux = [(0, 1), (1, 0)]
    swap_y = [(k, k ^ 1) for k in range(orb_count)]

    def across_y(a):
        return lax.ppermute(a, "orb", swap_y)

    def across_aux(a):
        return lax.ppermute(a, "aux", swap_aux)

    def hop_down(a, d):
        return lax.ppermute(a, "orb", [(k, k - 2) for k in range(2, orb_count) if k // 2 <= chain - d])

    def hop_up(a, d):
        return lax.ppermute(a, "orb", [(k, k + 2) for k in range(orb_count - 2) if k // 2 >= d - 1])

    extra = [
        jnp.pad(virt_energy[:, None, b:b + sp], ((0, 0), (0, 0), (0, half - sp))) for b, _, sp in wins]
    extra.append(jnp.zeros((occ_dev, EXTRA - len(wins), half), blocks.dtype))
    stored = extend(blocks, jnp.concatenate(extra, axis=1))

    downs, ups = [stored, hop_down(stored, 1)], [stored, hop_up(stored, 1)]
    local_other = across_aux(stored)

    orbitals = jnp.arange(owner_slot.shape[0], dtype=i32)
    hit_second = pairs[:, 1][:, None] == orbitals[None, :]
    slot_second = jnp.sum(jnp.where(hit_second, owner_slot[None, :], 0), axis=1)
    slots = jnp.arange(n_slots, dtype=i32)
    wanted_flat = jnp.any(slot_second[:, None] == slots[None, :], axis=0).astype(i32)
    wanted = wanted_flat.reshape(orb_count, occ_dev) > 0
    wanted_opp = across_y(wanted_flat).reshape(orb_count, occ_dev) > 0
    top = orb_count - 1
    tell = [(0, 3), (1, 2), (top, top - 3), (top - 1, top - 2)]
    wanted_far = lax.ppermute(wanted_flat, "orb", tell).reshape(orb_count, occ_dev) > 0
    local = jnp.arange(occ_dev, dtype=i32)[None, :]

    def two_of(table):
        return jnp.min(jnp.where(table, local, occ_dev - 1), axis=1), jnp.max(jnp.where(table, local, 0), axis=1)

    want_opp = two_of(wanted_opp)

    def far_place(rows):
        w = rows.astype(i32)
        earlier = (jnp.arange(occ_dev)[:, None] < jnp.arange(occ_dev)[None, :]).astype(i32)
        ahead = jnp.sum(w[:, :, None] * earlier[None], axis=1)
        ahead_not = jnp.sum((1 - w)[:, :, None] * earlier[None], axis=1)
        return jnp.where(rows, ahead, jnp.sum(w, axis=1, keepdims=True) + ahead_not)

    first_row = core * own_rows
    own_second = lax.dynamic_slice_in_dim(slot_second, first_row, own_rows, 0)
    own_pairs = lax.dynamic_slice_in_dim(pairs, first_row, own_rows, 0)
    src = own_second // occ_dev
    part = own_second % occ_dev
    rank = jnp.any(
        (slot_second[None, :] // occ_dev == src[:, None]) & (slot_second[None, :] < own_second[:, None]),
        axis=1).astype(i32)
    src_z, src_y = src // 2, src % 2
    dist = jnp.abs(src_z - z)
    is_opp = (src_y != y).astype(i32)
    from_up = src_z < z
    place_table = far_place(wanted_opp).reshape(-1)
    far = jnp.sum(jnp.where(own_second[:, None] == slots[None, :], place_table[None, :], 0), axis=1)
    both = 2 * dist <= chain - 1
    is_far = (dist == last) & (is_opp == 0)
    idx = jnp.where(is_opp == 1, rank + jnp.where(both & from_up, 2, 0), part)
    idx = jnp.where(is_far, far % 2, idx)
    which_away = jnp.where(is_opp == 1, 2, jnp.where(is_far, far // 2, from_up.astype(i32)))
    which = jnp.where(dist == 0, is_opp, which_away)
    rows = jnp.arange(own_rows, dtype=i32)
    before = (dist[None, :] < dist[:, None]) | ((dist[None, :] == dist[:, None]) & (rows[None, :] < rows[:, None]))
    place = jnp.sum(before.astype(i32), axis=1)
    order = jnp.sum(jnp.where(place[None, :] == rows[:, None], rows[None, :], 0), axis=1)
    bounds = jnp.sum((dist[None, :] < jnp.arange(chain + 1, dtype=i32)[:, None]).astype(i32), axis=1)
    width = max(own_rows, chain + 1)

    def padded(v):
        v = v.reshape(-1)
        return jnp.pad(v, (0, width - v.shape[0]))

    meta = jnp.stack([padded(bounds), padded(core * n_first), padded(order), padded(which), padded(idx)])

    def occ(col):
        hit = own_pairs[:, col][:, None] == orbitals[None, :]
        return jnp.sum(jnp.where(hit, occ_energy[None, :], 0.0), axis=1)

    shift = occ(0) + occ(1)
    ve1 = lax.dynamic_slice_in_dim(virt_energy, core * n_first, n_first, 0)
    ve1 = jnp.broadcast_to(ve1[:, :, None], (n_first, full, 128))

    dom = lax.dynamic_slice_in_dim(domains, first_row, own_rows, 0)
    base = jnp.concatenate([jnp.full((r,), b, i32) for b, r, _ in wins])
    span = max(sp for _, _, sp in wins)
    pick = ((dom - base)[..., None] == jnp.arange(span, dtype=i32)).astype(jnp.bfloat16)

    def idx_of(table, source):
        return lax.dynamic_index_in_dim(table, jnp.clip(source, 0, orb_count - 1), 0, keepdims=False)

    def two_for_opposite(source):
        return [idx_of(want_opp[0], source), idx_of(want_opp[1], source)]

    def pairs_at(d, sets, after, prev):
        return run_pairs(d, own_rows / chain, wins, meta, shift, ve1, pick, stored, local_other, sets, after, prev)

    def pairs_at(d, after, prev):
        return run_pairs(d, own_rows / chain, wins, meta, shift, ve1, pick, stored, local_other, sets[d], after, prev)

    y_load = copy_sets([0, 0], two_for_opposite(o), [stored])
    opp = [across_y(y_load)]
    early = [y_load, pick, meta]
    downs[1], ups[1] = tie(downs[1], early), tie(ups[1], early)
    sets = {}
    out = None
    for d in range(1, last):
        s_down, s_up = o + 2 * d, o - 2 * d
        loads = []
        if d + 1 < last:
            downs.append(hop_down(downs[d], d + 1))
            ups.append(hop_up(ups[d], d + 1))
        else:
            sends_down = z == 1
            turn_of = idx_of(far_place(wanted_far), jnp.where(sends_down, 2 * last + y, y))
            turn = [jnp.sum(jnp.where(turn_of == j, local[0], 0)) for j in range(occ_dev)]
            perm = [(2, 0), (3, 1), (2 * (last - 1), 2 * last), (2 * (last - 1) + 1, 2 * last + 1)]
            is_up = 1 - sends_down.astype(i32)
            load_a = copy_sets([is_up, is_up], turn[:2], [downs[d], ups[d]])
            load_b = copy_sets([is_up, is_up], turn[2:], [downs[d], ups[d]], [load_a])
            got_a, got_b = lax.ppermute(load_a, "orb", perm), lax.ppermute(load_b, "orb", perm)
            loads = [load_b]
            if d > 1:
                opp[d - 1] = tie(opp[d - 1], loads)
        if 2 * d <= last:
            theirs = copy_sets(
                [0, 0, 1, 1], two_for_opposite(s_down) + two_for_opposite(s_up), [downs[d], ups[d]], loads)
        else:
            is_up = (z + d > last).astype(i32)
            s = jnp.where(is_up == 1, s_up, s_down)
            theirs = copy_sets([is_up, is_up], two_for_opposite(s), [downs[d], ups[d]], loads)
        opp.append(across_y(theirs))
        if d == 1:
            sets[0] = [(stored, local_other), (opp[0], across_aux(opp[0]))]
        else:
            sets[d - 1] = [
                (downs[d - 1], across_aux(downs[d - 1])), (ups[d - 1], across_aux(ups[d - 1])),
                (opp[d - 1], across_aux(opp[d - 1]))]
            out = pairs_at(d - 2, [theirs] + loads, out)
    got_a = tie(got_a, [out])
    opp.append(across_y(got_a))
    sets[last - 1] = [
        (downs[last - 1], across_aux(downs[last - 1])), (ups[last - 1], across_aux(ups[last - 1])),
        (opp[last - 1], across_aux(opp[last - 1]))]
    out = pairs_at(last - 2, [got_a], out)
    out = pairs_at(last - 1, [got_a], out)
    got_b = tie(got_b, [out])
    sets[last] = [(got_a, across_aux(got_a)), (got_b, across_aux(got_b)), (opp[last], across_aux(opp[last]))]
    return pairs_at(last, [], out)


def solution(mesh):
    in_specs = (
        P(("groups", "orb"), None, "aux"),
        P(("groups", "orb"), None),
        P("groups"),
        P("groups"),
        P(("groups", "orb"), None),
        P(("groups", "orb"), None, None),
    )
    out_specs = P(("groups", "orb", "aux"), None, None)
    return jax.shard_map(
        per_device, mesh=mesh, in_specs=in_specs, out_specs=out_specs, check_vma=False
    )
```

```python
import functools

import jax
import jax.numpy as jnp
from jax import lax
from jax.experimental import pallas as pl
from jax.experimental.pallas import tpu as pltpu
from jax.sharding import PartitionSpec as P

NT = (((1,), (1,)), ((), ()))
VMEM_LIMIT = 56 * 1024 * 1024
EXTRA = 16


def windows(full, kept):
    slack = full - kept
    tile = 256 - slack if 0 <= slack <= 128 else kept
    found = []
    base = 0
    while base < kept:
        rows = min(tile, kept - base)
        found.append((base, rows, rows + slack))
        base += rows
    return found


def pair_kernel(call, wins, n_sets, n_skip, meta_ref, shift_ref, ve1_ref, pick_ref, own_ref, other_ref, *rest):
    sets = [(rest[2 * k], rest[2 * k + 1]) for k in range(n_sets)]
    rest = rest[2 * n_sets + n_skip:]
    (out_ref, first, second, pick, side_a, side_b, e1_buf, out_buf,
     first_sem, second_sem, pick_sem, out_sem) = rest
    pairs_here = out_ref.shape[0]
    kept = out_ref.shape[1]
    half = own_ref.shape[2]
    n_first = first.shape[0]
    lo = meta_ref[0, call]
    hi = meta_ref[0, call + 1]
    base_first = meta_ref[1, 0]

    def first_copies():
        out = []
        for k in range(n_first):
            out.append(pltpu.make_async_copy(
                own_ref.at[base_first + k], first.at[k, :, pl.ds(0, half)], first_sem.at[2 * k]))
            out.append(pltpu.make_async_copy(
                other_ref.at[base_first + k], first.at[k, :, pl.ds(half, half)], first_sem.at[2 * k + 1]))
        return out

    def fetch(i, slot):
        p = meta_ref[2, i]
        which = meta_ref[3, p]
        idx = meta_ref[4, p]
        pltpu.make_async_copy(pick_ref.at[p], pick.at[slot], pick_sem.at[slot]).start()
        for k, (x_own, x_other) in enumerate(sets):
            @pl.when(which == k)
            def _():
                pltpu.make_async_copy(
                    x_own.at[idx], second.at[slot, :, pl.ds(0, half)], second_sem.at[slot, 0]).start()
                pltpu.make_async_copy(
                    x_other.at[idx], second.at[slot, :, pl.ds(half, half)], second_sem.at[slot, 1]).start()

    def await_fetch(slot):
        pltpu.make_async_copy(pick_ref.at[0], pick.at[slot], pick_sem.at[slot]).wait()
        for k in range(2):
            pltpu.make_async_copy(
                sets[0][0].at[0], second.at[slot, :, pl.ds(k * half, half)], second_sem.at[slot, k]).wait()

    def out_copy(p, slot):
        return pltpu.make_async_copy(out_buf.at[slot], out_ref.at[p], out_sem.at[slot])

    @pl.when(hi > lo)
    def _():
        for c in first_copies():
            c.start()
        fetch(lo, lax.rem(lo, 2))
        for c in first_copies():
            c.wait()

    def step(i, carry):
        slot = lax.rem(i, 2)
        p = meta_ref[2, i]
        f = p // (pairs_here // n_first)

        @pl.when(i + 1 < hi)
        def _():
            fetch(i + 1, 1 - slot)

        await_fetch(slot)

        @pl.when(i >= lo + 2)
        def _():
            out_copy(p, slot).wait()

        e2_parts = []
        full = ve1_ref.shape[1]
        for t, (base, rows, span) in enumerate(wins):
            one = pick[slot, 0, base:base + rows, 0:span]
            got = jnp.dot(one, first[f, base:base + span, :], preferred_element_type=jnp.float32)
            side_a[base:base + rows, :] = got.astype(jnp.bfloat16)
            e1_buf[base:base + rows, :] = jnp.dot(
                one, ve1_ref[f, base:base + span, :], preferred_element_type=jnp.float32)
            two = pick[slot, 1, base:base + rows, 0:span]
            got = jnp.dot(two, second[slot, base:base + span, :], preferred_element_type=jnp.float32)
            side_b[base:base + rows, :] = got.astype(jnp.bfloat16)
            ve = second[slot, full:full + EXTRA, 0:span]
            e2_parts.append(
                lax.dot_general(ve, two, NT, preferred_element_type=jnp.float32)[t:t + 1])
        e2 = jnp.concatenate(e2_parts, axis=1)
        shift = shift_ref[p]
        c = lax.dot_general(side_a[...], side_b[...], NT, preferred_element_type=jnp.float32)
        for col in range(0, kept, 128):
            den = e1_buf[...] + e2[:, col:col + 128] - shift
            inv = pl.reciprocal(den, approx=True)
            neg = inv * (den * inv - 2.0)
            out_buf[slot, :, col:col + 128] = (c[:, col:col + 128] * neg).astype(jnp.bfloat16)
        out_copy(p, slot).start()
        return carry

    lax.fori_loop(lo, hi, step, 0)

    @pl.when(hi - lo >= 2)
    def _():
        out_copy(0, lax.rem(hi, 2)).wait()

    @pl.when(hi > lo)
    def _():
        out_copy(0, lax.rem(hi + 1, 2)).wait()


def run_pairs(call, wins, meta, shift, ve1, pick, own, other, sets, after, prev):
    pairs_here, _, kept, span = pick.shape
    n_first = ve1.shape[0]
    full, half = own.shape[1], own.shape[2]
    any_spec = ANY_SPEC
    smem = pl.BlockSpec(memory_space=pltpu.SMEM)
    vmem = pl.BlockSpec(memory_space=pltpu.VMEM)
    operands = [meta, shift, ve1, pick, own, other]
    for pair in sets:
        operands += list(pair)
    operands += after
    in_specs = [smem, smem, vmem] + [any_spec] * (len(operands) - 3)
    aliases = {}
    if prev is not None:
        aliases = {len(operands): 0}
        operands.append(prev)
        in_specs.append(any_spec)
    bf = jnp.bfloat16
    return pl.pallas_call(
        functools.partial(pair_kernel, call, wins, len(sets), len(after) + (prev is not None)),
        out_shape=jax.ShapeDtypeStruct((pairs_here, kept, kept), bf),
        in_specs=in_specs,
        out_specs=any_spec,
        scratch_shapes=[
            pltpu.VMEM((n_first, full, 2 * half), bf),
            pltpu.VMEM((2, full, 2 * half), bf),
            pltpu.VMEM((2, 2, kept, span), bf),
            pltpu.VMEM((kept, 2 * half), bf),
            pltpu.VMEM((kept, 2 * half), bf),
            pltpu.VMEM((kept, 128), jnp.float32),
            pltpu.VMEM((2, kept, kept), bf),
            pltpu.SemaphoreType.DMA((2 * n_first,)),
            pltpu.SemaphoreType.DMA((2, 2)),
            pltpu.SemaphoreType.DMA((2,)),
            pltpu.SemaphoreType.DMA((2,)),
        ],
        input_output_aliases=aliases,
        compiler_params=pltpu.CompilerParams(vmem_limit_bytes=VMEM_LIMIT),
        cost_estimate=pl.CostEstimate(flops=0, bytes_accessed=0, transcendentals=0),
        name=f"pairs_{call}",
    )(*operands)


def set_kernel(n_arrays, n_skip, table_ref, *rest):
    arrays = rest[:n_arrays]
    out_ref, held, in_sems, out_sems = rest[n_arrays + n_skip:]
    count = out_ref.shape[0]
    for j in range(count):
        for k, a in enumerate(arrays):
            @pl.when(table_ref[0, j] == k)
            def _():
                pltpu.make_async_copy(a.at[table_ref[1, j]], held.at[j], in_sems.at[j]).start()
    for j in range(count):
        pltpu.make_async_copy(arrays[0].at[0], held.at[j], in_sems.at[j]).wait()
        pltpu.make_async_copy(held.at[j], out_ref.at[j], out_sems.at[j]).start()
    for j in range(count):
        pltpu.make_async_copy(held.at[j], out_ref.at[j], out_sems.at[j]).wait()


ANY_SPEC = pl.BlockSpec(memory_space=pl.ANY)


def copy_sets(which, index, arrays, after=()):
    n = len(index)
    table = jnp.stack([jnp.stack([jnp.asarray(w, jnp.int32) for w in which]), jnp.stack(index)])
    block = arrays[0].shape[1:]
    return pl.pallas_call(
        functools.partial(set_kernel, len(arrays), len(after)),
        out_shape=jax.ShapeDtypeStruct((n,) + block, arrays[0].dtype),
        in_specs=[pl.BlockSpec(memory_space=pltpu.SMEM)] + [ANY_SPEC] * (len(arrays) + len(after)),
        out_specs=ANY_SPEC,
        scratch_shapes=[
            pltpu.VMEM((n,) + block, arrays[0].dtype),
            pltpu.SemaphoreType.DMA((n,)),
            pltpu.SemaphoreType.DMA((n,))],
        cost_estimate=pl.CostEstimate(flops=0, bytes_accessed=0, transcendentals=0),
        compiler_params=pltpu.CompilerParams(vmem_limit_bytes=VMEM_LIMIT),
        name="copy_sets",
    )(table, *arrays, *after)


def extend_kernel(wins, blocks_ref, energy_ref, out_ref, held, in_sems, out_sems):
    count, full, half = blocks_ref.shape
    for k in range(count):
        pltpu.make_async_copy(blocks_ref.at[k], held.at[k, 0:full], in_sems.at[k]).start()
    energy = energy_ref[...].astype(jnp.float32)
    span = max(sp for _, _, sp in wins)
    row = lax.broadcasted_iota(jnp.int32, (EXTRA, span), 0)
    for k in range(count):
        held[k, full:, :] = jnp.zeros((EXTRA, half), held.dtype)
        rows = jnp.zeros((EXTRA, span), jnp.float32)
        for t, (base, _, sp) in enumerate(wins):
            piece = energy[k:k + 1, base:base + sp]
            if sp < span:
                piece = jnp.concatenate([piece, jnp.zeros((1, span - sp), jnp.float32)], axis=1)
            rows = jnp.where(row == t, jnp.broadcast_to(piece, (EXTRA, span)), rows)
        held[k, full:, 0:span] = rows.astype(held.dtype)
    for k in range(count):
        pltpu.make_async_copy(blocks_ref.at[k], held.at[k, 0:full], in_sems.at[k]).wait()
        pltpu.make_async_copy(held.at[k], out_ref.at[k], out_sems.at[k]).start()
    for k in range(count):
        pltpu.make_async_copy(held.at[k], out_ref.at[k], out_sems.at[k]).wait()


def extend(blocks, energy, wins):
    count, full, half = blocks.shape
    shape = (count, full + EXTRA, half)
    return pl.pallas_call(
        functools.partial(extend_kernel, wins),
        out_shape=jax.ShapeDtypeStruct(shape, blocks.dtype),
        in_specs=[ANY_SPEC, pl.BlockSpec(memory_space=pltpu.VMEM)],
        out_specs=ANY_SPEC,
        scratch_shapes=[
            pltpu.VMEM(shape, blocks.dtype), pltpu.SemaphoreType.DMA((count,)), pltpu.SemaphoreType.DMA((count,))],
        compiler_params=pltpu.CompilerParams(vmem_limit_bytes=VMEM_LIMIT),
        name="extend",
    )(blocks, energy)


def tie(x, deps):
    return pl.pallas_call(
        lambda *refs: None,
        out_shape=jax.ShapeDtypeStruct(x.shape, x.dtype),
        in_specs=[ANY_SPEC] * (1 + len(deps)),
        out_specs=ANY_SPEC,
        input_output_aliases={0: 0},
        compiler_params=pltpu.CompilerParams(vmem_limit_bytes=VMEM_LIMIT),
        cost_estimate=pl.CostEstimate(flops=0, bytes_accessed=0, transcendentals=0),
        name="tie",
    )(x, *deps)


def per_device(blocks, virt_energy, occ_energy, owner_slot, pairs, domains):
    orb_count = lax.axis_size("orb")
    aux_count = lax.axis_size("aux")
    occ_dev, full, half = blocks.shape
    pair_dev = pairs.shape[0]
    kept = domains.shape[2]
    own_rows = pair_dev // aux_count
    n_first = occ_dev // aux_count
    core = lax.axis_index("aux")
    o = lax.axis_index("orb")
    z, y = o // 2, o % 2
    chain = orb_count // 2
    last = chain - 1
    n_slots = orb_count * occ_dev
    i32 = jnp.int32
    wins = windows(full, kept)

    swap_aux = [(0, 1), (1, 0)]
    swap_y = [(k, k ^ 1) for k in range(orb_count)]

    def across_y(a):
        return lax.ppermute(a, "orb", swap_y)

    def across_aux(a):
        return lax.ppermute(a, "aux", swap_aux)

    def hop_down(a, d):
        return lax.ppermute(a, "orb", [(k, k - 2) for k in range(2, orb_count) if k // 2 <= chain - d])

    def hop_up(a, d):
        return lax.ppermute(a, "orb", [(k, k + 2) for k in range(orb_count - 2) if k // 2 >= d - 1])

    stored = extend(blocks, virt_energy, wins)

    downs, ups = [stored, hop_down(stored, 1)], [stored, hop_up(stored, 1)]
    local_other = across_aux(stored)

    orbitals = jnp.arange(owner_slot.shape[0], dtype=i32)
    hit_second = pairs[:, 1][:, None] == orbitals[None, :]
    slot_second = jnp.sum(jnp.where(hit_second, owner_slot[None, :], 0), axis=1)
    slots = jnp.arange(n_slots, dtype=i32)
    wanted_flat = jnp.any(slot_second[:, None] == slots[None, :], axis=0).astype(i32)
    wanted_flat = tie(wanted_flat, [stored])
    wanted = wanted_flat.reshape(orb_count, occ_dev) > 0
    wanted_opp = across_y(wanted_flat).reshape(orb_count, occ_dev) > 0
    top = orb_count - 1
    tell = [(0, 3), (1, 2), (top, top - 3), (top - 1, top - 2)]
    wanted_far = lax.ppermute(wanted_flat, "orb", tell).reshape(orb_count, occ_dev) > 0
    local = jnp.arange(occ_dev, dtype=i32)[None, :]

    def two_of(table):
        return jnp.min(jnp.where(table, local, occ_dev - 1), axis=1), jnp.max(jnp.where(table, local, 0), axis=1)

    want, want_opp = two_of(wanted), two_of(wanted_opp)

    def far_place(rows):
        w = rows.astype(i32)
        earlier = (jnp.arange(occ_dev)[:, None] < jnp.arange(occ_dev)[None, :]).astype(i32)
        ahead = jnp.sum(w[:, :, None] * earlier[None], axis=1)
        ahead_not = jnp.sum((1 - w)[:, :, None] * earlier[None], axis=1)
        return jnp.where(rows, ahead, jnp.sum(w, axis=1, keepdims=True) + ahead_not)

    first_row = core * own_rows
    own_second = lax.dynamic_slice_in_dim(slot_second, first_row, own_rows, 0)
    own_pairs = lax.dynamic_slice_in_dim(pairs, first_row, own_rows, 0)
    src = own_second // occ_dev
    part = own_second % occ_dev
    rank = jnp.any(
        (slot_second[None, :] // occ_dev == src[:, None]) & (slot_second[None, :] < own_second[:, None]),
        axis=1).astype(i32)
    src_z, src_y = src // 2, src % 2
    dist = jnp.abs(src_z - z)
    is_opp = (src_y != y).astype(i32)
    from_up = src_z < z
    place_table = far_place(wanted_opp).reshape(-1)
    far = jnp.sum(jnp.where(own_second[:, None] == slots[None, :], place_table[None, :], 0), axis=1)
    both = 2 * dist <= chain - 1
    is_far = (dist == last) & (is_opp == 0)
    idx = jnp.where((dist == 0) & (is_opp == 0), part, rank + jnp.where(both & from_up, 2, 0))
    idx = jnp.where(is_far, far % 2, idx)
    which = jnp.where(is_far & (far < 2), 2, is_opp)
    stage = dist - (is_far & (far < 2)).astype(i32)
    rows = jnp.arange(own_rows, dtype=i32)
    before = (stage[None, :] < stage[:, None]) | ((stage[None, :] == stage[:, None]) & (rows[None, :] < rows[:, None]))
    place = jnp.sum(before.astype(i32), axis=1)
    order = jnp.sum(jnp.where(place[None, :] == rows[:, None], rows[None, :], 0), axis=1)
    bounds = jnp.sum((stage[None, :] < jnp.arange(chain + 1, dtype=i32)[:, None]).astype(i32), axis=1)
    width = max(own_rows, chain + 1)

    def padded(v):
        v = v.reshape(-1)
        return jnp.pad(v, (0, width - v.shape[0]))

    meta = jnp.stack([padded(bounds), padded(core * n_first), padded(order), padded(which), padded(idx)])

    def occ(col):
        hit = own_pairs[:, col][:, None] == orbitals[None, :]
        return jnp.sum(jnp.where(hit, occ_energy[None, :], 0.0), axis=1)

    shift = occ(0) + occ(1)
    ve1 = lax.dynamic_slice_in_dim(virt_energy, core * n_first, n_first, 0)
    ve1 = jnp.broadcast_to(ve1[:, :, None], (n_first, full, 128))

    dom = lax.dynamic_slice_in_dim(domains, first_row, own_rows, 0)
    base = jnp.concatenate([jnp.full((r,), b, i32) for b, r, _ in wins])
    span = max(sp for _, _, sp in wins)
    pick = ((dom - base)[..., None] == jnp.arange(span, dtype=i32)).astype(jnp.bfloat16)

    def idx_of(table, source):
        return lax.dynamic_index_in_dim(table, jnp.clip(source, 0, orb_count - 1), 0, keepdims=False)

    def two_for(table, source):
        return [idx_of(table[0], source), idx_of(table[1], source)]

    sets = {}

    def pairs_at(d, after, prev):
        return run_pairs(d, wins, meta, shift, ve1, pick, stored, local_other, sets[d], after, prev)

    def with_other(a):
        return a, across_aux(a)

    y_load = copy_sets([0, 0], two_for(want_opp, o), [stored])
    y_own, y_other = with_other(across_y(y_load))
    sets[0] = [(stored, local_other), (y_own, y_other)]
    early = [y_other, local_other, pick, meta]
    downs[1], ups[1] = tie(downs[1], early), tie(ups[1], early)
    out = None
    opp = None
    for d in range(1, last):
        s_down, s_up = o + 2 * d, o - 2 * d
        first = []
        if d + 1 < last:
            downs.append(hop_down(downs[d], d + 1))
            ups.append(hop_up(ups[d], d + 1))
        else:
            sends_down = z == 1
            turn_of = idx_of(far_place(wanted_far), jnp.where(sends_down, 2 * last + y, y))
            turn = [jnp.sum(jnp.where(turn_of == j, local[0], 0)) for j in range(occ_dev)]
            perm = [(2, 0), (3, 1), (2 * (last - 1), 2 * last), (2 * (last - 1) + 1, 2 * last + 1)]
            is_up = 1 - sends_down.astype(i32)
            load_a = copy_sets([is_up, is_up], turn[:2], [downs[d], ups[d]], [mine_other] if d > 1 else [])
            load_b = copy_sets([is_up, is_up], turn[2:], [downs[d], ups[d]], [load_a])
            got_a, got_b = lax.ppermute(load_a, "orb", perm), lax.ppermute(load_b, "orb", perm)
            first = [load_b]
        if 2 * d <= last:
            place_of = [0, 0, 1, 1]

            def both_ways(table):
                return two_for(table, s_down) + two_for(table, s_up)
        else:
            is_up = (z + d > last).astype(i32)
            place_of = [is_up, is_up]

            def both_ways(table):
                return two_for(table, jnp.where(is_up == 1, s_up, s_down))
        theirs = copy_sets(place_of, both_ways(want_opp), [downs[d], ups[d]], first)
        mine = copy_sets(place_of, both_ways(want), [downs[d], ups[d]], [theirs])
        if d > 1:
            sets[d - 1] = [(prev_mine, mine_other), with_other(tie(opp, first) if first else opp)]
            out = pairs_at(d - 2, [mine] + first, out)
        opp = across_y(theirs)
        prev_mine, mine_other = with_other(mine)
    got_a = tie(got_a, [out])
    far_opp = across_y(got_a)
    out = pairs_at(last - 2, [got_a], out)
    sets[last - 1] = [(prev_mine, mine_other), with_other(tie(opp, [out])), with_other(got_a)]
    out = pairs_at(last - 1, [], out)
    sets[last] = [with_other(tie(got_b, [out])), with_other(tie(far_opp, [out]))]
    return pairs_at(last, [], out)


def solution(mesh):
    in_specs = (
        P(("groups", "orb"), None, "aux"),
        P(("groups", "orb"), None),
        P("groups"),
        P("groups"),
        P(("groups", "orb"), None),
        P(("groups", "orb"), None, None),
    )
    out_specs = P(("groups", "orb", "aux"), None, None)
    return jax.shard_map(
        per_device, mesh=mesh, in_specs=in_specs, out_specs=out_specs, check_vma=False
    )
```

```python
import functools

import jax
import jax.numpy as jnp
from jax import lax
from jax.experimental import pallas as pl
from jax.experimental.pallas import tpu as pltpu
from jax.sharding import PartitionSpec as P

NT = (((1,), (1,)), ((), ()))
VMEM_LIMIT = 56 * 1024 * 1024
EXTRA = 16


def windows(full, kept):
    slack = full - kept
    tile = 256 - slack if 0 <= slack <= 128 else kept
    found = []
    base = 0
    while base < kept:
        rows = min(tile, kept - base)
        found.append((base, rows, rows + slack))
        base += rows
    return found


def pair_kernel(call, wins, n_sets, n_skip, meta_ref, shift_ref, ve1_ref, pick_ref, own_ref, other_ref, *rest):
    sets = [(rest[2 * k], rest[2 * k + 1]) for k in range(n_sets)]
    rest = rest[2 * n_sets + n_skip:]
    (out_ref, first, second, pick, side_a, side_b, e1_buf, out_buf,
     first_sem, second_sem, pick_sem, out_sem) = rest
    pairs_here = out_ref.shape[0]
    kept = out_ref.shape[1]
    half = own_ref.shape[2]
    n_first = first.shape[0]
    lo = meta_ref[0, call]
    hi = meta_ref[0, call + 1]
    base_first = meta_ref[1, 0]

    def first_copies():
        out = []
        for k in range(n_first):
            out.append(pltpu.make_async_copy(
                own_ref.at[base_first + k], first.at[k, :, pl.ds(0, half)], first_sem.at[2 * k]))
            out.append(pltpu.make_async_copy(
                other_ref.at[base_first + k], first.at[k, :, pl.ds(half, half)], first_sem.at[2 * k + 1]))
        return out

    def fetch(i, slot):
        p = meta_ref[2, i]
        which = meta_ref[3, p]
        idx = meta_ref[4, p]
        pltpu.make_async_copy(pick_ref.at[p], pick.at[slot], pick_sem.at[slot]).start()
        for k, (x_own, x_other) in enumerate(sets):
            @pl.when(which == k)
            def _():
                pltpu.make_async_copy(
                    x_own.at[idx], second.at[slot, :, pl.ds(0, half)], second_sem.at[slot, 0]).start()
                pltpu.make_async_copy(
                    x_other.at[idx], second.at[slot, :, pl.ds(half, half)], second_sem.at[slot, 1]).start()

    def await_fetch(slot):
        pltpu.make_async_copy(pick_ref.at[0], pick.at[slot], pick_sem.at[slot]).wait()
        for k in range(2):
            pltpu.make_async_copy(
                sets[0][0].at[0], second.at[slot, :, pl.ds(k * half, half)], second_sem.at[slot, k]).wait()

    def out_copy(p, slot):
        return pltpu.make_async_copy(out_buf.at[slot], out_ref.at[p], out_sem.at[slot])

    @pl.when(hi > lo)
    def _():
        for c in first_copies():
            c.start()
        fetch(lo, lax.rem(lo, 2))
        for c in first_copies():
            c.wait()

    def step(i, carry):
        slot = lax.rem(i, 2)
        p = meta_ref[2, i]
        f = p // (pairs_here // n_first)

        @pl.when(i + 1 < hi)
        def _():
            fetch(i + 1, 1 - slot)

        await_fetch(slot)

        @pl.when(i >= lo + 2)
        def _():
            out_copy(p, slot).wait()

        e2_parts = []
        full = ve1_ref.shape[1]
        for t, (base, rows, span) in enumerate(wins):
            one = pick[slot, 0, base:base + rows, 0:span]
            got = jnp.dot(one, first[f, base:base + span, :], preferred_element_type=jnp.float32)
            side_a[base:base + rows, :] = got.astype(jnp.bfloat16)
            e1_buf[base:base + rows, :] = jnp.dot(
                one, ve1_ref[f, base:base + span, :], preferred_element_type=jnp.float32)
            two = pick[slot, 1, base:base + rows, 0:span]
            got = jnp.dot(two, second[slot, base:base + span, :], preferred_element_type=jnp.float32)
            side_b[base:base + rows, :] = got.astype(jnp.bfloat16)
            ve = second[slot, full:full + EXTRA, 0:span]
            e2_parts.append(
                lax.dot_general(ve, two, NT, preferred_element_type=jnp.float32)[t:t + 1])
        e2 = jnp.concatenate(e2_parts, axis=1)
        shift = shift_ref[p]
        c = lax.dot_general(side_a[...], side_b[...], NT, preferred_element_type=jnp.float32)
        for col in range(0, kept, 128):
            den = e1_buf[...] + e2[:, col:col + 128] - shift
            inv = pl.reciprocal(den, approx=True)
            neg = inv * (den * inv - 2.0)
            out_buf[slot, :, col:col + 128] = (c[:, col:col + 128] * neg).astype(jnp.bfloat16)
        out_copy(p, slot).start()
        return carry

    lax.fori_loop(lo, hi, step, 0)

    @pl.when(hi - lo >= 2)
    def _():
        out_copy(0, lax.rem(hi, 2)).wait()

    @pl.when(hi > lo)
    def _():
        out_copy(0, lax.rem(hi + 1, 2)).wait()


def run_pairs(call, wins, meta, shift, ve1, pick, own, other, sets, after, prev):
    pairs_here, _, kept, span = pick.shape
    n_first = ve1.shape[0]
    full, half = own.shape[1], own.shape[2]
    any_spec = ANY_SPEC
    smem = pl.BlockSpec(memory_space=pltpu.SMEM)
    vmem = pl.BlockSpec(memory_space=pltpu.VMEM)
    operands = [meta, shift, ve1, pick, own, other]
    for pair in sets:
        operands += list(pair)
    operands += after
    in_specs = [smem, smem, vmem] + [any_spec] * (len(operands) - 3)
    aliases = {}
    if prev is not None:
        aliases = {len(operands): 0}
        operands.append(prev)
        in_specs.append(any_spec)
    bf = jnp.bfloat16
    return pl.pallas_call(
        functools.partial(pair_kernel, call, wins, len(sets), len(after) + (prev is not None)),
        out_shape=jax.ShapeDtypeStruct((pairs_here, kept, kept), bf),
        in_specs=in_specs,
        out_specs=any_spec,
        scratch_shapes=[
            pltpu.VMEM((n_first, full, 2 * half), bf),
            pltpu.VMEM((2, full, 2 * half), bf),
            pltpu.VMEM((2, 2, kept, span), bf),
            pltpu.VMEM((kept, 2 * half), bf),
            pltpu.VMEM((kept, 2 * half), bf),
            pltpu.VMEM((kept, 128), jnp.float32),
            pltpu.VMEM((2, kept, kept), bf),
            pltpu.SemaphoreType.DMA((2 * n_first,)),
            pltpu.SemaphoreType.DMA((2, 2)),
            pltpu.SemaphoreType.DMA((2,)),
            pltpu.SemaphoreType.DMA((2,)),
        ],
        input_output_aliases=aliases,
        compiler_params=pltpu.CompilerParams(vmem_limit_bytes=VMEM_LIMIT),
        cost_estimate=pl.CostEstimate(flops=0, bytes_accessed=0, transcendentals=0),
        name=f"pairs_{call}",
    )(*operands)


def set_kernel(n_arrays, n_skip, table_ref, *rest):
    arrays = rest[:n_arrays]
    out_ref, held, in_sems, out_sems = rest[n_arrays + n_skip:]
    count = out_ref.shape[0]
    for j in range(count):
        for k, a in enumerate(arrays):
            @pl.when(table_ref[0, j] == k)
            def _():
                pltpu.make_async_copy(a.at[table_ref[1, j]], held.at[j], in_sems.at[j]).start()
    for j in range(count):
        pltpu.make_async_copy(arrays[0].at[0], held.at[j], in_sems.at[j]).wait()
        pltpu.make_async_copy(held.at[j], out_ref.at[j], out_sems.at[j]).start()
    for j in range(count):
        pltpu.make_async_copy(held.at[j], out_ref.at[j], out_sems.at[j]).wait()


ANY_SPEC = pl.BlockSpec(memory_space=pl.ANY)


def copy_sets(which, index, arrays, after=()):
    n = len(index)
    table = jnp.stack([jnp.stack([jnp.asarray(w, jnp.int32) for w in which]), jnp.stack(index)])
    block = arrays[0].shape[1:]
    return pl.pallas_call(
        functools.partial(set_kernel, len(arrays), len(after)),
        out_shape=jax.ShapeDtypeStruct((n,) + block, arrays[0].dtype),
        in_specs=[pl.BlockSpec(memory_space=pltpu.SMEM)] + [ANY_SPEC] * (len(arrays) + len(after)),
        out_specs=ANY_SPEC,
        scratch_shapes=[
            pltpu.VMEM((n,) + block, arrays[0].dtype),
            pltpu.SemaphoreType.DMA((n,)),
            pltpu.SemaphoreType.DMA((n,))],
        cost_estimate=pl.CostEstimate(flops=0, bytes_accessed=0, transcendentals=0),
        compiler_params=pltpu.CompilerParams(vmem_limit_bytes=VMEM_LIMIT),
        name="copy_sets",
    )(table, *arrays, *after)


def extend_kernel(wins, blocks_ref, energy_ref, out_ref, held, in_sems, out_sems):
    count, full, half = blocks_ref.shape
    for k in range(count):
        pltpu.make_async_copy(blocks_ref.at[k], held.at[k, 0:full], in_sems.at[k]).start()
    energy = energy_ref[...].astype(jnp.float32)
    span = max(sp for _, _, sp in wins)
    row = lax.broadcasted_iota(jnp.int32, (EXTRA, span), 0)
    for k in range(count):
        held[k, full:, :] = jnp.zeros((EXTRA, half), held.dtype)
        rows = jnp.zeros((EXTRA, span), jnp.float32)
        for t, (base, _, sp) in enumerate(wins):
            piece = energy[k:k + 1, base:base + sp]
            if sp < span:
                piece = jnp.concatenate([piece, jnp.zeros((1, span - sp), jnp.float32)], axis=1)
            rows = jnp.where(row == t, jnp.broadcast_to(piece, (EXTRA, span)), rows)
        held[k, full:, 0:span] = rows.astype(held.dtype)
    for k in range(count):
        pltpu.make_async_copy(blocks_ref.at[k], held.at[k, 0:full], in_sems.at[k]).wait()
        pltpu.make_async_copy(held.at[k], out_ref.at[k], out_sems.at[k]).start()
    for k in range(count):
        pltpu.make_async_copy(held.at[k], out_ref.at[k], out_sems.at[k]).wait()


def extend(blocks, energy, wins):
    count, full, half = blocks.shape
    shape = (count, full + EXTRA, half)
    return pl.pallas_call(
        functools.partial(extend_kernel, wins),
        out_shape=jax.ShapeDtypeStruct(shape, blocks.dtype),
        in_specs=[ANY_SPEC, pl.BlockSpec(memory_space=pltpu.VMEM)],
        out_specs=ANY_SPEC,
        scratch_shapes=[
            pltpu.VMEM(shape, blocks.dtype), pltpu.SemaphoreType.DMA((count,)), pltpu.SemaphoreType.DMA((count,))],
        compiler_params=pltpu.CompilerParams(vmem_limit_bytes=VMEM_LIMIT),
        name="extend",
    )(blocks, energy)


def tie(x, deps):
    return pl.pallas_call(
        lambda *refs: None,
        out_shape=jax.ShapeDtypeStruct(x.shape, x.dtype),
        in_specs=[ANY_SPEC] * (1 + len(deps)),
        out_specs=ANY_SPEC,
        input_output_aliases={0: 0},
        compiler_params=pltpu.CompilerParams(vmem_limit_bytes=VMEM_LIMIT),
        cost_estimate=pl.CostEstimate(flops=0, bytes_accessed=0, transcendentals=0),
        name="tie",
    )(x, *deps)


def per_device(blocks, virt_energy, occ_energy, owner_slot, pairs, domains):
    orb_count = lax.axis_size("orb")
    aux_count = lax.axis_size("aux")
    occ_dev, full, half = blocks.shape
    pair_dev = pairs.shape[0]
    kept = domains.shape[2]
    own_rows = pair_dev // aux_count
    n_first = occ_dev // aux_count
    core = lax.axis_index("aux")
    o = lax.axis_index("orb")
    z, y = o // 2, o % 2
    chain = orb_count // 2
    last = chain - 1
    n_slots = orb_count * occ_dev
    i32 = jnp.int32
    wins = windows(full, kept)

    swap_aux = [(0, 1), (1, 0)]
    swap_y = [(k, k ^ 1) for k in range(orb_count)]

    def across_y(a):
        return lax.ppermute(a, "orb", swap_y)

    def across_aux(a):
        return lax.ppermute(a, "aux", swap_aux)

    def hop_down(a, d):
        return lax.ppermute(a, "orb", [(k, k - 2) for k in range(2, orb_count) if k // 2 <= chain - d])

    def hop_up(a, d):
        return lax.ppermute(a, "orb", [(k, k + 2) for k in range(orb_count - 2) if k // 2 >= d - 1])

    stored = extend(blocks, virt_energy, wins)

    downs, ups = [stored, hop_down(stored, 1)], [stored, hop_up(stored, 1)]
    local_other = across_aux(stored)

    orbitals = jnp.arange(owner_slot.shape[0], dtype=i32)
    hit_second = pairs[:, 1][:, None] == orbitals[None, :]
    slot_second = jnp.sum(jnp.where(hit_second, owner_slot[None, :], 0), axis=1)
    slots = jnp.arange(n_slots, dtype=i32)
    wanted_flat = jnp.any(slot_second[:, None] == slots[None, :], axis=0).astype(i32)
    wanted_flat = tie(wanted_flat, [stored])
    wanted = wanted_flat.reshape(orb_count, occ_dev) > 0
    wanted_both = jnp.stack([wanted_flat, across_y(wanted_flat)])
    wanted_opp = wanted_both[1].reshape(orb_count, occ_dev) > 0
    local = jnp.arange(occ_dev, dtype=i32)[None, :]

    def two_of(table):
        return jnp.min(jnp.where(table, local, occ_dev - 1), axis=1), jnp.max(jnp.where(table, local, 0), axis=1)

    want, want_opp = two_of(wanted), two_of(wanted_opp)

    first_row = core * own_rows
    own_second = lax.dynamic_slice_in_dim(slot_second, first_row, own_rows, 0)
    own_pairs = lax.dynamic_slice_in_dim(pairs, first_row, own_rows, 0)
    src = own_second // occ_dev
    part = own_second % occ_dev
    rank = jnp.any(
        (slot_second[None, :] // occ_dev == src[:, None]) & (slot_second[None, :] < own_second[:, None]),
        axis=1).astype(i32)
    src_z, src_y = src // 2, src % 2
    dist = jnp.abs(src_z - z)
    is_opp = (src_y != y).astype(i32)
    from_up = src_z < z
    both = 2 * dist <= chain - 1
    is_far = dist == last
    at_hand = (dist <= 1) & (is_opp == 0)
    idx = jnp.where(at_hand, part, rank + jnp.where(both & from_up, 2, 0))
    which_col = jnp.where(dist == 0, 3, jnp.where((dist == 1) & from_up, 2, jnp.where(is_far, 2, 1)))
    which = jnp.where(is_opp == 1, is_far.astype(i32), which_col)
    stage_col = jnp.where(is_far, last - 2, jnp.maximum(dist - 1, 0))
    stage = jnp.where(is_opp == 1, jnp.minimum(dist, last - 1), stage_col)
    rows = jnp.arange(own_rows, dtype=i32)
    before = (stage[None, :] < stage[:, None]) | ((stage[None, :] == stage[:, None]) & (rows[None, :] < rows[:, None]))
    place = jnp.sum(before.astype(i32), axis=1)
    order = jnp.sum(jnp.where(place[None, :] == rows[:, None], rows[None, :], 0), axis=1)
    bounds = jnp.sum((stage[None, :] < jnp.arange(chain + 1, dtype=i32)[:, None]).astype(i32), axis=1)
    width = max(own_rows, chain + 1)

    def padded(v):
        v = v.reshape(-1)
        return jnp.pad(v, (0, width - v.shape[0]))

    meta = jnp.stack([padded(bounds), padded(core * n_first), padded(order), padded(which), padded(idx)])

    def occ(col):
        hit = own_pairs[:, col][:, None] == orbitals[None, :]
        return jnp.sum(jnp.where(hit, occ_energy[None, :], 0.0), axis=1)

    shift = occ(0) + occ(1)
    ve1 = lax.dynamic_slice_in_dim(virt_energy, core * n_first, n_first, 0)
    ve1 = jnp.broadcast_to(ve1[:, :, None], (n_first, full, 128))

    dom = lax.dynamic_slice_in_dim(domains, first_row, own_rows, 0)
    base = jnp.concatenate([jnp.full((r,), b, i32) for b, r, _ in wins])
    span = max(sp for _, _, sp in wins)
    pick = ((dom - base)[..., None] == jnp.arange(span, dtype=i32)).astype(jnp.bfloat16)

    def idx_of(table, source):
        return lax.dynamic_index_in_dim(table, jnp.clip(source, 0, orb_count - 1), 0, keepdims=False)

    def two_for(table, source):
        return [idx_of(table[0], source), idx_of(table[1], source)]

    sets = {}

    def pairs_at(d, after, prev):
        return run_pairs(d, wins, meta, shift, ve1, pick, stored, local_other, sets[d], after, prev)

    def with_other(a):
        return a, across_aux(a)

    y_load = copy_sets([0, 0], two_for(want_opp, o), [stored])
    opp = with_other(across_y(y_load))
    top = orb_count - 1
    tell = [(0, 2), (1, 3), (top, top - 2), (top - 1, top - 3)]
    wanted_far = lax.ppermute(tie(wanted_both, [y_load]), "orb", tell).reshape(2, orb_count, occ_dev) > 0
    far_own, far_opp = two_of(wanted_far[0]), two_of(wanted_far[1])
    early = [opp[1], local_other, pick, meta]
    downs[1], ups[1] = tie(downs[1], early), tie(ups[1], early)
    out = None
    for d in range(1, last):
        s_down, s_up = o + 2 * d, o - 2 * d
        first = []
        if d + 1 < last:
            downs.append(hop_down(downs[d], d + 1))
            ups.append(hop_up(ups[d], d + 1))
        else:
            sends_down = z == 1
            source = jnp.where(sends_down, 2 * last + y, y)
            from_set = [1 - sends_down.astype(i32)] * 2
            perm = [(2, 0), (3, 1), (2 * (last - 1), 2 * last), (2 * (last - 1) + 1, 2 * last + 1)]
            load_over = copy_sets(from_set, two_for(far_opp, source), [downs[d], ups[d]], [out])
            load_own = copy_sets(from_set, two_for(far_own, source), [downs[d], ups[d]], [load_over])
            far_b = lax.ppermute(across_y(load_over), "orb", perm)
            far_a = lax.ppermute(load_own, "orb", perm)
            first = [load_own]
        if 2 * d <= last:
            place_of = [0, 0, 1, 1]

            def both_ways(table):
                return two_for(table, s_down) + two_for(table, s_up)
        else:
            is_up = (z + d > last).astype(i32)
            place_of = [is_up, is_up]

            def both_ways(table):
                return two_for(table, jnp.where(is_up == 1, s_up, s_down))
        theirs = copy_sets(place_of, both_ways(want_opp), [downs[d], ups[d]], first)
        if d == 1:
            sets[0] = [opp, with_other(downs[1]), with_other(ups[1]), (stored, local_other)]
            out = pairs_at(0, [theirs], out)
        else:
            mine = copy_sets(place_of, both_ways(want), [downs[d], ups[d]], [theirs])
            sets[d - 1] = [with_other(tie(opp, first) if first else opp), with_other(mine)]
            if d + 1 == last:
                sets[d - 1].append(with_other(far_a))
            out = pairs_at(d - 1, [mine], out)
        opp = across_y(theirs)
    sets[last - 1] = [with_other(tie(opp, [out])), with_other(tie(far_b, [out]))]
    return pairs_at(last - 1, [], out)


def solution(mesh):
    in_specs = (
        P(("groups", "orb"), None, "aux"),
        P(("groups", "orb"), None),
        P("groups"),
        P("groups"),
        P(("groups", "orb"), None),
        P(("groups", "orb"), None, None),
    )
    out_specs = P(("groups", "orb", "aux"), None, None)
    return jax.shard_map(
        per_device, mesh=mesh, in_specs=in_specs, out_specs=out_specs, check_vma=False
    )
```

```python
import functools

import jax
import jax.numpy as jnp
from jax import lax
from jax.experimental import pallas as pl
from jax.experimental.pallas import tpu as pltpu
from jax.sharding import PartitionSpec as P

NT = (((1,), (1,)), ((), ()))
VMEM_LIMIT = 56 * 1024 * 1024
EXTRA = 16


def windows(full, kept):
    slack = full - kept
    tile = 256 - slack if 0 <= slack <= 128 else kept
    found = []
    base = 0
    while base < kept:
        rows = min(tile, kept - base)
        found.append((base, rows, rows + slack))
        base += rows
    return found


def pair_kernel(call, wins, n_sets, n_skip, meta_ref, shift_ref, ve1_ref, pick_ref, own_ref, other_ref, *rest):
    sets = [(rest[2 * k], rest[2 * k + 1]) for k in range(n_sets)]
    rest = rest[2 * n_sets + n_skip:]
    (out_ref, first, second, pick, side_a, side_b, e1_buf, out_buf,
     first_sem, second_sem, pick_sem, out_sem) = rest
    pairs_here = out_ref.shape[0]
    kept = out_ref.shape[1]
    half = own_ref.shape[2]
    n_first = first.shape[0]
    lo = meta_ref[0, call]
    hi = meta_ref[0, call + 1]
    base_first = meta_ref[1, 0]

    def first_copies():
        out = []
        for k in range(n_first):
            out.append(pltpu.make_async_copy(
                own_ref.at[base_first + k], first.at[k, :, pl.ds(0, half)], first_sem.at[2 * k]))
            out.append(pltpu.make_async_copy(
                other_ref.at[base_first + k], first.at[k, :, pl.ds(half, half)], first_sem.at[2 * k + 1]))
        return out

    def fetch(i, slot):
        p = meta_ref[2, i]
        which = meta_ref[3, p]
        idx = meta_ref[4, p]
        pltpu.make_async_copy(pick_ref.at[p], pick.at[slot], pick_sem.at[slot]).start()
        for k, (x_own, x_other) in enumerate(sets):
            @pl.when(which == k)
            def _():
                pltpu.make_async_copy(
                    x_own.at[idx], second.at[slot, :, pl.ds(0, half)], second_sem.at[slot, 0]).start()
                pltpu.make_async_copy(
                    x_other.at[idx], second.at[slot, :, pl.ds(half, half)], second_sem.at[slot, 1]).start()

    def await_fetch(slot):
        pltpu.make_async_copy(pick_ref.at[0], pick.at[slot], pick_sem.at[slot]).wait()
        for k in range(2):
            pltpu.make_async_copy(
                sets[0][0].at[0], second.at[slot, :, pl.ds(k * half, half)], second_sem.at[slot, k]).wait()

    def out_copy(p, slot):
        return pltpu.make_async_copy(out_buf.at[slot], out_ref.at[p], out_sem.at[slot])

    @pl.when(hi > lo)
    def _():
        for c in first_copies():
            c.start()
        fetch(lo, lax.rem(lo, 2))
        for c in first_copies():
            c.wait()

    def step(i, carry):
        slot = lax.rem(i, 2)
        p = meta_ref[2, i]
        f = p // (pairs_here // n_first)

        @pl.when(i + 1 < hi)
        def _():
            fetch(i + 1, 1 - slot)

        await_fetch(slot)

        @pl.when(i >= lo + 2)
        def _():
            out_copy(p, slot).wait()

        e2_parts = []
        full = ve1_ref.shape[1]
        for t, (base, rows, span) in enumerate(wins):
            one = pick[slot, 0, base:base + rows, 0:span]
            got = jnp.dot(one, first[f, base:base + span, :], preferred_element_type=jnp.float32)
            side_a[base:base + rows, :] = got.astype(jnp.bfloat16)
            e1_buf[base:base + rows, :] = jnp.dot(
                one, ve1_ref[f, base:base + span, :], preferred_element_type=jnp.float32)
            two = pick[slot, 1, base:base + rows, 0:span]
            got = jnp.dot(two, second[slot, base:base + span, :], preferred_element_type=jnp.float32)
            side_b[base:base + rows, :] = got.astype(jnp.bfloat16)
            ve = second[slot, full:full + EXTRA, 0:span]
            e2_parts.append(
                lax.dot_general(ve, two, NT, preferred_element_type=jnp.float32)[t:t + 1])
        e2 = jnp.concatenate(e2_parts, axis=1)
        shift = shift_ref[p]
        chunk = min(kept, 256)
        for start in range(0, kept, chunk):
            c = lax.dot_general(
                side_a[...], side_b[start:start + chunk, :], NT, preferred_element_type=jnp.float32)
            for col in range(0, chunk, 128):
                den = e1_buf[...] + e2[:, start + col:start + col + 128] - shift
                inv = pl.reciprocal(den, approx=True)
                neg = inv * (den * inv - 2.0)
                out_buf[slot, :, start + col:start + col + 128] = (
                    c[:, col:col + 128] * neg).astype(jnp.bfloat16)
        out_copy(p, slot).start()
        return carry

    lax.fori_loop(lo, hi, step, 0)

    @pl.when(hi - lo >= 2)
    def _():
        out_copy(0, lax.rem(hi, 2)).wait()

    @pl.when(hi > lo)
    def _():
        out_copy(0, lax.rem(hi + 1, 2)).wait()


def run_pairs(call, wins, meta, shift, ve1, pick, own, other, sets, after, prev):
    pairs_here, _, kept, span = pick.shape
    n_first = ve1.shape[0]
    full, half = own.shape[1], own.shape[2]
    any_spec = ANY_SPEC
    smem = pl.BlockSpec(memory_space=pltpu.SMEM)
    vmem = pl.BlockSpec(memory_space=pltpu.VMEM)
    operands = [meta, shift, ve1, pick, own, other]
    for pair in sets:
        operands += list(pair)
    operands += after
    in_specs = [smem, smem, vmem] + [any_spec] * (len(operands) - 3)
    aliases = {}
    if prev is not None:
        aliases = {len(operands): 0}
        operands.append(prev)
        in_specs.append(any_spec)
    bf = jnp.bfloat16
    return pl.pallas_call(
        functools.partial(pair_kernel, call, wins, len(sets), len(after) + (prev is not None)),
        out_shape=jax.ShapeDtypeStruct((pairs_here, kept, kept), bf),
        in_specs=in_specs,
        out_specs=any_spec,
        scratch_shapes=[
            pltpu.VMEM((n_first, full, 2 * half), bf),
            pltpu.VMEM((2, full, 2 * half), bf),
            pltpu.VMEM((2, 2, kept, span), bf),
            pltpu.VMEM((kept, 2 * half), bf),
            pltpu.VMEM((kept, 2 * half), bf),
            pltpu.VMEM((kept, 128), jnp.float32),
            pltpu.VMEM((2, kept, kept), bf),
            pltpu.SemaphoreType.DMA((2 * n_first,)),
            pltpu.SemaphoreType.DMA((2, 2)),
            pltpu.SemaphoreType.DMA((2,)),
            pltpu.SemaphoreType.DMA((2,)),
        ],
        input_output_aliases=aliases,
        compiler_params=pltpu.CompilerParams(vmem_limit_bytes=VMEM_LIMIT),
        cost_estimate=pl.CostEstimate(flops=0, bytes_accessed=0, transcendentals=0),
        name=f"pairs_{call}",
    )(*operands)


def set_kernel(n_arrays, n_skip, sizes, table_ref, *rest):
    arrays = rest[:n_arrays]
    outs = rest[n_arrays + n_skip:-3]
    held, in_sems, out_sems = rest[-3:]
    places = [(o, k) for o, size in zip(outs, sizes) for k in range(size)]
    for j in range(len(places)):
        for k, a in enumerate(arrays):
            @pl.when(table_ref[0, j] == k)
            def _():
                pltpu.make_async_copy(a.at[table_ref[1, j]], held.at[j], in_sems.at[j]).start()
    for j, (o, k) in enumerate(places):
        pltpu.make_async_copy(arrays[0].at[0], held.at[j], in_sems.at[j]).wait()
        pltpu.make_async_copy(held.at[j], o.at[k], out_sems.at[j]).start()
    for j, (o, k) in enumerate(places):
        pltpu.make_async_copy(held.at[j], o.at[k], out_sems.at[j]).wait()


ANY_SPEC = pl.BlockSpec(memory_space=pl.ANY)


def copy_sets(which, index, arrays, after=(), sizes=None):
    n = len(index)
    sizes = sizes or [n]
    table = jnp.stack([jnp.stack([jnp.asarray(w, jnp.int32) for w in which]), jnp.stack(index)])
    block = arrays[0].shape[1:]
    outs = pl.pallas_call(
        functools.partial(set_kernel, len(arrays), len(after), sizes),
        out_shape=[jax.ShapeDtypeStruct((size,) + block, arrays[0].dtype) for size in sizes],
        in_specs=[pl.BlockSpec(memory_space=pltpu.SMEM)] + [ANY_SPEC] * (len(arrays) + len(after)),
        out_specs=[ANY_SPEC] * len(sizes),
        scratch_shapes=[
            pltpu.VMEM((n,) + block, arrays[0].dtype),
            pltpu.SemaphoreType.DMA((n,)),
            pltpu.SemaphoreType.DMA((n,))],
        cost_estimate=pl.CostEstimate(flops=0, bytes_accessed=0, transcendentals=0),
        compiler_params=pltpu.CompilerParams(vmem_limit_bytes=VMEM_LIMIT),
        name="copy_sets",
    )(table, *arrays, *after)
    return outs if len(sizes) > 1 else outs[0]


def extend_kernel(wins, blocks_ref, energy_ref, out_ref, held, in_sems, out_sems):
    count, full, half = blocks_ref.shape
    for k in range(count):
        pltpu.make_async_copy(blocks_ref.at[k], held.at[k, 0:full], in_sems.at[k]).start()
    energy = energy_ref[...].astype(jnp.float32)
    span = max(sp for _, _, sp in wins)
    row = lax.broadcasted_iota(jnp.int32, (EXTRA, span), 0)
    for k in range(count):
        held[k, full:, :] = jnp.zeros((EXTRA, half), held.dtype)
        rows = jnp.zeros((EXTRA, span), jnp.float32)
        for t, (base, _, sp) in enumerate(wins):
            piece = energy[k:k + 1, base:base + sp]
            if sp < span:
                piece = jnp.concatenate([piece, jnp.zeros((1, span - sp), jnp.float32)], axis=1)
            rows = jnp.where(row == t, jnp.broadcast_to(piece, (EXTRA, span)), rows)
        held[k, full:, 0:span] = rows.astype(held.dtype)
    for k in range(count):
        pltpu.make_async_copy(blocks_ref.at[k], held.at[k, 0:full], in_sems.at[k]).wait()
        pltpu.make_async_copy(held.at[k], out_ref.at[k], out_sems.at[k]).start()
    for k in range(count):
        pltpu.make_async_copy(held.at[k], out_ref.at[k], out_sems.at[k]).wait()


def extend(blocks, energy, wins):
    count, full, half = blocks.shape
    shape = (count, full + EXTRA, half)
    return pl.pallas_call(
        functools.partial(extend_kernel, wins),
        out_shape=jax.ShapeDtypeStruct(shape, blocks.dtype),
        in_specs=[ANY_SPEC, pl.BlockSpec(memory_space=pltpu.VMEM)],
        out_specs=ANY_SPEC,
        scratch_shapes=[
            pltpu.VMEM(shape, blocks.dtype), pltpu.SemaphoreType.DMA((count,)), pltpu.SemaphoreType.DMA((count,))],
        compiler_params=pltpu.CompilerParams(vmem_limit_bytes=VMEM_LIMIT),
        name="extend",
    )(blocks, energy)


def tie(x, deps):
    return pl.pallas_call(
        lambda *refs: None,
        out_shape=jax.ShapeDtypeStruct(x.shape, x.dtype),
        in_specs=[ANY_SPEC] * (1 + len(deps)),
        out_specs=ANY_SPEC,
        input_output_aliases={0: 0},
        compiler_params=pltpu.CompilerParams(vmem_limit_bytes=VMEM_LIMIT),
        cost_estimate=pl.CostEstimate(flops=0, bytes_accessed=0, transcendentals=0),
        name="tie",
    )(x, *deps)


def per_device(blocks, virt_energy, occ_energy, owner_slot, pairs, domains):
    orb_count = lax.axis_size("orb")
    aux_count = lax.axis_size("aux")
    occ_dev, full, half = blocks.shape
    pair_dev = pairs.shape[0]
    kept = domains.shape[2]
    own_rows = pair_dev // aux_count
    n_first = occ_dev // aux_count
    core = lax.axis_index("aux")
    o = lax.axis_index("orb")
    z, y = o // 2, o % 2
    chain = orb_count // 2
    last = chain - 1
    n_slots = orb_count * occ_dev
    i32 = jnp.int32
    wins = windows(full, kept)

    swap_aux = [(0, 1), (1, 0)]
    swap_y = [(k, k ^ 1) for k in range(orb_count)]

    def across_y(a):
        return lax.ppermute(a, "orb", swap_y)

    def across_aux(a):
        return lax.ppermute(a, "aux", swap_aux)

    def hop_down(a, d):
        return lax.ppermute(a, "orb", [(k, k - 2) for k in range(2, orb_count) if k // 2 <= chain - d])

    def hop_up(a, d):
        return lax.ppermute(a, "orb", [(k, k + 2) for k in range(orb_count - 2) if k // 2 >= d - 1])

    stored = extend(blocks, virt_energy, wins)

    downs, ups = [stored, hop_down(stored, 1)], [stored, hop_up(stored, 1)]
    local_other = across_aux(stored)

    orbitals = jnp.arange(owner_slot.shape[0], dtype=i32)
    hit_second = pairs[:, 1][:, None] == orbitals[None, :]
    slot_second = jnp.sum(jnp.where(hit_second, owner_slot[None, :], 0), axis=1)
    slots = jnp.arange(n_slots, dtype=i32)
    wanted_flat = jnp.any(slot_second[:, None] == slots[None, :], axis=0).astype(i32)
    wanted_flat = tie(wanted_flat, [stored])
    wanted = wanted_flat.reshape(orb_count, occ_dev) > 0
    wanted_both = jnp.stack([wanted_flat, across_y(wanted_flat)])
    wanted_opp = wanted_both[1].reshape(orb_count, occ_dev) > 0
    local = jnp.arange(occ_dev, dtype=i32)[None, :]

    def two_of(table):
        return jnp.min(jnp.where(table, local, occ_dev - 1), axis=1), jnp.max(jnp.where(table, local, 0), axis=1)

    want, want_opp = two_of(wanted), two_of(wanted_opp)

    first_row = core * own_rows
    own_second = lax.dynamic_slice_in_dim(slot_second, first_row, own_rows, 0)
    own_pairs = lax.dynamic_slice_in_dim(pairs, first_row, own_rows, 0)
    src = own_second // occ_dev
    part = own_second % occ_dev
    rank = jnp.any(
        (slot_second[None, :] // occ_dev == src[:, None]) & (slot_second[None, :] < own_second[:, None]),
        axis=1).astype(i32)
    src_z, src_y = src // 2, src % 2
    dist = jnp.abs(src_z - z)
    is_opp = (src_y != y).astype(i32)
    from_up = src_z < z
    both = 2 * dist <= chain - 1
    is_far = dist == last
    at_hand = (dist <= 1) & (is_opp == 0)
    idx = jnp.where(at_hand, part, rank + jnp.where(both & from_up, 2, 0))
    which_col = jnp.where(dist == 0, 3, jnp.where((dist == 1) & from_up, 2, jnp.where(is_far, 2, 1)))
    which = jnp.where(is_opp == 1, is_far.astype(i32), which_col)
    stage_col = jnp.where(is_far, last - 2, jnp.maximum(dist - 1, 0))
    stage = jnp.where(is_opp == 1, jnp.minimum(dist, last - 1), stage_col)
    rows = jnp.arange(own_rows, dtype=i32)
    before = (stage[None, :] < stage[:, None]) | ((stage[None, :] == stage[:, None]) & (rows[None, :] < rows[:, None]))
    place = jnp.sum(before.astype(i32), axis=1)
    order = jnp.sum(jnp.where(place[None, :] == rows[:, None], rows[None, :], 0), axis=1)
    bounds = jnp.sum((stage[None, :] < jnp.arange(chain + 1, dtype=i32)[:, None]).astype(i32), axis=1)
    width = max(own_rows, chain + 1)

    def padded(v):
        v = v.reshape(-1)
        return jnp.pad(v, (0, width - v.shape[0]))

    meta = jnp.stack([padded(bounds), padded(core * n_first), padded(order), padded(which), padded(idx)])

    def occ(col):
        hit = own_pairs[:, col][:, None] == orbitals[None, :]
        return jnp.sum(jnp.where(hit, occ_energy[None, :], 0.0), axis=1)

    shift = occ(0) + occ(1)
    ve1 = lax.dynamic_slice_in_dim(virt_energy, core * n_first, n_first, 0)
    ve1 = jnp.broadcast_to(ve1[:, :, None], (n_first, full, 128))

    dom = lax.dynamic_slice_in_dim(domains, first_row, own_rows, 0)
    base = jnp.concatenate([jnp.full((r,), b, i32) for b, r, _ in wins])
    span = max(sp for _, _, sp in wins)
    pick = ((dom - base)[..., None] == jnp.arange(span, dtype=i32)).astype(jnp.bfloat16)

    def idx_of(table, source):
        return lax.dynamic_index_in_dim(table, jnp.clip(source, 0, orb_count - 1), 0, keepdims=False)

    def two_for(table, source):
        return [idx_of(table[0], source), idx_of(table[1], source)]

    sets = {}

    def pairs_at(d, after, prev):
        return run_pairs(d, wins, meta, shift, ve1, pick, stored, local_other, sets[d], after, prev)

    def with_other(a):
        return a, across_aux(a)

    y_load = copy_sets([0, 0], two_for(want_opp, o), [stored])
    opp = with_other(across_y(y_load))
    top = orb_count - 1
    tell = [(0, 2), (1, 3), (top, top - 2), (top - 1, top - 3)]
    wanted_far = lax.ppermute(tie(wanted_both, [y_load]), "orb", tell).reshape(2, orb_count, occ_dev) > 0
    far_own, far_opp = two_of(wanted_far[0]), two_of(wanted_far[1])
    early = [opp[1], local_other, pick, meta]
    downs[1], ups[1] = tie(downs[1], early), tie(ups[1], early)
    out = None
    for d in range(1, last):
        s_down, s_up = o + 2 * d, o - 2 * d
        first = []
        if d + 1 < last:
            downs.append(hop_down(downs[d], d + 1))
            ups.append(hop_up(ups[d], d + 1))
        else:
            sends_down = z == 1
            source = jnp.where(sends_down, 2 * last + y, y)
            from_set = [1 - sends_down.astype(i32)] * 4
            perm = [(2, 0), (3, 1), (2 * (last - 1), 2 * last), (2 * (last - 1) + 1, 2 * last + 1)]
            load_over, load_own = copy_sets(
                from_set, two_for(far_opp, source) + two_for(far_own, source), [downs[d], ups[d]], [out], [2, 2])
            far_b = lax.ppermute(across_y(load_over), "orb", perm)
            far_a = lax.ppermute(load_own, "orb", perm)
            first = [load_own]
        if 2 * d <= last:
            place_of = [0, 0, 1, 1]

            def both_ways(table):
                return two_for(table, s_down) + two_for(table, s_up)
        else:
            is_up = (z + d > last).astype(i32)
            place_of = [is_up, is_up]

            def both_ways(table):
                return two_for(table, jnp.where(is_up == 1, s_up, s_down))
        if d == 1:
            theirs = copy_sets(place_of, both_ways(want_opp), [downs[d], ups[d]])
            sets[0] = [opp, with_other(downs[1]), with_other(ups[1]), (stored, local_other)]
            out = pairs_at(0, [theirs], out)
        else:
            theirs, mine = copy_sets(
                place_of * 2, both_ways(want_opp) + both_ways(want), [downs[d], ups[d]], first, [len(place_of)] * 2)
            sets[d - 1] = [with_other(tie(opp, first) if first else opp), with_other(mine)]
            if d + 1 == last:
                sets[d - 1].append(with_other(far_a))
            out = pairs_at(d - 1, [mine], out)
        opp = across_y(theirs)
    sets[last - 1] = [with_other(tie(opp, [out])), with_other(tie(far_b, [out]))]
    return pairs_at(last - 1, [], out)


def solution(mesh):
    in_specs = (
        P(("groups", "orb"), None, "aux"),
        P(("groups", "orb"), None),
        P("groups"),
        P("groups"),
        P(("groups", "orb"), None),
        P(("groups", "orb"), None, None),
    )
    out_specs = P(("groups", "orb", "aux"), None, None)
    return jax.shard_map(
        per_device, mesh=mesh, in_specs=in_specs, out_specs=out_specs, check_vma=False
    )
```

```python
import functools

import jax
import jax.numpy as jnp
from jax import lax
from jax.experimental import pallas as pl
from jax.experimental.pallas import tpu as pltpu
from jax.sharding import PartitionSpec as P

NT = (((1,), (1,)), ((), ()))
VMEM_LIMIT = 56 * 1024 * 1024
EXTRA = 16


def windows(full, kept):
    slack = full - kept
    tile = 256 - slack if 0 <= slack <= 128 else kept
    found = []
    base = 0
    while base < kept:
        rows = min(tile, kept - base)
        found.append((base, rows, rows + slack))
        base += rows
    return found


def pair_kernel(call, wins, n_sets, n_skip, meta_ref, shift_ref, ve1_ref, pick_ref, own_ref, other_ref, *rest):
    sets = [(rest[2 * k], rest[2 * k + 1]) for k in range(n_sets)]
    rest = rest[2 * n_sets + n_skip:]
    (out_ref, first, second, pick, side_a, side_b, e1_buf, out_buf,
     first_sem, second_sem, pick_sem, out_sem) = rest
    pairs_here = out_ref.shape[0]
    kept = out_ref.shape[1]
    half = own_ref.shape[2]
    n_first = first.shape[0]
    lo = meta_ref[0, call]
    hi = meta_ref[0, call + 1]
    base_first = meta_ref[1, 0]

    def first_copies():
        out = []
        for k in range(n_first):
            out.append(pltpu.make_async_copy(
                own_ref.at[base_first + k], first.at[k, :, pl.ds(0, half)], first_sem.at[2 * k]))
            out.append(pltpu.make_async_copy(
                other_ref.at[base_first + k], first.at[k, :, pl.ds(half, half)], first_sem.at[2 * k + 1]))
        return out

    def fetch(i, slot):
        p = meta_ref[2, i]
        which = meta_ref[3, p]
        idx = meta_ref[4, p]
        pltpu.make_async_copy(pick_ref.at[p], pick.at[slot], pick_sem.at[slot]).start()
        for k, (x_own, x_other) in enumerate(sets):
            @pl.when(which == k)
            def _():
                pltpu.make_async_copy(
                    x_own.at[idx], second.at[slot, :, pl.ds(0, half)], second_sem.at[slot, 0]).start()
                pltpu.make_async_copy(
                    x_other.at[idx], second.at[slot, :, pl.ds(half, half)], second_sem.at[slot, 1]).start()

    def await_fetch(slot):
        pltpu.make_async_copy(pick_ref.at[0], pick.at[slot], pick_sem.at[slot]).wait()
        for k in range(2):
            pltpu.make_async_copy(
                sets[0][0].at[0], second.at[slot, :, pl.ds(k * half, half)], second_sem.at[slot, k]).wait()

    def out_copy(p, slot):
        return pltpu.make_async_copy(out_buf.at[slot], out_ref.at[p], out_sem.at[slot])

    @pl.when(hi > lo)
    def _():
        for c in first_copies():
            c.start()
        fetch(lo, lax.rem(lo, 2))
        for c in first_copies():
            c.wait()

    def step(i, carry):
        slot = lax.rem(i, 2)
        p = meta_ref[2, i]
        f = p // (pairs_here // n_first)

        @pl.when(i + 1 < hi)
        def _():
            fetch(i + 1, 1 - slot)

        await_fetch(slot)

        @pl.when(i >= lo + 2)
        def _():
            out_copy(p, slot).wait()

        e2_parts = []
        full = ve1_ref.shape[1]
        for t, (base, rows, span) in enumerate(wins):
            one = pick[slot, 0, base:base + rows, 0:span]
            got = jnp.dot(one, first[f, base:base + span, :], preferred_element_type=jnp.float32)
            side_a[base:base + rows, :] = got.astype(jnp.bfloat16)
            e1_buf[base:base + rows, :] = jnp.dot(
                one, ve1_ref[f, base:base + span, :], preferred_element_type=jnp.float32)
            two = pick[slot, 1, base:base + rows, 0:span]
            got = jnp.dot(two, second[slot, base:base + span, :], preferred_element_type=jnp.float32)
            side_b[base:base + rows, :] = got.astype(jnp.bfloat16)
            ve = second[slot, full:full + EXTRA, 0:span]
            e2_parts.append(
                lax.dot_general(ve, two, NT, preferred_element_type=jnp.float32)[t:t + 1])
        e2 = jnp.concatenate(e2_parts, axis=1)
        shift = shift_ref[p]
        chunk = min(kept, 256)
        for start in range(0, kept, chunk):
            c = lax.dot_general(
                side_a[...], side_b[start:start + chunk, :], NT, preferred_element_type=jnp.float32)
            for col in range(0, chunk, 128):
                den = e1_buf[...] + e2[:, start + col:start + col + 128] - shift
                inv = pl.reciprocal(den, approx=True)
                neg = inv * (den * inv - 2.0)
                out_buf[slot, :, start + col:start + col + 128] = (
                    c[:, col:col + 128] * neg).astype(jnp.bfloat16)
        out_copy(p, slot).start()
        return carry

    lax.fori_loop(lo, hi, step, 0)

    @pl.when(hi - lo >= 2)
    def _():
        out_copy(0, lax.rem(hi, 2)).wait()

    @pl.when(hi > lo)
    def _():
        out_copy(0, lax.rem(hi + 1, 2)).wait()


def run_pairs(call, wins, meta, shift, ve1, pick, own, other, sets, after, prev):
    pairs_here, _, kept, span = pick.shape
    n_first = ve1.shape[0]
    full, half = own.shape[1], own.shape[2]
    any_spec = ANY_SPEC
    smem = pl.BlockSpec(memory_space=pltpu.SMEM)
    vmem = pl.BlockSpec(memory_space=pltpu.VMEM)
    operands = [meta, shift, ve1, pick, own, other]
    for pair in sets:
        operands += list(pair)
    operands += after
    in_specs = [smem, smem, vmem] + [any_spec] * (len(operands) - 3)
    aliases = {}
    if prev is not None:
        aliases = {len(operands): 0}
        operands.append(prev)
        in_specs.append(any_spec)
    bf = jnp.bfloat16
    return pl.pallas_call(
        functools.partial(pair_kernel, call, wins, len(sets), len(after) + (prev is not None)),
        out_shape=jax.ShapeDtypeStruct((pairs_here, kept, kept), bf),
        in_specs=in_specs,
        out_specs=any_spec,
        scratch_shapes=[
            pltpu.VMEM((n_first, full, 2 * half), bf),
            pltpu.VMEM((2, full, 2 * half), bf),
            pltpu.VMEM((2, 2, kept, span), bf),
            pltpu.VMEM((kept, 2 * half), bf),
            pltpu.VMEM((kept, 2 * half), bf),
            pltpu.VMEM((kept, 128), jnp.float32),
            pltpu.VMEM((2, kept, kept), bf),
            pltpu.SemaphoreType.DMA((2 * n_first,)),
            pltpu.SemaphoreType.DMA((2, 2)),
            pltpu.SemaphoreType.DMA((2,)),
            pltpu.SemaphoreType.DMA((2,)),
        ],
        input_output_aliases=aliases,
        compiler_params=pltpu.CompilerParams(vmem_limit_bytes=VMEM_LIMIT),
        cost_estimate=pl.CostEstimate(flops=0, bytes_accessed=0, transcendentals=0),
        name=f"pairs_{call}",
    )(*operands)


def set_kernel(n_arrays, n_skip, sizes, table_ref, *rest):
    arrays = rest[:n_arrays]
    outs = rest[n_arrays + n_skip:-3]
    held, in_sems, out_sems = rest[-3:]
    places = [(o, k) for o, size in zip(outs, sizes) for k in range(size)]
    for j in range(len(places)):
        for k, a in enumerate(arrays):
            @pl.when(table_ref[0, j] == k)
            def _():
                pltpu.make_async_copy(a.at[table_ref[1, j]], held.at[j], in_sems.at[j]).start()
    for j, (o, k) in enumerate(places):
        pltpu.make_async_copy(arrays[0].at[0], held.at[j], in_sems.at[j]).wait()
        pltpu.make_async_copy(held.at[j], o.at[k], out_sems.at[j]).start()
    for j, (o, k) in enumerate(places):
        pltpu.make_async_copy(held.at[j], o.at[k], out_sems.at[j]).wait()


ANY_SPEC = pl.BlockSpec(memory_space=pl.ANY)


def copy_sets(which, index, arrays, after=(), sizes=None):
    n = len(index)
    sizes = sizes or [n]
    table = jnp.stack([jnp.stack([jnp.asarray(w, jnp.int32) for w in which]), jnp.stack(index)])
    block = arrays[0].shape[1:]
    outs = pl.pallas_call(
        functools.partial(set_kernel, len(arrays), len(after), sizes),
        out_shape=[jax.ShapeDtypeStruct((size,) + block, arrays[0].dtype) for size in sizes],
        in_specs=[pl.BlockSpec(memory_space=pltpu.SMEM)] + [ANY_SPEC] * (len(arrays) + len(after)),
        out_specs=[ANY_SPEC] * len(sizes),
        scratch_shapes=[
            pltpu.VMEM((n,) + block, arrays[0].dtype),
            pltpu.SemaphoreType.DMA((n,)),
            pltpu.SemaphoreType.DMA((n,))],
        cost_estimate=pl.CostEstimate(flops=0, bytes_accessed=0, transcendentals=0),
        compiler_params=pltpu.CompilerParams(vmem_limit_bytes=VMEM_LIMIT),
        name="copy_sets",
    )(table, *arrays, *after)
    return outs if len(sizes) > 1 else outs[0]


def extend_kernel(wins, blocks_ref, energy_ref, out_ref, held, in_sems, out_sems):
    count, full, half = blocks_ref.shape
    for k in range(count):
        pltpu.make_async_copy(blocks_ref.at[k], held.at[k, 0:full], in_sems.at[k]).start()
    energy = energy_ref[...].astype(jnp.float32)
    span = max(sp for _, _, sp in wins)
    row = lax.broadcasted_iota(jnp.int32, (EXTRA, span), 0)
    for k in range(count):
        held[k, full:, :] = jnp.zeros((EXTRA, half), held.dtype)
        rows = jnp.zeros((EXTRA, span), jnp.float32)
        for t, (base, _, sp) in enumerate(wins):
            piece = energy[k:k + 1, base:base + sp]
            if sp < span:
                piece = jnp.concatenate([piece, jnp.zeros((1, span - sp), jnp.float32)], axis=1)
            rows = jnp.where(row == t, jnp.broadcast_to(piece, (EXTRA, span)), rows)
        held[k, full:, 0:span] = rows.astype(held.dtype)
    for k in range(count):
        pltpu.make_async_copy(blocks_ref.at[k], held.at[k, 0:full], in_sems.at[k]).wait()
        pltpu.make_async_copy(held.at[k], out_ref.at[k], out_sems.at[k]).start()
    for k in range(count):
        pltpu.make_async_copy(held.at[k], out_ref.at[k], out_sems.at[k]).wait()


def extend(blocks, energy, wins):
    count, full, half = blocks.shape
    shape = (count, full + EXTRA, half)
    return pl.pallas_call(
        functools.partial(extend_kernel, wins),
        out_shape=jax.ShapeDtypeStruct(shape, blocks.dtype),
        in_specs=[ANY_SPEC, pl.BlockSpec(memory_space=pltpu.VMEM)],
        out_specs=ANY_SPEC,
        scratch_shapes=[
            pltpu.VMEM(shape, blocks.dtype), pltpu.SemaphoreType.DMA((count,)), pltpu.SemaphoreType.DMA((count,))],
        compiler_params=pltpu.CompilerParams(vmem_limit_bytes=VMEM_LIMIT),
        name="extend",
    )(blocks, energy)


def tie(x, deps):
    return pl.pallas_call(
        lambda *refs: None,
        out_shape=jax.ShapeDtypeStruct(x.shape, x.dtype),
        in_specs=[ANY_SPEC] * (1 + len(deps)),
        out_specs=ANY_SPEC,
        input_output_aliases={0: 0},
        compiler_params=pltpu.CompilerParams(vmem_limit_bytes=VMEM_LIMIT),
        cost_estimate=pl.CostEstimate(flops=0, bytes_accessed=0, transcendentals=0),
        name="tie",
    )(x, *deps)


def per_device(blocks, virt_energy, occ_energy, owner_slot, pairs, domains):
    orb_count = lax.axis_size("orb")
    aux_count = lax.axis_size("aux")
    occ_dev, full, half = blocks.shape
    pair_dev = pairs.shape[0]
    kept = domains.shape[2]
    own_rows = pair_dev // aux_count
    n_first = occ_dev // aux_count
    core = lax.axis_index("aux")
    o = lax.axis_index("orb")
    z, y = o // 2, o % 2
    chain = orb_count // 2
    last = chain - 1
    n_slots = orb_count * occ_dev
    i32 = jnp.int32
    wins = windows(full, kept)

    swap_aux = [(0, 1), (1, 0)]
    swap_y = [(k, k ^ 1) for k in range(orb_count)]

    def across_y(a):
        return lax.ppermute(a, "orb", swap_y)

    def across_aux(a):
        return lax.ppermute(a, "aux", swap_aux)

    def hop_down(a, d):
        return lax.ppermute(a, "orb", [(k, k - 2) for k in range(2, orb_count) if k // 2 <= chain - d])

    def hop_up(a, d):
        return lax.ppermute(a, "orb", [(k, k + 2) for k in range(orb_count - 2) if k // 2 >= d - 1])

    stored = extend(blocks, virt_energy, wins)

    downs, ups = [stored, hop_down(stored, 1)], [stored, hop_up(stored, 1)]
    local_other = across_aux(stored)

    orbitals = jnp.arange(owner_slot.shape[0], dtype=i32)
    hit_second = pairs[:, 1][:, None] == orbitals[None, :]
    slot_second = jnp.sum(jnp.where(hit_second, owner_slot[None, :], 0), axis=1)
    slots = jnp.arange(n_slots, dtype=i32)
    wanted_flat = jnp.any(slot_second[:, None] == slots[None, :], axis=0).astype(i32)
    wanted_flat = tie(wanted_flat, [stored])
    wanted = wanted_flat.reshape(orb_count, occ_dev) > 0
    wanted_both = jnp.stack([wanted_flat, across_y(wanted_flat)])
    wanted_opp = wanted_both[1].reshape(orb_count, occ_dev) > 0
    local = jnp.arange(occ_dev, dtype=i32)[None, :]

    def two_of(table):
        return jnp.min(jnp.where(table, local, occ_dev - 1), axis=1), jnp.max(jnp.where(table, local, 0), axis=1)

    want, want_opp = two_of(wanted), two_of(wanted_opp)

    first_row = core * own_rows
    own_second = lax.dynamic_slice_in_dim(slot_second, first_row, own_rows, 0)
    own_pairs = lax.dynamic_slice_in_dim(pairs, first_row, own_rows, 0)
    src = own_second // occ_dev
    part = own_second % occ_dev
    rank = jnp.any(
        (slot_second[None, :] // occ_dev == src[:, None]) & (slot_second[None, :] < own_second[:, None]),
        axis=1).astype(i32)
    src_z, src_y = src // 2, src % 2
    dist = jnp.abs(src_z - z)
    is_opp = (src_y != y).astype(i32)
    from_up = src_z < z
    both = 2 * dist <= chain - 1
    is_far = dist == last
    at_hand = (dist <= 1) & (is_opp == 0)
    idx = jnp.where(at_hand, part, rank + jnp.where(both & from_up, 2, 0))
    which_col = jnp.where(dist == 0, 3, jnp.where((dist == 1) & from_up, 2, jnp.where(is_far, 2, 1)))
    which = jnp.where(is_opp == 1, is_far.astype(i32), which_col)
    stage_col = jnp.where(is_far, last - 2, jnp.maximum(dist - 1, 0))
    stage = jnp.where(is_opp == 1, jnp.minimum(dist, last - 1), stage_col)
    rows = jnp.arange(own_rows, dtype=i32)
    before = (stage[None, :] < stage[:, None]) | ((stage[None, :] == stage[:, None]) & (rows[None, :] < rows[:, None]))
    place = jnp.sum(before.astype(i32), axis=1)
    order = jnp.sum(jnp.where(place[None, :] == rows[:, None], rows[None, :], 0), axis=1)
    bounds = jnp.sum((stage[None, :] < jnp.arange(chain + 1, dtype=i32)[:, None]).astype(i32), axis=1)
    width = max(own_rows, chain + 1)

    def padded(v):
        v = v.reshape(-1)
        return jnp.pad(v, (0, width - v.shape[0]))

    meta = jnp.stack([padded(bounds), padded(core * n_first), padded(order), padded(which), padded(idx)])

    def occ(col):
        hit = own_pairs[:, col][:, None] == orbitals[None, :]
        return jnp.sum(jnp.where(hit, occ_energy[None, :], 0.0), axis=1)

    shift = occ(0) + occ(1)
    ve1 = lax.dynamic_slice_in_dim(virt_energy, core * n_first, n_first, 0)
    ve1 = jnp.broadcast_to(ve1[:, :, None], (n_first, full, 128))

    dom = lax.dynamic_slice_in_dim(domains, first_row, own_rows, 0)
    base = jnp.concatenate([jnp.full((r,), b, i32) for b, r, _ in wins])
    span = max(sp for _, _, sp in wins)
    pick = ((dom - base)[..., None] == jnp.arange(span, dtype=i32)).astype(jnp.bfloat16)

    def idx_of(table, source):
        return lax.dynamic_index_in_dim(table, jnp.clip(source, 0, orb_count - 1), 0, keepdims=False)

    def two_for(table, source):
        return [idx_of(table[0], source), idx_of(table[1], source)]

    sets = {}

    def pairs_at(d, after, prev):
        return run_pairs(d, wins, meta, shift, ve1, pick, stored, local_other, sets[d], after, prev)

    def with_other(a):
        return a, across_aux(a)

    y_load = copy_sets([0, 0], two_for(want_opp, o), [stored])
    opp = with_other(across_y(y_load))
    told = tie(wanted_both, [y_load])

    def tell(at_first_end, at_last_end):
        perm = [(c, 2 * at_first_end + c) for c in range(2)]
        perm += [(2 * last + c, 2 * at_last_end + c) for c in range(2)]
        return lax.ppermute(told, "orb", perm).reshape(2, orb_count, occ_dev) > 0

    far_opp = two_of(tell(last - 1, 1)[1])
    far_own = two_of(tell(1, last - 1)[0])
    over = None
    early = [opp[1], local_other, pick, meta, far_own[0], far_opp[0]]
    downs[1], ups[1] = tie(downs[1], early), tie(ups[1], early)
    out = None

    def far_perm(left):
        down = [(2 * (left + 1) + c, 2 * left + c) for c in range(2)]
        return down + [(2 * (last - left - 1) + c, 2 * (last - left) + c) for c in range(2)]

    for d in range(1, last):
        s_down, s_up = o + 2 * d, o - 2 * d
        first = []
        if d + 1 < last:
            downs.append(hop_down(downs[d], d + 1))
            ups.append(hop_up(ups[d], d + 1))
        else:
            sends_down = z == 1
            source = jnp.where(sends_down, 2 * last + y, y)
            from_set = [1 - sends_down.astype(i32)] * 2
            load_own = copy_sets(from_set, two_for(far_own, source), [downs[d], ups[d]])
            far_a = lax.ppermute(load_own, "orb", far_perm(0))
            first = [load_own, out]
        if 2 * d <= last:
            place_of = [0, 0, 1, 1]

            def both_ways(table):
                return two_for(table, s_down) + two_for(table, s_up)
        else:
            is_up = (z + d > last).astype(i32)
            place_of = [is_up, is_up]

            def both_ways(table):
                return two_for(table, jnp.where(is_up == 1, s_up, s_down))
        if d > 1:
            over = lax.ppermute(tie(over, [downs[d], ups[d]]), "orb", far_perm(last - d))
        if d == 1:
            is_up = (z == 1).astype(i32)
            load_over = copy_sets(
                [is_up] * 2, two_for(far_opp, jnp.where(is_up == 1, y, 2 * last + y)), [downs[d], ups[d]])
            over = across_y(load_over)
            sets[0] = [opp, with_other(downs[1]), with_other(ups[1]), (stored, local_other)]
            theirs = copy_sets(place_of, both_ways(want_opp), [downs[d], ups[d]], [over])
            out = pairs_at(0, [theirs] + downs[2:] + ups[2:], out)
        else:
            theirs, mine = copy_sets(
                place_of * 2, both_ways(want_opp) + both_ways(want), [downs[d], ups[d]], first, [len(place_of)] * 2)
            sets[d - 1] = [with_other(tie(opp, [mine] + ([over] if d + 1 == last else []))), with_other(mine)]
            if d + 1 == last:
                sets[d - 1].append(with_other(far_a))
            out = pairs_at(d - 1, [mine], out)
        opp = across_y(theirs)
        if d + 1 == last:
            far_b = lax.ppermute(over, "orb", far_perm(0))
    sets[last - 1] = [with_other(tie(opp, [out])), with_other(tie(far_b, [out]))]
    return pairs_at(last - 1, [], out)


def solution(mesh):
    in_specs = (
        P(("groups", "orb"), None, "aux"),
        P(("groups", "orb"), None),
        P("groups"),
        P("groups"),
        P(("groups", "orb"), None),
        P(("groups", "orb"), None, None),
    )
    out_specs = P(("groups", "orb", "aux"), None, None)
    return jax.shard_map(
        per_device, mesh=mesh, in_specs=in_specs, out_specs=out_specs, check_vma=False
    )
```

```python
import functools

import jax
import jax.numpy as jnp
from jax import lax
from jax.experimental import pallas as pl
from jax.experimental.pallas import tpu as pltpu
from jax.sharding import PartitionSpec as P

NT = (((1,), (1,)), ((), ()))
VMEM_LIMIT = 63 * 1024 * 1024
EXTRA = 16


def windows(full, kept):
    slack = full - kept
    tile = 256 - slack if 0 <= slack <= 128 else kept
    found = []
    base = 0
    while base < kept:
        rows = min(tile, kept - base)
        found.append((base, rows, rows + slack))
        base += rows
    return found


def pair_kernel(call, wins, n_sets, n_skip, meta_ref, shift_ref, ve1_ref, pick_ref, own_ref, other_ref, *rest):
    sets = [(rest[2 * k], rest[2 * k + 1]) for k in range(n_sets)]
    rest = rest[2 * n_sets + n_skip:]
    (out_ref, first, second, pick, side_a, side_b, e1_buf, out_buf,
     first_sem, second_sem, pick_sem, out_sem) = rest
    pairs_here = out_ref.shape[0]
    kept = out_ref.shape[1]
    half = own_ref.shape[2]
    n_first = first.shape[0]
    lo = meta_ref[0, call]
    hi = meta_ref[0, call + 1]
    base_first = meta_ref[1, 0]

    def first_copies():
        out = []
        for k in range(n_first):
            out.append(pltpu.make_async_copy(
                own_ref.at[base_first + k], first.at[k, :, pl.ds(0, half)], first_sem.at[2 * k]))
            out.append(pltpu.make_async_copy(
                other_ref.at[base_first + k], first.at[k, :, pl.ds(half, half)], first_sem.at[2 * k + 1]))
        return out

    def fetch(i, slot):
        p = meta_ref[2, i]
        which = meta_ref[3, p]
        idx = meta_ref[4, p]
        pltpu.make_async_copy(pick_ref.at[p], pick.at[slot], pick_sem.at[slot]).start()
        for k, (x_own, x_other) in enumerate(sets):
            @pl.when(which == k)
            def _():
                pltpu.make_async_copy(
                    x_own.at[idx], second.at[slot, :, pl.ds(0, half)], second_sem.at[slot, 0]).start()
                pltpu.make_async_copy(
                    x_other.at[idx], second.at[slot, :, pl.ds(half, half)], second_sem.at[slot, 1]).start()

    def await_fetch(slot):
        pltpu.make_async_copy(pick_ref.at[0], pick.at[slot], pick_sem.at[slot]).wait()
        for k in range(2):
            pltpu.make_async_copy(
                sets[0][0].at[0], second.at[slot, :, pl.ds(k * half, half)], second_sem.at[slot, k]).wait()

    def out_copy(p, slot):
        return pltpu.make_async_copy(out_buf.at[slot], out_ref.at[p], out_sem.at[slot])

    @pl.when(hi > lo)
    def _():
        for c in first_copies():
            c.start()
        fetch(lo, lax.rem(lo, 2))
        for c in first_copies():
            c.wait()

    def step(i, carry):
        slot = lax.rem(i, 2)
        p = meta_ref[2, i]
        f = p // (pairs_here // n_first)

        @pl.when(i + 1 < hi)
        def _():
            fetch(i + 1, 1 - slot)

        await_fetch(slot)

        @pl.when(i >= lo + 2)
        def _():
            out_copy(p, slot).wait()

        e2_parts = []
        full = ve1_ref.shape[1]
        for t, (base, rows, span) in enumerate(wins):
            one = pick[slot, 0, base:base + rows, 0:span]
            got = jnp.dot(one, first[f, base:base + span, :], preferred_element_type=jnp.float32)
            side_a[base:base + rows, :] = got.astype(jnp.bfloat16)
            e1_buf[base:base + rows, :] = jnp.dot(
                one, ve1_ref[f, base:base + span, :], preferred_element_type=jnp.float32)
            two = pick[slot, 1, base:base + rows, 0:span]
            got = jnp.dot(two, second[slot, base:base + span, :], preferred_element_type=jnp.float32)
            side_b[base:base + rows, :] = got.astype(jnp.bfloat16)
            ve = second[slot, full:full + EXTRA, 0:span]
            e2_parts.append(
                lax.dot_general(ve, two, NT, preferred_element_type=jnp.float32)[t:t + 1])
        e2 = jnp.concatenate(e2_parts, axis=1)
        shift = shift_ref[p]
        chunk = min(kept, 256)
        for start in range(0, kept, chunk):
            c = lax.dot_general(
                side_a[...], side_b[start:start + chunk, :], NT, preferred_element_type=jnp.float32)
            for col in range(0, chunk, 128):
                den = e1_buf[...] + e2[:, start + col:start + col + 128] - shift
                inv = pl.reciprocal(den, approx=True)
                neg = inv * (den * inv - 2.0)
                out_buf[slot, :, start + col:start + col + 128] = (
                    c[:, col:col + 128] * neg).astype(jnp.bfloat16)
        out_copy(p, slot).start()
        return carry

    lax.fori_loop(lo, hi, step, 0)

    @pl.when(hi - lo >= 2)
    def _():
        out_copy(0, lax.rem(hi, 2)).wait()

    @pl.when(hi > lo)
    def _():
        out_copy(0, lax.rem(hi + 1, 2)).wait()


def run_pairs(call, wins, meta, shift, ve1, pick, own, other, sets, after, prev):
    pairs_here, _, kept, span = pick.shape
    n_first = ve1.shape[0]
    full, half = own.shape[1], own.shape[2]
    any_spec = ANY_SPEC
    smem = pl.BlockSpec(memory_space=pltpu.SMEM)
    vmem = pl.BlockSpec(memory_space=pltpu.VMEM)
    operands = [meta, shift, ve1, pick, own, other]
    for pair in sets:
        operands += list(pair)
    operands += after
    in_specs = [smem, smem, vmem] + [any_spec] * (len(operands) - 3)
    aliases = {}
    if prev is not None:
        aliases = {len(operands): 0}
        operands.append(prev)
        in_specs.append(any_spec)
    bf = jnp.bfloat16
    return pl.pallas_call(
        functools.partial(pair_kernel, call, wins, len(sets), len(after) + (prev is not None)),
        out_shape=jax.ShapeDtypeStruct((pairs_here, kept, kept), bf),
        in_specs=in_specs,
        out_specs=any_spec,
        scratch_shapes=[
            pltpu.VMEM((n_first, full, 2 * half), bf),
            pltpu.VMEM((2, full, 2 * half), bf),
            pltpu.VMEM((2, 2, kept, span), bf),
            pltpu.VMEM((kept, 2 * half), bf),
            pltpu.VMEM((kept, 2 * half), bf),
            pltpu.VMEM((kept, 128), jnp.float32),
            pltpu.VMEM((2, kept, kept), bf),
            pltpu.SemaphoreType.DMA((2 * n_first,)),
            pltpu.SemaphoreType.DMA((2, 2)),
            pltpu.SemaphoreType.DMA((2,)),
            pltpu.SemaphoreType.DMA((2,)),
        ],
        input_output_aliases=aliases,
        compiler_params=pltpu.CompilerParams(vmem_limit_bytes=VMEM_LIMIT),
        cost_estimate=pl.CostEstimate(flops=0, bytes_accessed=0, transcendentals=0),
        name=f"pairs_{call}",
    )(*operands)


def set_kernel(n_arrays, n_skip, sizes, table_ref, *rest):
    arrays = rest[:n_arrays]
    outs = rest[n_arrays + n_skip:-3]
    held, in_sems, out_sems = rest[-3:]
    places = [(o, k) for o, size in zip(outs, sizes) for k in range(size)]
    for j in range(len(places)):
        for k, a in enumerate(arrays):
            @pl.when(table_ref[0, j] == k)
            def _():
                pltpu.make_async_copy(a.at[table_ref[1, j]], held.at[j], in_sems.at[j]).start()
    for j, (o, k) in enumerate(places):
        pltpu.make_async_copy(arrays[0].at[0], held.at[j], in_sems.at[j]).wait()
        pltpu.make_async_copy(held.at[j], o.at[k], out_sems.at[j]).start()
    for j, (o, k) in enumerate(places):
        pltpu.make_async_copy(held.at[j], o.at[k], out_sems.at[j]).wait()


ANY_SPEC = pl.BlockSpec(memory_space=pl.ANY)


def copy_sets(which, index, arrays, after=(), sizes=None):
    n = len(index)
    sizes = sizes or [n]
    table = jnp.stack([jnp.stack([jnp.asarray(w, jnp.int32) for w in which]), jnp.stack(index)])
    block = arrays[0].shape[1:]
    outs = pl.pallas_call(
        functools.partial(set_kernel, len(arrays), len(after), sizes),
        out_shape=[jax.ShapeDtypeStruct((size,) + block, arrays[0].dtype) for size in sizes],
        in_specs=[pl.BlockSpec(memory_space=pltpu.SMEM)] + [ANY_SPEC] * (len(arrays) + len(after)),
        out_specs=[ANY_SPEC] * len(sizes),
        scratch_shapes=[
            pltpu.VMEM((n,) + block, arrays[0].dtype),
            pltpu.SemaphoreType.DMA((n,)),
            pltpu.SemaphoreType.DMA((n,))],
        cost_estimate=pl.CostEstimate(flops=0, bytes_accessed=0, transcendentals=0),
        compiler_params=pltpu.CompilerParams(vmem_limit_bytes=VMEM_LIMIT),
        name="copy_sets",
    )(table, *arrays, *after)
    return outs if len(sizes) > 1 else outs[0]


def extend_kernel(wins, blocks_ref, energy_ref, out_ref, held, in_sems, out_sems):
    count, full, half = blocks_ref.shape
    for k in range(count):
        pltpu.make_async_copy(blocks_ref.at[k], held.at[k, 0:full], in_sems.at[k]).start()
    energy = energy_ref[...].astype(jnp.float32)
    span = max(sp for _, _, sp in wins)
    row = lax.broadcasted_iota(jnp.int32, (EXTRA, span), 0)
    for k in range(count):
        held[k, full:, :] = jnp.zeros((EXTRA, half), held.dtype)
        rows = jnp.zeros((EXTRA, span), jnp.float32)
        for t, (base, _, sp) in enumerate(wins):
            piece = energy[k:k + 1, base:base + sp]
            if sp < span:
                piece = jnp.concatenate([piece, jnp.zeros((1, span - sp), jnp.float32)], axis=1)
            rows = jnp.where(row == t, jnp.broadcast_to(piece, (EXTRA, span)), rows)
        held[k, full:, 0:span] = rows.astype(held.dtype)
    for k in range(count):
        pltpu.make_async_copy(blocks_ref.at[k], held.at[k, 0:full], in_sems.at[k]).wait()
        pltpu.make_async_copy(held.at[k], out_ref.at[k], out_sems.at[k]).start()
    for k in range(count):
        pltpu.make_async_copy(held.at[k], out_ref.at[k], out_sems.at[k]).wait()


def extend(blocks, energy, wins):
    count, full, half = blocks.shape
    shape = (count, full + EXTRA, half)
    return pl.pallas_call(
        functools.partial(extend_kernel, wins),
        out_shape=jax.ShapeDtypeStruct(shape, blocks.dtype),
        in_specs=[ANY_SPEC, pl.BlockSpec(memory_space=pltpu.VMEM)],
        out_specs=ANY_SPEC,
        scratch_shapes=[
            pltpu.VMEM(shape, blocks.dtype), pltpu.SemaphoreType.DMA((count,)), pltpu.SemaphoreType.DMA((count,))],
        compiler_params=pltpu.CompilerParams(vmem_limit_bytes=VMEM_LIMIT),
        name="extend",
    )(blocks, energy)


def tie(x, deps):
    return pl.pallas_call(
        lambda *refs: None,
        out_shape=jax.ShapeDtypeStruct(x.shape, x.dtype),
        in_specs=[ANY_SPEC] * (1 + len(deps)),
        out_specs=ANY_SPEC,
        input_output_aliases={0: 0},
        compiler_params=pltpu.CompilerParams(vmem_limit_bytes=VMEM_LIMIT),
        cost_estimate=pl.CostEstimate(flops=0, bytes_accessed=0, transcendentals=0),
        name="tie",
    )(x, *deps)


def per_device(blocks, virt_energy, occ_energy, owner_slot, pairs, domains):
    orb_count = lax.axis_size("orb")
    aux_count = lax.axis_size("aux")
    occ_dev, full, half = blocks.shape
    pair_dev = pairs.shape[0]
    kept = domains.shape[2]
    own_rows = pair_dev // aux_count
    n_first = occ_dev // aux_count
    core = lax.axis_index("aux")
    o = lax.axis_index("orb")
    z, y = o // 2, o % 2
    chain = orb_count // 2
    last = chain - 1
    n_slots = orb_count * occ_dev
    i32 = jnp.int32
    wins = windows(full, kept)

    swap_aux = [(0, 1), (1, 0)]
    swap_y = [(k, k ^ 1) for k in range(orb_count)]

    def across_y(a):
        return lax.ppermute(a, "orb", swap_y)

    def across_aux(a):
        return lax.ppermute(a, "aux", swap_aux)

    def hop_down(a, d):
        return lax.ppermute(a, "orb", [(k, k - 2) for k in range(2, orb_count) if k // 2 <= chain - d])

    def hop_up(a, d):
        return lax.ppermute(a, "orb", [(k, k + 2) for k in range(orb_count - 2) if k // 2 >= d - 1])

    stored = extend(blocks, virt_energy, wins)

    downs, ups = [stored, hop_down(stored, 1)], [stored, hop_up(stored, 1)]
    local_other = across_aux(stored)

    orbitals = jnp.arange(owner_slot.shape[0], dtype=i32)
    hit_second = pairs[:, 1][:, None] == orbitals[None, :]
    slot_second = jnp.sum(jnp.where(hit_second, owner_slot[None, :], 0), axis=1)
    slots = jnp.arange(n_slots, dtype=i32)
    wanted_flat = jnp.any(slot_second[:, None] == slots[None, :], axis=0).astype(i32)
    wanted_flat = tie(wanted_flat, [stored])
    wanted = wanted_flat.reshape(orb_count, occ_dev) > 0
    wanted_both = jnp.stack([wanted_flat, across_y(wanted_flat)])
    wanted_opp = wanted_both[1].reshape(orb_count, occ_dev) > 0
    local = jnp.arange(occ_dev, dtype=i32)[None, :]

    def two_of(table):
        return jnp.min(jnp.where(table, local, occ_dev - 1), axis=1), jnp.max(jnp.where(table, local, 0), axis=1)

    want, want_opp = two_of(wanted), two_of(wanted_opp)

    first_row = core * own_rows
    own_second = lax.dynamic_slice_in_dim(slot_second, first_row, own_rows, 0)
    own_pairs = lax.dynamic_slice_in_dim(pairs, first_row, own_rows, 0)
    src = own_second // occ_dev
    part = own_second % occ_dev
    rank = jnp.any(
        (slot_second[None, :] // occ_dev == src[:, None]) & (slot_second[None, :] < own_second[:, None]),
        axis=1).astype(i32)
    src_z, src_y = src // 2, src % 2
    dist = jnp.abs(src_z - z)
    is_opp = (src_y != y).astype(i32)
    from_up = src_z < z
    both = 2 * dist <= chain - 1
    is_far = dist == last
    at_hand = (dist <= 1) & (is_opp == 0)
    idx = jnp.where(at_hand, part, rank + jnp.where(both & from_up, 2, 0))
    which_col = jnp.where(dist == 0, 3, jnp.where((dist == 1) & from_up, 2, jnp.where(is_far, 2, 1)))
    which = jnp.where(is_opp == 1, is_far.astype(i32), which_col)
    stage_col = jnp.where(is_far, last - 2, jnp.maximum(dist - 1, 0))
    stage = jnp.where(is_opp == 1, jnp.minimum(dist, last - 1), stage_col)
    rows = jnp.arange(own_rows, dtype=i32)
    before = (stage[None, :] < stage[:, None]) | ((stage[None, :] == stage[:, None]) & (rows[None, :] < rows[:, None]))
    place = jnp.sum(before.astype(i32), axis=1)
    order = jnp.sum(jnp.where(place[None, :] == rows[:, None], rows[None, :], 0), axis=1)
    bounds = jnp.sum((stage[None, :] < jnp.arange(chain + 1, dtype=i32)[:, None]).astype(i32), axis=1)
    width = max(own_rows, chain + 1)

    def padded(v):
        v = v.reshape(-1)
        return jnp.pad(v, (0, width - v.shape[0]))

    meta = jnp.stack([padded(bounds), padded(core * n_first), padded(order), padded(which), padded(idx)])

    def occ(col):
        hit = own_pairs[:, col][:, None] == orbitals[None, :]
        return jnp.sum(jnp.where(hit, occ_energy[None, :], 0.0), axis=1)

    shift = occ(0) + occ(1)
    ve1 = lax.dynamic_slice_in_dim(virt_energy, core * n_first, n_first, 0)
    ve1 = jnp.broadcast_to(ve1[:, :, None], (n_first, full, 128))

    dom = lax.dynamic_slice_in_dim(domains, first_row, own_rows, 0)
    base = jnp.concatenate([jnp.full((r,), b, i32) for b, r, _ in wins])
    span = max(sp for _, _, sp in wins)
    pick = ((dom - base)[..., None] == jnp.arange(span, dtype=i32)).astype(jnp.bfloat16)

    def idx_of(table, source):
        return lax.dynamic_index_in_dim(table, jnp.clip(source, 0, orb_count - 1), 0, keepdims=False)

    def two_for(table, source):
        return [idx_of(table[0], source), idx_of(table[1], source)]

    sets = {}

    def pairs_at(d, after, prev):
        return run_pairs(d, wins, meta, shift, ve1, pick, stored, local_other, sets[d], after, prev)

    def with_other(a):
        return a, across_aux(a)

    y_load = copy_sets([0, 0], two_for(want_opp, o), [stored])
    opp = with_other(across_y(y_load))
    top = orb_count - 1
    tell = [(0, 2), (1, 3), (top, top - 2), (top - 1, top - 3)]
    wanted_far = lax.ppermute(tie(wanted_both, [y_load]), "orb", tell).reshape(2, orb_count, occ_dev) > 0
    far_own, far_opp = two_of(wanted_far[0]), two_of(wanted_far[1])
    early = [opp[1], local_other, pick, meta]
    downs[1], ups[1] = tie(downs[1], early), tie(ups[1], early)
    out = None
    for d in range(1, last):
        s_down, s_up = o + 2 * d, o - 2 * d
        first = []
        if d + 1 < last:
            downs.append(hop_down(downs[d], d + 1))
            ups.append(hop_up(ups[d], d + 1))
        else:
            sends_down = z == 1
            source = jnp.where(sends_down, 2 * last + y, y)
            from_set = [1 - sends_down.astype(i32)] * 4
            perm = [(2, 0), (3, 1), (2 * (last - 1), 2 * last), (2 * (last - 1) + 1, 2 * last + 1)]
            load_over, load_own = copy_sets(
                from_set, two_for(far_opp, source) + two_for(far_own, source), [downs[d], ups[d]], [out], [2, 2])
            far_b = lax.ppermute(across_y(load_over), "orb", perm)
            far_a = lax.ppermute(load_own, "orb", perm)
            first = [load_own]
        if 2 * d <= last:
            place_of = [0, 0, 1, 1]

            def both_ways(table):
                return two_for(table, s_down) + two_for(table, s_up)
        else:
            is_up = (z + d > last).astype(i32)
            place_of = [is_up, is_up]

            def both_ways(table):
                return two_for(table, jnp.where(is_up == 1, s_up, s_down))
        if d == 1:
            theirs = copy_sets(place_of, both_ways(want_opp), [downs[d], ups[d]])
            sets[0] = [opp, with_other(downs[1]), with_other(ups[1]), (stored, local_other)]
            out = pairs_at(0, [theirs], out)
        else:
            theirs, mine = copy_sets(
                place_of * 2, both_ways(want_opp) + both_ways(want), [downs[d], ups[d]], first, [len(place_of)] * 2)
            sets[d - 1] = [with_other(tie(opp, first) if first else opp), with_other(mine)]
            if d + 1 == last:
                sets[d - 1].append(with_other(far_a))
            out = pairs_at(d - 1, [mine], out)
        opp = across_y(theirs)
    sets[last - 1] = [with_other(tie(opp, [out])), with_other(tie(far_b, [out]))]
    return pairs_at(last - 1, [], out)


def solution(mesh):
    in_specs = (
        P(("groups", "orb"), None, "aux"),
        P(("groups", "orb"), None),
        P("groups"),
        P("groups"),
        P(("groups", "orb"), None),
        P(("groups", "orb"), None, None),
    )
    out_specs = P(("groups", "orb", "aux"), None, None)
    return jax.shard_map(
        per_device, mesh=mesh, in_specs=in_specs, out_specs=out_specs, check_vma=False
    )
```

```python
import functools

import jax
import jax.numpy as jnp
from jax import lax
from jax.experimental import pallas as pl
from jax.experimental.pallas import tpu as pltpu
from jax.sharding import PartitionSpec as P

NT = (((1,), (1,)), ((), ()))
VMEM_LIMIT = 63 * 1024 * 1024
EXTRA = 16


def windows(full, kept):
    slack = full - kept
    tile = 256 - slack if 0 <= slack <= 128 else kept
    found = []
    base = 0
    while base < kept:
        rows = min(tile, kept - base)
        found.append((base, rows, rows + slack))
        base += rows
    return found


def pair_kernel(call, wins, n_sets, n_skip, meta_ref, shift_ref, ve1_ref, pick_ref, own_ref, other_ref, *rest):
    sets = [(rest[2 * k], rest[2 * k + 1]) for k in range(n_sets)]
    rest = rest[2 * n_sets + n_skip:]
    (out_ref, first, second, pick, side_a, side_b, e1_buf, out_buf,
     first_sem, second_sem, pick_sem, out_sem) = rest
    pairs_here = out_ref.shape[0]
    kept = out_ref.shape[1]
    half = own_ref.shape[2]
    n_first = first.shape[0]
    lo = meta_ref[0, call]
    hi = meta_ref[0, call + 1]
    base_first = meta_ref[1, 0]

    def first_copies():
        out = []
        for k in range(n_first):
            out.append(pltpu.make_async_copy(
                own_ref.at[base_first + k], first.at[k, :, pl.ds(0, half)], first_sem.at[2 * k]))
            out.append(pltpu.make_async_copy(
                other_ref.at[base_first + k], first.at[k, :, pl.ds(half, half)], first_sem.at[2 * k + 1]))
        return out

    def fetch(i, slot):
        p = meta_ref[2, i]
        which = meta_ref[3, p]
        idx = meta_ref[4, p]
        pltpu.make_async_copy(pick_ref.at[p], pick.at[slot], pick_sem.at[slot]).start()
        for k, (x_own, x_other) in enumerate(sets):
            @pl.when(which == k)
            def _():
                pltpu.make_async_copy(
                    x_own.at[idx], second.at[slot, :, pl.ds(0, half)], second_sem.at[slot, 0]).start()
                pltpu.make_async_copy(
                    x_other.at[idx], second.at[slot, :, pl.ds(half, half)], second_sem.at[slot, 1]).start()

    def await_fetch(slot):
        pltpu.make_async_copy(pick_ref.at[0], pick.at[slot], pick_sem.at[slot]).wait()
        for k in range(2):
            pltpu.make_async_copy(
                sets[0][0].at[0], second.at[slot, :, pl.ds(k * half, half)], second_sem.at[slot, k]).wait()

    def out_copy(p, slot):
        return pltpu.make_async_copy(out_buf.at[slot], out_ref.at[p], out_sem.at[slot])

    @pl.when(hi > lo)
    def _():
        for c in first_copies():
            c.start()
        fetch(lo, lax.rem(lo, 2))
        for c in first_copies():
            c.wait()

    def step(i, carry):
        slot = lax.rem(i, 2)
        p = meta_ref[2, i]
        f = p // (pairs_here // n_first)

        @pl.when(i + 1 < hi)
        def _():
            fetch(i + 1, 1 - slot)

        await_fetch(slot)

        @pl.when(i >= lo + 2)
        def _():
            out_copy(p, slot).wait()

        e2_parts = []
        full = ve1_ref.shape[1]
        for t, (base, rows, span) in enumerate(wins):
            one = pick[slot, 0, base:base + rows, 0:span]
            got = jnp.dot(one, first[f, base:base + span, :], preferred_element_type=jnp.float32)
            side_a[base:base + rows, :] = got.astype(jnp.bfloat16)
            e1_buf[base:base + rows, :] = jnp.dot(
                one, ve1_ref[f, base:base + span, :], preferred_element_type=jnp.float32)
            two = pick[slot, 1, base:base + rows, 0:span]
            got = jnp.dot(two, second[slot, base:base + span, :], preferred_element_type=jnp.float32)
            side_b[base:base + rows, :] = got.astype(jnp.bfloat16)
            ve = second[slot, full:full + EXTRA, 0:span]
            e2_parts.append(
                lax.dot_general(ve, two, NT, preferred_element_type=jnp.float32)[t:t + 1])
        e2 = jnp.concatenate(e2_parts, axis=1)
        shift = shift_ref[p]
        chunk = min(kept, 256)
        for start in range(0, kept, chunk):
            c = lax.dot_general(
                side_a[...], side_b[start:start + chunk, :], NT, preferred_element_type=jnp.float32)
            for col in range(0, chunk, 128):
                den = e1_buf[...] + e2[:, start + col:start + col + 128] - shift
                inv = pl.reciprocal(den, approx=True)
                neg = inv * (den * inv - 2.0)
                out_buf[slot, :, start + col:start + col + 128] = (
                    c[:, col:col + 128] * neg).astype(jnp.bfloat16)
        out_copy(p, slot).start()
        return carry

    lax.fori_loop(lo, hi, step, 0)

    @pl.when(hi - lo >= 2)
    def _():
        out_copy(0, lax.rem(hi, 2)).wait()

    @pl.when(hi > lo)
    def _():
        out_copy(0, lax.rem(hi + 1, 2)).wait()


def run_pairs(call, wins, meta, shift, ve1, pick, own, other, sets, after, prev):
    pairs_here, _, kept, span = pick.shape
    n_first = ve1.shape[0]
    full, half = own.shape[1], own.shape[2]
    any_spec = ANY_SPEC
    smem = pl.BlockSpec(memory_space=pltpu.SMEM)
    vmem = pl.BlockSpec(memory_space=pltpu.VMEM)
    operands = [meta, shift, ve1, pick, own, other]
    for pair in sets:
        operands += list(pair)
    operands += after
    in_specs = [smem, smem, vmem] + [any_spec] * (len(operands) - 3)
    aliases = {}
    if prev is not None:
        aliases = {len(operands): 0}
        operands.append(prev)
        in_specs.append(any_spec)
    bf = jnp.bfloat16
    return pl.pallas_call(
        functools.partial(pair_kernel, call, wins, len(sets), len(after) + (prev is not None)),
        out_shape=jax.ShapeDtypeStruct((pairs_here, kept, kept), bf),
        in_specs=in_specs,
        out_specs=any_spec,
        scratch_shapes=[
            pltpu.VMEM((n_first, full, 2 * half), bf),
            pltpu.VMEM((2, full, 2 * half), bf),
            pltpu.VMEM((2, 2, kept, span), bf),
            pltpu.VMEM((kept, 2 * half), bf),
            pltpu.VMEM((kept, 2 * half), bf),
            pltpu.VMEM((kept, 128), jnp.float32),
            pltpu.VMEM((2, kept, kept), bf),
            pltpu.SemaphoreType.DMA((2 * n_first,)),
            pltpu.SemaphoreType.DMA((2, 2)),
            pltpu.SemaphoreType.DMA((2,)),
            pltpu.SemaphoreType.DMA((2,)),
        ],
        input_output_aliases=aliases,
        compiler_params=pltpu.CompilerParams(vmem_limit_bytes=VMEM_LIMIT),
        cost_estimate=pl.CostEstimate(flops=0, bytes_accessed=0, transcendentals=0),
        name=f"pairs_{call}",
    )(*operands)


def set_kernel(n_arrays, n_skip, sizes, table_ref, *rest):
    arrays = rest[:n_arrays]
    outs = rest[n_arrays + n_skip:-3]
    held, in_sems, out_sems = rest[-3:]
    places = [(o, k) for o, size in zip(outs, sizes) for k in range(size)]
    for j in range(len(places)):
        for k, a in enumerate(arrays):
            @pl.when(table_ref[0, j] == k)
            def _():
                pltpu.make_async_copy(a.at[table_ref[1, j]], held.at[j], in_sems.at[j]).start()
    for j, (o, k) in enumerate(places):
        pltpu.make_async_copy(arrays[0].at[0], held.at[j], in_sems.at[j]).wait()
        pltpu.make_async_copy(held.at[j], o.at[k], out_sems.at[j]).start()
    for j, (o, k) in enumerate(places):
        pltpu.make_async_copy(held.at[j], o.at[k], out_sems.at[j]).wait()


ANY_SPEC = pl.BlockSpec(memory_space=pl.ANY)


def copy_sets(which, index, arrays, after=(), sizes=None):
    n = len(index)
    sizes = sizes or [n]
    table = jnp.stack([jnp.stack([jnp.asarray(w, jnp.int32) for w in which]), jnp.stack(index)])
    block = arrays[0].shape[1:]
    outs = pl.pallas_call(
        functools.partial(set_kernel, len(arrays), len(after), sizes),
        out_shape=[jax.ShapeDtypeStruct((size,) + block, arrays[0].dtype) for size in sizes],
        in_specs=[pl.BlockSpec(memory_space=pltpu.SMEM)] + [ANY_SPEC] * (len(arrays) + len(after)),
        out_specs=[ANY_SPEC] * len(sizes),
        scratch_shapes=[
            pltpu.VMEM((n,) + block, arrays[0].dtype),
            pltpu.SemaphoreType.DMA((n,)),
            pltpu.SemaphoreType.DMA((n,))],
        cost_estimate=pl.CostEstimate(flops=0, bytes_accessed=0, transcendentals=0),
        compiler_params=pltpu.CompilerParams(vmem_limit_bytes=VMEM_LIMIT),
        name="copy_sets",
    )(table, *arrays, *after)
    return outs if len(sizes) > 1 else outs[0]


def extend_kernel(wins, blocks_ref, energy_ref, out_ref, held, in_sems, out_sems):
    count, full, half = blocks_ref.shape
    for k in range(count):
        pltpu.make_async_copy(blocks_ref.at[k], held.at[k, 0:full], in_sems.at[k]).start()
    energy = energy_ref[...].astype(jnp.float32)
    span = max(sp for _, _, sp in wins)
    row = lax.broadcasted_iota(jnp.int32, (EXTRA, span), 0)
    for k in range(count):
        held[k, full:, :] = jnp.zeros((EXTRA, half), held.dtype)
        rows = jnp.zeros((EXTRA, span), jnp.float32)
        for t, (base, _, sp) in enumerate(wins):
            piece = energy[k:k + 1, base:base + sp]
            if sp < span:
                piece = jnp.concatenate([piece, jnp.zeros((1, span - sp), jnp.float32)], axis=1)
            rows = jnp.where(row == t, jnp.broadcast_to(piece, (EXTRA, span)), rows)
        held[k, full:, 0:span] = rows.astype(held.dtype)
    for k in range(count):
        pltpu.make_async_copy(blocks_ref.at[k], held.at[k, 0:full], in_sems.at[k]).wait()
        pltpu.make_async_copy(held.at[k], out_ref.at[k], out_sems.at[k]).start()
    for k in range(count):
        pltpu.make_async_copy(held.at[k], out_ref.at[k], out_sems.at[k]).wait()


def extend(blocks, energy, wins):
    count, full, half = blocks.shape
    shape = (count, full + EXTRA, half)
    return pl.pallas_call(
        functools.partial(extend_kernel, wins),
        out_shape=jax.ShapeDtypeStruct(shape, blocks.dtype),
        in_specs=[ANY_SPEC, pl.BlockSpec(memory_space=pltpu.VMEM)],
        out_specs=ANY_SPEC,
        scratch_shapes=[
            pltpu.VMEM(shape, blocks.dtype), pltpu.SemaphoreType.DMA((count,)), pltpu.SemaphoreType.DMA((count,))],
        compiler_params=pltpu.CompilerParams(vmem_limit_bytes=VMEM_LIMIT),
        name="extend",
    )(blocks, energy)


def tie(x, deps):
    return pl.pallas_call(
        lambda *refs: None,
        out_shape=jax.ShapeDtypeStruct(x.shape, x.dtype),
        in_specs=[ANY_SPEC] * (1 + len(deps)),
        out_specs=ANY_SPEC,
        input_output_aliases={0: 0},
        compiler_params=pltpu.CompilerParams(vmem_limit_bytes=VMEM_LIMIT),
        cost_estimate=pl.CostEstimate(flops=0, bytes_accessed=0, transcendentals=0),
        name="tie",
    )(x, *deps)


def per_device(blocks, virt_energy, occ_energy, owner_slot, pairs, domains):
    orb_count = lax.axis_size("orb")
    aux_count = lax.axis_size("aux")
    occ_dev, full, half = blocks.shape
    pair_dev = pairs.shape[0]
    kept = domains.shape[2]
    own_rows = pair_dev // aux_count
    n_first = occ_dev // aux_count
    core = lax.axis_index("aux")
    o = lax.axis_index("orb")
    z, y = o // 2, o % 2
    chain = orb_count // 2
    last = chain - 1
    n_slots = orb_count * occ_dev
    i32 = jnp.int32
    wins = windows(full, kept)

    swap_aux = [(0, 1), (1, 0)]
    swap_y = [(k, k ^ 1) for k in range(orb_count)]

    def across_y(a):
        return lax.ppermute(a, "orb", swap_y)

    def across_y_inside(a):
        return lax.ppermute(a, "orb", [pair for pair in swap_y if 0 < pair[0] // 2 < last])

    def across_aux(a):
        return lax.ppermute(a, "aux", swap_aux)

    def hop_down(a, d):
        return lax.ppermute(a, "orb", [(k, k - 2) for k in range(2, orb_count) if k // 2 <= chain - d])

    def hop_up(a, d):
        return lax.ppermute(a, "orb", [(k, k + 2) for k in range(orb_count - 2) if k // 2 >= d - 1])

    stored = extend(blocks, virt_energy, wins)

    downs, ups = [stored, hop_down(stored, 1)], [stored, hop_up(stored, 1)]
    local_other = across_aux(stored)

    orbitals = jnp.arange(owner_slot.shape[0], dtype=i32)
    hit_second = pairs[:, 1][:, None] == orbitals[None, :]
    slot_second = jnp.sum(jnp.where(hit_second, owner_slot[None, :], 0), axis=1)
    slots = jnp.arange(n_slots, dtype=i32)
    wanted_flat = jnp.any(slot_second[:, None] == slots[None, :], axis=0).astype(i32)
    wanted_flat = tie(wanted_flat, [stored])
    wanted = wanted_flat.reshape(orb_count, occ_dev) > 0
    wanted_both = jnp.stack([wanted_flat, across_y(wanted_flat)])
    wanted_opp = wanted_both[1].reshape(orb_count, occ_dev) > 0
    local = jnp.arange(occ_dev, dtype=i32)[None, :]

    def two_of(table):
        return jnp.min(jnp.where(table, local, occ_dev - 1), axis=1), jnp.max(jnp.where(table, local, 0), axis=1)

    want, want_opp = two_of(wanted), two_of(wanted_opp)

    first_row = core * own_rows
    own_second = lax.dynamic_slice_in_dim(slot_second, first_row, own_rows, 0)
    own_pairs = lax.dynamic_slice_in_dim(pairs, first_row, own_rows, 0)
    src = own_second // occ_dev
    part = own_second % occ_dev
    rank = jnp.any(
        (slot_second[None, :] // occ_dev == src[:, None]) & (slot_second[None, :] < own_second[:, None]),
        axis=1).astype(i32)
    src_z, src_y = src // 2, src % 2
    dist = jnp.abs(src_z - z)
    is_opp = (src_y != y).astype(i32)
    from_up = src_z < z
    both = 2 * dist <= chain - 1
    is_far = dist == last
    at_hand = (dist <= 1) & (is_opp == 0)
    idx = jnp.where(at_hand, part, rank + jnp.where(both & from_up, 2, 0))
    which_col = jnp.where(dist == 0, 3, jnp.where((dist == 1) & from_up, 2, jnp.where(is_far, 2, 1)))
    at_end = (z == 0) | (z == last)
    is_early = at_end & (dist == last - 1)
    which = jnp.where(is_opp == 1, jnp.where(is_early, 3, is_far.astype(i32)), which_col)
    stage_col = jnp.where(is_far, last - 2, jnp.maximum(dist - 1, 0))
    stage = jnp.where(is_opp == 1, jnp.minimum(dist, last - 1) - is_early.astype(i32), stage_col)
    rows = jnp.arange(own_rows, dtype=i32)
    before = (stage[None, :] < stage[:, None]) | ((stage[None, :] == stage[:, None]) & (rows[None, :] < rows[:, None]))
    place = jnp.sum(before.astype(i32), axis=1)
    order = jnp.sum(jnp.where(place[None, :] == rows[:, None], rows[None, :], 0), axis=1)
    bounds = jnp.sum((stage[None, :] < jnp.arange(chain + 1, dtype=i32)[:, None]).astype(i32), axis=1)
    width = max(own_rows, chain + 1)

    def padded(v):
        v = v.reshape(-1)
        return jnp.pad(v, (0, width - v.shape[0]))

    meta = jnp.stack([padded(bounds), padded(core * n_first), padded(order), padded(which), padded(idx)])

    def occ(col):
        hit = own_pairs[:, col][:, None] == orbitals[None, :]
        return jnp.sum(jnp.where(hit, occ_energy[None, :], 0.0), axis=1)

    shift = occ(0) + occ(1)
    ve1 = lax.dynamic_slice_in_dim(virt_energy, core * n_first, n_first, 0)
    ve1 = jnp.broadcast_to(ve1[:, :, None], (n_first, full, 128))

    dom = lax.dynamic_slice_in_dim(domains, first_row, own_rows, 0)
    base = jnp.concatenate([jnp.full((r,), b, i32) for b, r, _ in wins])
    span = max(sp for _, _, sp in wins)
    pick = ((dom - base)[..., None] == jnp.arange(span, dtype=i32)).astype(jnp.bfloat16)

    def idx_of(table, source):
        return lax.dynamic_index_in_dim(table, jnp.clip(source, 0, orb_count - 1), 0, keepdims=False)

    def two_for(table, source):
        return [idx_of(table[0], source), idx_of(table[1], source)]

    sets = {}

    def pairs_at(d, after, prev):
        return run_pairs(d, wins, meta, shift, ve1, pick, stored, local_other, sets[d], after, prev)

    def with_other(a):
        return a, across_aux(a)

    y_load = copy_sets([0, 0], two_for(want_opp, o), [stored])
    opp = with_other(across_y(y_load))
    top = orb_count - 1
    tell = [(0, 2), (1, 3), (top, top - 2), (top - 1, top - 3)]
    wanted_far = lax.ppermute(tie(wanted_both, [y_load]), "orb", tell).reshape(2, orb_count, occ_dev) > 0
    far_own, far_opp = two_of(wanted_far[0]), two_of(wanted_far[1])
    early = [opp[1], local_other, pick, meta]
    downs[1], ups[1] = tie(downs[1], early), tie(ups[1], early)
    out = None
    for d in range(1, last):
        s_down, s_up = o + 2 * d, o - 2 * d
        first = []
        if d + 1 < last:
            downs.append(hop_down(downs[d], d + 1))
            ups.append(hop_up(ups[d], d + 1))
        else:
            sends_down = z == 1
            source = jnp.where(sends_down, 2 * last + y, y)
            from_set = [1 - sends_down.astype(i32)] * 4
            perm = [(2, 0), (3, 1), (2 * (last - 1), 2 * last), (2 * (last - 1) + 1, 2 * last + 1)]
            over_set = jnp.where(at_end, (z == last).astype(i32), from_set[0])
            end_source = jnp.where(z == 0, s_down, s_up)
            over_pick = [
                jnp.where(at_end, a, b) for a, b in zip(two_for(want_opp, end_source), two_for(far_opp, source))]
            load_over, load_own = copy_sets(
                [over_set] * 2 + from_set[2:], over_pick + two_for(far_own, source), [downs[d], ups[d]], [out], [2, 2])
            over = across_y(load_over)
            far_b = lax.ppermute(over, "orb", perm)
            far_a = lax.ppermute(load_own, "orb", perm)
            first = [load_own]
        if 2 * d <= last:
            place_of = [0, 0, 1, 1]

            def both_ways(table):
                return two_for(table, s_down) + two_for(table, s_up)
        else:
            is_up = (z + d > last).astype(i32)
            place_of = [is_up, is_up]

            def both_ways(table):
                return two_for(table, jnp.where(is_up == 1, s_up, s_down))
        if d == 1:
            theirs = copy_sets(place_of, both_ways(want_opp), [downs[d], ups[d]])
            sets[0] = [opp, with_other(downs[1]), with_other(ups[1]), (stored, local_other)]
            out = pairs_at(0, [theirs], out)
        else:
            theirs, mine = copy_sets(
                place_of * 2, both_ways(want_opp) + both_ways(want), [downs[d], ups[d]], first, [len(place_of)] * 2)
            sets[d - 1] = [with_other(tie(opp, first) if first else opp), with_other(mine)]
            if d + 1 == last:
                sets[d - 1] += [with_other(far_a), with_other(over)]
            out = pairs_at(d - 1, [mine], out)
        opp = across_y(theirs) if d + 1 < last else across_y_inside(theirs)
    sets[last - 1] = [with_other(tie(opp, [out])), with_other(tie(far_b, [out]))]
    return pairs_at(last - 1, [], out)


def solution(mesh):
    in_specs = (
        P(("groups", "orb"), None, "aux"),
        P(("groups", "orb"), None),
        P("groups"),
        P("groups"),
        P(("groups", "orb"), None),
        P(("groups", "orb"), None, None),
    )
    out_specs = P(("groups", "orb", "aux"), None, None)
    return jax.shard_map(
        per_device, mesh=mesh, in_specs=in_specs, out_specs=out_specs, check_vma=False
    )
```

```python
import functools

import jax
import jax.numpy as jnp
from jax import lax
from jax.experimental import pallas as pl
from jax.experimental.pallas import tpu as pltpu
from jax.sharding import PartitionSpec as P

NT = (((1,), (1,)), ((), ()))
VMEM_LIMIT = 63 * 1024 * 1024
EXTRA = 16


def windows(full, kept):
    slack = full - kept
    tile = 256 - slack if 0 <= slack <= 128 else kept
    found = []
    base = 0
    while base < kept:
        rows = min(tile, kept - base)
        found.append((base, rows, rows + slack))
        base += rows
    return found


def pair_kernel(call, wins, n_sets, n_skip, meta_ref, shift_ref, ve1_ref, pick_ref, own_ref, other_ref, *rest):
    sets = [(rest[2 * k], rest[2 * k + 1]) for k in range(n_sets)]
    rest = rest[2 * n_sets + n_skip:]
    (out_ref, first, second, pick, side_a, side_b, e1_buf, out_buf,
     first_sem, second_sem, pick_sem, out_sem) = rest
    pairs_here = out_ref.shape[0]
    kept = out_ref.shape[1]
    half = own_ref.shape[2]
    n_first = first.shape[0]
    lo = meta_ref[0, call]
    hi = meta_ref[0, call + 1]
    base_first = meta_ref[1, 0]

    def first_copies():
        out = []
        for k in range(n_first):
            out.append(pltpu.make_async_copy(
                own_ref.at[base_first + k], first.at[k, :, pl.ds(0, half)], first_sem.at[2 * k]))
            out.append(pltpu.make_async_copy(
                other_ref.at[base_first + k], first.at[k, :, pl.ds(half, half)], first_sem.at[2 * k + 1]))
        return out

    def fetch(i, slot):
        p = meta_ref[2, i]
        which = meta_ref[3, p]
        idx = meta_ref[4, p]
        pltpu.make_async_copy(pick_ref.at[p], pick.at[slot], pick_sem.at[slot]).start()
        for k, (x_own, x_other) in enumerate(sets):
            @pl.when(which == k)
            def _():
                pltpu.make_async_copy(
                    x_own.at[idx], second.at[slot, :, pl.ds(0, half)], second_sem.at[slot, 0]).start()
                pltpu.make_async_copy(
                    x_other.at[idx], second.at[slot, :, pl.ds(half, half)], second_sem.at[slot, 1]).start()

    def await_fetch(slot):
        pltpu.make_async_copy(pick_ref.at[0], pick.at[slot], pick_sem.at[slot]).wait()
        for k in range(2):
            pltpu.make_async_copy(
                sets[0][0].at[0], second.at[slot, :, pl.ds(k * half, half)], second_sem.at[slot, k]).wait()

    def out_copy(p, slot):
        return pltpu.make_async_copy(out_buf.at[slot], out_ref.at[p], out_sem.at[slot])

    @pl.when(hi > lo)
    def _():
        for c in first_copies():
            c.start()
        fetch(lo, lax.rem(lo, 2))
        for c in first_copies():
            c.wait()

    def step(i, carry):
        slot = lax.rem(i, 2)
        p = meta_ref[2, i]
        f = p // (pairs_here // n_first)

        @pl.when(i + 1 < hi)
        def _():
            fetch(i + 1, 1 - slot)

        await_fetch(slot)

        @pl.when(i >= lo + 2)
        def _():
            out_copy(p, slot).wait()

        e2_parts = []
        full = ve1_ref.shape[1]
        for t, (base, rows, span) in enumerate(wins):
            one = pick[slot, 0, base:base + rows, 0:span]
            got = jnp.dot(one, first[f, base:base + span, :], preferred_element_type=jnp.float32)
            side_a[base:base + rows, :] = got.astype(jnp.bfloat16)
            e1_buf[base:base + rows, :] = jnp.dot(
                one, ve1_ref[f, base:base + span, :], preferred_element_type=jnp.float32)
            two = pick[slot, 1, base:base + rows, 0:span]
            got = jnp.dot(two, second[slot, base:base + span, :], preferred_element_type=jnp.float32)
            side_b[base:base + rows, :] = got.astype(jnp.bfloat16)
            ve = second[slot, full:full + EXTRA, 0:span]
            e2_parts.append(
                lax.dot_general(ve, two, NT, preferred_element_type=jnp.float32)[t:t + 1])
        e2 = jnp.concatenate(e2_parts, axis=1)
        shift = shift_ref[p]
        chunk = min(kept, 256)
        for start in range(0, kept, chunk):
            c = lax.dot_general(
                side_a[...], side_b[start:start + chunk, :], NT, preferred_element_type=jnp.float32)
            for col in range(0, chunk, 128):
                den = e1_buf[...] + e2[:, start + col:start + col + 128] - shift
                inv = pl.reciprocal(den, approx=True)
                neg = inv * (den * inv - 2.0)
                out_buf[slot, :, start + col:start + col + 128] = (
                    c[:, col:col + 128] * neg).astype(jnp.bfloat16)
        out_copy(p, slot).start()
        return carry

    lax.fori_loop(lo, hi, step, 0)

    @pl.when(hi - lo >= 2)
    def _():
        out_copy(0, lax.rem(hi, 2)).wait()

    @pl.when(hi > lo)
    def _():
        out_copy(0, lax.rem(hi + 1, 2)).wait()


def run_pairs(call, wins, meta, shift, ve1, pick, own, other, sets, after, prev):
    pairs_here, _, kept, span = pick.shape
    n_first = ve1.shape[0]
    full, half = own.shape[1], own.shape[2]
    any_spec = ANY_SPEC
    smem = pl.BlockSpec(memory_space=pltpu.SMEM)
    vmem = pl.BlockSpec(memory_space=pltpu.VMEM)
    operands = [meta, shift, ve1, pick, own, other]
    for pair in sets:
        operands += list(pair)
    operands += after
    in_specs = [smem, smem, vmem] + [any_spec] * (len(operands) - 3)
    aliases = {}
    if prev is not None:
        aliases = {len(operands): 0}
        operands.append(prev)
        in_specs.append(any_spec)
    bf = jnp.bfloat16
    return pl.pallas_call(
        functools.partial(pair_kernel, call, wins, len(sets), len(after) + (prev is not None)),
        out_shape=jax.ShapeDtypeStruct((pairs_here, kept, kept), bf),
        in_specs=in_specs,
        out_specs=any_spec,
        scratch_shapes=[
            pltpu.VMEM((n_first, full, 2 * half), bf),
            pltpu.VMEM((2, full, 2 * half), bf),
            pltpu.VMEM((2, 2, kept, span), bf),
            pltpu.VMEM((kept, 2 * half), bf),
            pltpu.VMEM((kept, 2 * half), bf),
            pltpu.VMEM((kept, 128), jnp.float32),
            pltpu.VMEM((2, kept, kept), bf),
            pltpu.SemaphoreType.DMA((2 * n_first,)),
            pltpu.SemaphoreType.DMA((2, 2)),
            pltpu.SemaphoreType.DMA((2,)),
            pltpu.SemaphoreType.DMA((2,)),
        ],
        input_output_aliases=aliases,
        compiler_params=pltpu.CompilerParams(vmem_limit_bytes=VMEM_LIMIT),
        cost_estimate=pl.CostEstimate(flops=0, bytes_accessed=0, transcendentals=0),
        name=f"pairs_{call}",
    )(*operands)


def set_kernel(n_arrays, n_skip, sizes, table_ref, *rest):
    arrays = rest[:n_arrays]
    outs = rest[n_arrays + n_skip:-3]
    held, in_sems, out_sems = rest[-3:]
    places = [(o, k) for o, size in zip(outs, sizes) for k in range(size)]
    for j in range(len(places)):
        for k, a in enumerate(arrays):
            @pl.when(table_ref[0, j] == k)
            def _():
                pltpu.make_async_copy(a.at[table_ref[1, j]], held.at[j], in_sems.at[j]).start()
    for j, (o, k) in enumerate(places):
        pltpu.make_async_copy(arrays[0].at[0], held.at[j], in_sems.at[j]).wait()
        pltpu.make_async_copy(held.at[j], o.at[k], out_sems.at[j]).start()
    for j, (o, k) in enumerate(places):
        pltpu.make_async_copy(held.at[j], o.at[k], out_sems.at[j]).wait()


ANY_SPEC = pl.BlockSpec(memory_space=pl.ANY)


def copy_sets(which, index, arrays, after=(), sizes=None):
    n = len(index)
    sizes = sizes or [n]
    table = jnp.stack([jnp.stack([jnp.asarray(w, jnp.int32) for w in which]), jnp.stack(index)])
    block = arrays[0].shape[1:]
    outs = pl.pallas_call(
        functools.partial(set_kernel, len(arrays), len(after), sizes),
        out_shape=[jax.ShapeDtypeStruct((size,) + block, arrays[0].dtype) for size in sizes],
        in_specs=[pl.BlockSpec(memory_space=pltpu.SMEM)] + [ANY_SPEC] * (len(arrays) + len(after)),
        out_specs=[ANY_SPEC] * len(sizes),
        scratch_shapes=[
            pltpu.VMEM((n,) + block, arrays[0].dtype),
            pltpu.SemaphoreType.DMA((n,)),
            pltpu.SemaphoreType.DMA((n,))],
        cost_estimate=pl.CostEstimate(flops=0, bytes_accessed=0, transcendentals=0),
        compiler_params=pltpu.CompilerParams(vmem_limit_bytes=VMEM_LIMIT),
        name="copy_sets",
    )(table, *arrays, *after)
    return outs if len(sizes) > 1 else outs[0]


def extend_kernel(wins, blocks_ref, energy_ref, out_ref, held, in_sems, out_sems):
    count, full, half = blocks_ref.shape
    for k in range(count):
        pltpu.make_async_copy(blocks_ref.at[k], held.at[k, 0:full], in_sems.at[k]).start()
    energy = energy_ref[...].astype(jnp.float32)
    span = max(sp for _, _, sp in wins)
    row = lax.broadcasted_iota(jnp.int32, (EXTRA, span), 0)
    for k in range(count):
        held[k, full:, :] = jnp.zeros((EXTRA, half), held.dtype)
        rows = jnp.zeros((EXTRA, span), jnp.float32)
        for t, (base, _, sp) in enumerate(wins):
            piece = energy[k:k + 1, base:base + sp]
            if sp < span:
                piece = jnp.concatenate([piece, jnp.zeros((1, span - sp), jnp.float32)], axis=1)
            rows = jnp.where(row == t, jnp.broadcast_to(piece, (EXTRA, span)), rows)
        held[k, full:, 0:span] = rows.astype(held.dtype)
    for k in range(count):
        pltpu.make_async_copy(blocks_ref.at[k], held.at[k, 0:full], in_sems.at[k]).wait()
        pltpu.make_async_copy(held.at[k], out_ref.at[k], out_sems.at[k]).start()
    for k in range(count):
        pltpu.make_async_copy(held.at[k], out_ref.at[k], out_sems.at[k]).wait()


def extend(blocks, energy, wins):
    count, full, half = blocks.shape
    shape = (count, full + EXTRA, half)
    return pl.pallas_call(
        functools.partial(extend_kernel, wins),
        out_shape=jax.ShapeDtypeStruct(shape, blocks.dtype),
        in_specs=[ANY_SPEC, pl.BlockSpec(memory_space=pltpu.VMEM)],
        out_specs=ANY_SPEC,
        scratch_shapes=[
            pltpu.VMEM(shape, blocks.dtype), pltpu.SemaphoreType.DMA((count,)), pltpu.SemaphoreType.DMA((count,))],
        compiler_params=pltpu.CompilerParams(vmem_limit_bytes=VMEM_LIMIT),
        name="extend",
    )(blocks, energy)


def tie(x, deps):
    return pl.pallas_call(
        lambda *refs: None,
        out_shape=jax.ShapeDtypeStruct(x.shape, x.dtype),
        in_specs=[ANY_SPEC] * (1 + len(deps)),
        out_specs=ANY_SPEC,
        input_output_aliases={0: 0},
        compiler_params=pltpu.CompilerParams(vmem_limit_bytes=VMEM_LIMIT),
        cost_estimate=pl.CostEstimate(flops=0, bytes_accessed=0, transcendentals=0),
        name="tie",
    )(x, *deps)


def per_device(blocks, virt_energy, occ_energy, owner_slot, pairs, domains):
    orb_count = lax.axis_size("orb")
    aux_count = lax.axis_size("aux")
    occ_dev, full, half = blocks.shape
    pair_dev = pairs.shape[0]
    kept = domains.shape[2]
    own_rows = pair_dev // aux_count
    n_first = occ_dev // aux_count
    core = lax.axis_index("aux")
    o = lax.axis_index("orb")
    z, y = o // 2, o % 2
    chain = orb_count // 2
    last = chain - 1
    n_slots = orb_count * occ_dev
    i32 = jnp.int32
    wins = windows(full, kept)

    swap_aux = [(0, 1), (1, 0)]
    swap_y = [(k, k ^ 1) for k in range(orb_count)]

    def across_y(a):
        return lax.ppermute(a, "orb", swap_y)

    def across_y_inside(a):
        return lax.ppermute(a, "orb", [pair for pair in swap_y if 0 < pair[0] // 2 < last])

    def across_aux(a):
        return lax.ppermute(a, "aux", swap_aux)

    def hop_down(a, d):
        return lax.ppermute(a, "orb", [(k, k - 2) for k in range(2, orb_count) if k // 2 <= chain - d])

    def hop_up(a, d):
        return lax.ppermute(a, "orb", [(k, k + 2) for k in range(orb_count - 2) if k // 2 >= d - 1])

    stored = extend(blocks, virt_energy, wins)

    downs, ups = [stored, hop_down(stored, 1)], [stored, hop_up(stored, 1)]
    local_other = across_aux(stored)

    orbitals = jnp.arange(owner_slot.shape[0], dtype=i32)
    hit_second = pairs[:, 1][:, None] == orbitals[None, :]
    slot_second = jnp.sum(jnp.where(hit_second, owner_slot[None, :], 0), axis=1)
    slots = jnp.arange(n_slots, dtype=i32)
    wanted_flat = jnp.any(slot_second[:, None] == slots[None, :], axis=0).astype(i32)
    wanted_flat = tie(wanted_flat, [stored])
    wanted = wanted_flat.reshape(orb_count, occ_dev) > 0
    wanted_both = jnp.stack([wanted_flat, across_y(wanted_flat)])
    wanted_opp = wanted_both[1].reshape(orb_count, occ_dev) > 0
    local = jnp.arange(occ_dev, dtype=i32)[None, :]

    def two_of(table):
        return jnp.min(jnp.where(table, local, occ_dev - 1), axis=1), jnp.max(jnp.where(table, local, 0), axis=1)

    want, want_opp = two_of(wanted), two_of(wanted_opp)

    first_row = core * own_rows
    own_second = lax.dynamic_slice_in_dim(slot_second, first_row, own_rows, 0)
    own_pairs = lax.dynamic_slice_in_dim(pairs, first_row, own_rows, 0)
    src = own_second // occ_dev
    part = own_second % occ_dev
    rank = jnp.any(
        (slot_second[None, :] // occ_dev == src[:, None]) & (slot_second[None, :] < own_second[:, None]),
        axis=1).astype(i32)
    src_z, src_y = src // 2, src % 2
    dist = jnp.abs(src_z - z)
    is_opp = (src_y != y).astype(i32)
    from_up = src_z < z
    both = 2 * dist <= chain - 1
    is_far = dist == last
    at_hand = (dist <= 1) & (is_opp == 0)
    idx = jnp.where(at_hand, part, rank + jnp.where(both & from_up, 2, 0))
    which_col = jnp.where(dist == 0, 3, jnp.where((dist == 1) & from_up, 2, jnp.where(is_far, 2, 1)))
    at_end = (z == 0) | (z == last)
    is_early = at_end & (dist == last - 1)
    which = jnp.where(is_opp == 1, jnp.where(is_early, 3, (dist == last - 1).astype(i32)), which_col)
    stage_col = jnp.where(is_far, last - 2, jnp.maximum(dist - 1, 0))
    stage = jnp.where(is_opp == 1, jnp.minimum(dist, last - 1) - is_early.astype(i32), stage_col)
    rows = jnp.arange(own_rows, dtype=i32)
    before = (stage[None, :] < stage[:, None]) | ((stage[None, :] == stage[:, None]) & (rows[None, :] < rows[:, None]))
    place = jnp.sum(before.astype(i32), axis=1)
    order = jnp.sum(jnp.where(place[None, :] == rows[:, None], rows[None, :], 0), axis=1)
    bounds = jnp.sum((stage[None, :] < jnp.arange(chain + 1, dtype=i32)[:, None]).astype(i32), axis=1)
    width = max(own_rows, chain + 1)

    def padded(v):
        v = v.reshape(-1)
        return jnp.pad(v, (0, width - v.shape[0]))

    meta = jnp.stack([padded(bounds), padded(core * n_first), padded(order), padded(which), padded(idx)])

    def occ(col):
        hit = own_pairs[:, col][:, None] == orbitals[None, :]
        return jnp.sum(jnp.where(hit, occ_energy[None, :], 0.0), axis=1)

    shift = occ(0) + occ(1)
    ve1 = lax.dynamic_slice_in_dim(virt_energy, core * n_first, n_first, 0)
    ve1 = jnp.broadcast_to(ve1[:, :, None], (n_first, full, 128))

    dom = lax.dynamic_slice_in_dim(domains, first_row, own_rows, 0)
    base = jnp.concatenate([jnp.full((r,), b, i32) for b, r, _ in wins])
    span = max(sp for _, _, sp in wins)
    pick = ((dom - base)[..., None] == jnp.arange(span, dtype=i32)).astype(jnp.bfloat16)

    def idx_of(table, source):
        return lax.dynamic_index_in_dim(table, jnp.clip(source, 0, orb_count - 1), 0, keepdims=False)

    def two_for(table, source):
        return [idx_of(table[0], source), idx_of(table[1], source)]

    sets = {}

    def pairs_at(d, after, prev):
        return run_pairs(d, wins, meta, shift, ve1, pick, stored, local_other, sets[d], after, prev)

    def with_other(a):
        return a, across_aux(a)

    y_load = copy_sets([0, 0], two_for(want_opp, o), [stored])
    opp = with_other(across_y(y_load))
    top = orb_count - 1
    tell = [(0, 2), (1, 3), (top, top - 2), (top - 1, top - 3)]
    wanted_far = lax.ppermute(tie(wanted_both, [y_load]), "orb", tell).reshape(2, orb_count, occ_dev) > 0
    far_own, far_opp = two_of(wanted_far[0]), two_of(wanted_far[1])
    early = [opp[1], local_other, pick, meta]
    downs[1], ups[1] = tie(downs[1], early), tie(ups[1], early)
    out = None
    for d in range(1, last):
        s_down, s_up = o + 2 * d, o - 2 * d
        first = []
        if d + 1 < last:
            downs.append(hop_down(downs[d], d + 1))
            ups.append(hop_up(ups[d], d + 1))
        else:
            sends_down = z == 1
            source = jnp.where(sends_down, 2 * last + y, y)
            from_set = [1 - sends_down.astype(i32)] * 4
            perm = [(2, 0), (3, 1), (2 * (last - 1), 2 * last), (2 * (last - 1) + 1, 2 * last + 1)]
            over_set = jnp.where(at_end, (z == last).astype(i32), from_set[0])
            end_source = jnp.where(z == 0, s_down, s_up)
            over_pick = [
                jnp.where(at_end, a, b) for a, b in zip(two_for(want_opp, end_source), two_for(far_opp, source))]
            load_over, load_own = copy_sets(
                [over_set] * 2 + from_set[2:], over_pick + two_for(far_own, source), [downs[d], ups[d]], [out], [2, 2])
            over = across_y(load_over)
            far_b = lax.ppermute(over, "orb", perm)
            far_a = lax.ppermute(load_own, "orb", perm)
            first = [load_own]
        if 2 * d <= last:
            place_of = [0, 0, 1, 1]

            def both_ways(table):
                return two_for(table, s_down) + two_for(table, s_up)
        else:
            is_up = (z + d > last).astype(i32)
            place_of = [is_up, is_up]

            def both_ways(table):
                return two_for(table, jnp.where(is_up == 1, s_up, s_down))
        if d == 1:
            theirs = copy_sets(place_of, both_ways(want_opp), [downs[d], ups[d]])
            sets[0] = [opp, with_other(downs[1]), with_other(ups[1]), (stored, local_other)]
            out = pairs_at(0, [theirs], out)
        else:
            theirs, mine = copy_sets(
                place_of * 2, both_ways(want_opp) + both_ways(want), [downs[d], ups[d]], first, [len(place_of)] * 2)
            sets[d - 1] = [with_other(tie(opp, first) if first else opp), with_other(mine)]
            if d + 1 == last:
                sets[d - 1] += [with_other(far_a), with_other(over)]
            out = pairs_at(d - 1, [mine], out)
        opp = across_y(theirs) if d + 1 < last else across_y_inside(theirs)
    sets[last - 1] = [with_other(tie(far_b, [out])), with_other(tie(opp, [out]))]
    return pairs_at(last - 1, [], out)


def solution(mesh):
    in_specs = (
        P(("groups", "orb"), None, "aux"),
        P(("groups", "orb"), None),
        P("groups"),
        P("groups"),
        P(("groups", "orb"), None),
        P(("groups", "orb"), None, None),
    )
    out_specs = P(("groups", "orb", "aux"), None, None)
    return jax.shard_map(
        per_device, mesh=mesh, in_specs=in_specs, out_specs=out_specs, check_vma=False
    )
```

```python
import functools

import jax
import jax.numpy as jnp
from jax import lax
from jax.experimental import pallas as pl
from jax.experimental.pallas import tpu as pltpu
from jax.sharding import PartitionSpec as P

NT = (((1,), (1,)), ((), ()))
VMEM_LIMIT = 63 * 1024 * 1024
EXTRA = 16


def windows(full, kept):
    slack = full - kept
    tile = 256 - slack if 0 <= slack <= 128 else kept
    found = []
    base = 0
    while base < kept:
        rows = min(tile, kept - base)
        found.append((base, rows, rows + slack))
        base += rows
    return found


def pair_kernel(call, wins, n_sets, n_skip, meta_ref, shift_ref, ve1_ref, pick_ref, own_ref, other_ref, *rest):
    sets = [(rest[2 * k], rest[2 * k + 1]) for k in range(n_sets)]
    rest = rest[2 * n_sets + n_skip:]
    (out_ref, first, second, pick, side_a, side_b, e1_buf, out_buf,
     first_sem, second_sem, pick_sem, out_sem) = rest
    pairs_here = out_ref.shape[0]
    kept = out_ref.shape[1]
    half = own_ref.shape[2]
    n_first = first.shape[0]
    lo = meta_ref[0, call]
    hi = meta_ref[0, call + 1]
    base_first = meta_ref[1, 0]

    def first_copies():
        out = []
        for k in range(n_first):
            out.append(pltpu.make_async_copy(
                own_ref.at[base_first + k], first.at[k, :, pl.ds(0, half)], first_sem.at[2 * k]))
            out.append(pltpu.make_async_copy(
                other_ref.at[base_first + k], first.at[k, :, pl.ds(half, half)], first_sem.at[2 * k + 1]))
        return out

    def fetch(i, slot):
        p = meta_ref[2, i]
        which = meta_ref[3, p]
        idx = meta_ref[4, p]
        pltpu.make_async_copy(pick_ref.at[p], pick.at[slot], pick_sem.at[slot]).start()
        for k, (x_own, x_other) in enumerate(sets):
            @pl.when(which == k)
            def _():
                pltpu.make_async_copy(
                    x_own.at[idx], second.at[slot, :, pl.ds(0, half)], second_sem.at[slot, 0]).start()
                pltpu.make_async_copy(
                    x_other.at[idx], second.at[slot, :, pl.ds(half, half)], second_sem.at[slot, 1]).start()

    def await_fetch(slot):
        pltpu.make_async_copy(pick_ref.at[0], pick.at[slot], pick_sem.at[slot]).wait()
        for k in range(2):
            pltpu.make_async_copy(
                sets[0][0].at[0], second.at[slot, :, pl.ds(k * half, half)], second_sem.at[slot, k]).wait()

    def out_copy(p, slot):
        return pltpu.make_async_copy(out_buf.at[slot], out_ref.at[p], out_sem.at[slot])

    @pl.when(hi > lo)
    def _():
        for c in first_copies():
            c.start()
        fetch(lo, lax.rem(lo, 2))
        for c in first_copies():
            c.wait()

    def step(i, carry):
        slot = lax.rem(i, 2)
        p = meta_ref[2, i]
        f = p // (pairs_here // n_first)

        @pl.when(i + 1 < hi)
        def _():
            fetch(i + 1, 1 - slot)

        await_fetch(slot)

        @pl.when(i >= lo + 2)
        def _():
            out_copy(p, slot).wait()

        e2_parts = []
        full = ve1_ref.shape[1]
        for t, (base, rows, span) in enumerate(wins):
            one = pick[slot, 0, base:base + rows, 0:span]
            got = jnp.dot(one, first[f, base:base + span, :], preferred_element_type=jnp.float32)
            side_a[base:base + rows, :] = got.astype(jnp.bfloat16)
            e1_buf[base:base + rows, :] = jnp.dot(
                one, ve1_ref[f, base:base + span, :], preferred_element_type=jnp.float32)
            two = pick[slot, 1, base:base + rows, 0:span]
            got = jnp.dot(two, second[slot, base:base + span, :], preferred_element_type=jnp.float32)
            side_b[base:base + rows, :] = got.astype(jnp.bfloat16)
            ve = second[slot, full:full + EXTRA, 0:span]
            e2_parts.append(
                lax.dot_general(ve, two, NT, preferred_element_type=jnp.float32)[t:t + 1])
        e2 = jnp.concatenate(e2_parts, axis=1)
        shift = shift_ref[p]
        chunk = min(kept, 256)
        for start in range(0, kept, chunk):
            c = lax.dot_general(
                side_a[...], side_b[start:start + chunk, :], NT, preferred_element_type=jnp.float32)
            for col in range(0, chunk, 128):
                den = e1_buf[...] + e2[:, start + col:start + col + 128] - shift
                inv = pl.reciprocal(den, approx=True)
                neg = inv * (den * inv - 2.0)
                out_buf[slot, :, start + col:start + col + 128] = (
                    c[:, col:col + 128] * neg).astype(jnp.bfloat16)
        out_copy(p, slot).start()
        return carry

    lax.fori_loop(lo, hi, step, 0)

    @pl.when(hi - lo >= 2)
    def _():
        out_copy(0, lax.rem(hi, 2)).wait()

    @pl.when(hi > lo)
    def _():
        out_copy(0, lax.rem(hi + 1, 2)).wait()


def run_pairs(call, wins, meta, shift, ve1, pick, own, other, sets, after, prev):
    pairs_here, _, kept, span = pick.shape
    n_first = ve1.shape[0]
    full, half = own.shape[1], own.shape[2]
    any_spec = ANY_SPEC
    smem = pl.BlockSpec(memory_space=pltpu.SMEM)
    vmem = pl.BlockSpec(memory_space=pltpu.VMEM)
    operands = [meta, shift, ve1, pick, own, other]
    for pair in sets:
        operands += list(pair)
    operands += after
    in_specs = [smem, smem, vmem] + [any_spec] * (len(operands) - 3)
    aliases = {}
    if prev is not None:
        aliases = {len(operands): 0}
        operands.append(prev)
        in_specs.append(any_spec)
    bf = jnp.bfloat16
    return pl.pallas_call(
        functools.partial(pair_kernel, call, wins, len(sets), len(after) + (prev is not None)),
        out_shape=jax.ShapeDtypeStruct((pairs_here, kept, kept), bf),
        in_specs=in_specs,
        out_specs=any_spec,
        scratch_shapes=[
            pltpu.VMEM((n_first, full, 2 * half), bf),
            pltpu.VMEM((2, full, 2 * half), bf),
            pltpu.VMEM((2, 2, kept, span), bf),
            pltpu.VMEM((kept, 2 * half), bf),
            pltpu.VMEM((kept, 2 * half), bf),
            pltpu.VMEM((kept, 128), jnp.float32),
            pltpu.VMEM((2, kept, kept), bf),
            pltpu.SemaphoreType.DMA((2 * n_first,)),
            pltpu.SemaphoreType.DMA((2, 2)),
            pltpu.SemaphoreType.DMA((2,)),
            pltpu.SemaphoreType.DMA((2,)),
        ],
        input_output_aliases=aliases,
        compiler_params=pltpu.CompilerParams(vmem_limit_bytes=VMEM_LIMIT),
        cost_estimate=pl.CostEstimate(flops=0, bytes_accessed=0, transcendentals=0),
        name=f"pairs_{call}",
    )(*operands)


def halves(rows):
    cut = rows // 32 * 16
    return [(0, cut), (cut, rows - cut)]


def set_kernel(n_arrays, n_skip, sizes, table_ref, *rest):
    arrays = rest[:n_arrays]
    outs = rest[n_arrays + n_skip:-3]
    held, in_sems, out_sems = rest[-3:]
    places = [(o, k) for o, size in zip(outs, sizes) for k in range(size)]
    cuts = [pl.ds(start, rows) for start, rows in halves(held.shape[1])]
    for j in range(len(places)):
        for k, a in enumerate(arrays):
            @pl.when(table_ref[0, j] == k)
            def _():
                for c, cut in enumerate(cuts):
                    pltpu.make_async_copy(a.at[table_ref[1, j], cut], held.at[j, cut], in_sems.at[j, c]).start()
    for j, (o, k) in enumerate(places):
        for c, cut in enumerate(cuts):
            pltpu.make_async_copy(arrays[0].at[0, cut], held.at[j, cut], in_sems.at[j, c]).wait()
            pltpu.make_async_copy(held.at[j, cut], o.at[k, cut], out_sems.at[j, c]).start()
    for j, (o, k) in enumerate(places):
        for c, cut in enumerate(cuts):
            pltpu.make_async_copy(held.at[j, cut], o.at[k, cut], out_sems.at[j, c]).wait()


ANY_SPEC = pl.BlockSpec(memory_space=pl.ANY)


def copy_sets(which, index, arrays, after=(), sizes=None):
    n = len(index)
    sizes = sizes or [n]
    table = jnp.stack([jnp.stack([jnp.asarray(w, jnp.int32) for w in which]), jnp.stack(index)])
    block = arrays[0].shape[1:]
    outs = pl.pallas_call(
        functools.partial(set_kernel, len(arrays), len(after), sizes),
        out_shape=[jax.ShapeDtypeStruct((size,) + block, arrays[0].dtype) for size in sizes],
        in_specs=[pl.BlockSpec(memory_space=pltpu.SMEM)] + [ANY_SPEC] * (len(arrays) + len(after)),
        out_specs=[ANY_SPEC] * len(sizes),
        scratch_shapes=[
            pltpu.VMEM((n,) + block, arrays[0].dtype),
            pltpu.SemaphoreType.DMA((n, 2)),
            pltpu.SemaphoreType.DMA((n, 2))],
        cost_estimate=pl.CostEstimate(flops=0, bytes_accessed=0, transcendentals=0),
        compiler_params=pltpu.CompilerParams(vmem_limit_bytes=VMEM_LIMIT),
        name="copy_sets",
    )(table, *arrays, *after)
    return outs if len(sizes) > 1 else outs[0]


def extend_kernel(wins, blocks_ref, energy_ref, out_ref, held, in_sems, out_sems):
    count, full, half = blocks_ref.shape
    cuts = halves(full)

    def arrive(k, c):
        rows = pl.ds(*cuts[c])
        return pltpu.make_async_copy(blocks_ref.at[k, rows], held.at[k, rows], in_sems.at[k, c])

    def leave(k, c):
        rows = pl.ds(cuts[c][0], cuts[c][1] + c * EXTRA)
        return pltpu.make_async_copy(held.at[k, rows], out_ref.at[k, rows], out_sems.at[k, c])

    for k in range(count):
        for c in range(2):
            arrive(k, c).start()
    energy = energy_ref[...].astype(jnp.float32)
    span = max(sp for _, _, sp in wins)
    row = lax.broadcasted_iota(jnp.int32, (EXTRA, span), 0)
    for k in range(count):
        held[k, full:, :] = jnp.zeros((EXTRA, half), held.dtype)
        rows = jnp.zeros((EXTRA, span), jnp.float32)
        for t, (base, _, sp) in enumerate(wins):
            piece = energy[k:k + 1, base:base + sp]
            if sp < span:
                piece = jnp.concatenate([piece, jnp.zeros((1, span - sp), jnp.float32)], axis=1)
            rows = jnp.where(row == t, jnp.broadcast_to(piece, (EXTRA, span)), rows)
        held[k, full:, 0:span] = rows.astype(held.dtype)
    for k in range(count):
        for c in range(2):
            arrive(k, c).wait()
            leave(k, c).start()
    for k in range(count):
        for c in range(2):
            leave(k, c).wait()


def extend(blocks, energy, wins):
    count, full, half = blocks.shape
    shape = (count, full + EXTRA, half)
    return pl.pallas_call(
        functools.partial(extend_kernel, wins),
        out_shape=jax.ShapeDtypeStruct(shape, blocks.dtype),
        in_specs=[ANY_SPEC, pl.BlockSpec(memory_space=pltpu.VMEM)],
        out_specs=ANY_SPEC,
        scratch_shapes=[
            pltpu.VMEM(shape, blocks.dtype), pltpu.SemaphoreType.DMA((count, 2)), pltpu.SemaphoreType.DMA((count, 2))],
        compiler_params=pltpu.CompilerParams(vmem_limit_bytes=VMEM_LIMIT),
        name="extend",
    )(blocks, energy)


def tie(x, deps):
    return pl.pallas_call(
        lambda *refs: None,
        out_shape=jax.ShapeDtypeStruct(x.shape, x.dtype),
        in_specs=[ANY_SPEC] * (1 + len(deps)),
        out_specs=ANY_SPEC,
        input_output_aliases={0: 0},
        compiler_params=pltpu.CompilerParams(vmem_limit_bytes=VMEM_LIMIT),
        cost_estimate=pl.CostEstimate(flops=0, bytes_accessed=0, transcendentals=0),
        name="tie",
    )(x, *deps)


def per_device(blocks, virt_energy, occ_energy, owner_slot, pairs, domains):
    orb_count = lax.axis_size("orb")
    aux_count = lax.axis_size("aux")
    occ_dev, full, half = blocks.shape
    pair_dev = pairs.shape[0]
    kept = domains.shape[2]
    own_rows = pair_dev // aux_count
    n_first = occ_dev // aux_count
    core = lax.axis_index("aux")
    o = lax.axis_index("orb")
    z, y = o // 2, o % 2
    chain = orb_count // 2
    last = chain - 1
    n_slots = orb_count * occ_dev
    i32 = jnp.int32
    wins = windows(full, kept)

    swap_aux = [(0, 1), (1, 0)]
    swap_y = [(k, k ^ 1) for k in range(orb_count)]

    def across_y(a):
        return lax.ppermute(a, "orb", swap_y)

    def across_y_inside(a):
        return lax.ppermute(a, "orb", [pair for pair in swap_y if 0 < pair[0] // 2 < last])

    def across_aux(a):
        return lax.ppermute(a, "aux", swap_aux)

    def hop_down(a, d):
        return lax.ppermute(a, "orb", [(k, k - 2) for k in range(2, orb_count) if k // 2 <= chain - d])

    def hop_up(a, d):
        return lax.ppermute(a, "orb", [(k, k + 2) for k in range(orb_count - 2) if k // 2 >= d - 1])

    stored = extend(blocks, virt_energy, wins)

    downs, ups = [stored, hop_down(stored, 1)], [stored, hop_up(stored, 1)]
    local_other = across_aux(stored)

    orbitals = jnp.arange(owner_slot.shape[0], dtype=i32)
    hit_second = pairs[:, 1][:, None] == orbitals[None, :]
    slot_second = jnp.sum(jnp.where(hit_second, owner_slot[None, :], 0), axis=1)
    slots = jnp.arange(n_slots, dtype=i32)
    wanted_flat = jnp.any(slot_second[:, None] == slots[None, :], axis=0).astype(i32)
    wanted_flat = tie(wanted_flat, [stored])
    wanted = wanted_flat.reshape(orb_count, occ_dev) > 0
    wanted_both = jnp.stack([wanted_flat, across_y(wanted_flat)])
    wanted_opp = wanted_both[1].reshape(orb_count, occ_dev) > 0
    local = jnp.arange(occ_dev, dtype=i32)[None, :]

    def two_of(table):
        return jnp.min(jnp.where(table, local, occ_dev - 1), axis=1), jnp.max(jnp.where(table, local, 0), axis=1)

    want, want_opp = two_of(wanted), two_of(wanted_opp)

    first_row = core * own_rows
    own_second = lax.dynamic_slice_in_dim(slot_second, first_row, own_rows, 0)
    own_pairs = lax.dynamic_slice_in_dim(pairs, first_row, own_rows, 0)
    src = own_second // occ_dev
    part = own_second % occ_dev
    rank = jnp.any(
        (slot_second[None, :] // occ_dev == src[:, None]) & (slot_second[None, :] < own_second[:, None]),
        axis=1).astype(i32)
    src_z, src_y = src // 2, src % 2
    dist = jnp.abs(src_z - z)
    is_opp = (src_y != y).astype(i32)
    from_up = src_z < z
    both = 2 * dist <= chain - 1
    is_far = dist == last
    at_hand = (dist <= 1) & (is_opp == 0)
    idx = jnp.where(at_hand, part, rank + jnp.where(both & from_up, 2, 0))
    which_col = jnp.where(dist == 0, 3, jnp.where((dist == 1) & from_up, 2, jnp.where(is_far, 2, 1)))
    at_end = (z == 0) | (z == last)
    is_early = at_end & (dist == last - 1)
    which = jnp.where(is_opp == 1, jnp.where(is_early, 3, is_far.astype(i32)), which_col)
    stage_col = jnp.where(is_far, last - 2, jnp.maximum(dist - 1, 0))
    stage = jnp.where(is_opp == 1, jnp.minimum(dist, last - 1) - is_early.astype(i32), stage_col)
    rows = jnp.arange(own_rows, dtype=i32)
    before = (stage[None, :] < stage[:, None]) | ((stage[None, :] == stage[:, None]) & (rows[None, :] < rows[:, None]))
    place = jnp.sum(before.astype(i32), axis=1)
    order = jnp.sum(jnp.where(place[None, :] == rows[:, None], rows[None, :], 0), axis=1)
    bounds = jnp.sum((stage[None, :] < jnp.arange(chain + 1, dtype=i32)[:, None]).astype(i32), axis=1)
    width = max(own_rows, chain + 1)

    def padded(v):
        v = v.reshape(-1)
        return jnp.pad(v, (0, width - v.shape[0]))

    meta = jnp.stack([padded(bounds), padded(core * n_first), padded(order), padded(which), padded(idx)])

    def occ(col):
        hit = own_pairs[:, col][:, None] == orbitals[None, :]
        return jnp.sum(jnp.where(hit, occ_energy[None, :], 0.0), axis=1)

    shift = occ(0) + occ(1)
    ve1 = lax.dynamic_slice_in_dim(virt_energy, core * n_first, n_first, 0)
    ve1 = jnp.broadcast_to(ve1[:, :, None], (n_first, full, 128))

    dom = lax.dynamic_slice_in_dim(domains, first_row, own_rows, 0)
    base = jnp.concatenate([jnp.full((r,), b, i32) for b, r, _ in wins])
    span = max(sp for _, _, sp in wins)
    pick = ((dom - base)[..., None] == jnp.arange(span, dtype=i32)).astype(jnp.bfloat16)

    def idx_of(table, source):
        return lax.dynamic_index_in_dim(table, jnp.clip(source, 0, orb_count - 1), 0, keepdims=False)

    def two_for(table, source):
        return [idx_of(table[0], source), idx_of(table[1], source)]

    sets = {}

    def pairs_at(d, after, prev):
        return run_pairs(d, wins, meta, shift, ve1, pick, stored, local_other, sets[d], after, prev)

    def with_other(a):
        return a, across_aux(a)

    y_load = copy_sets([0, 0], two_for(want_opp, o), [stored])
    opp = with_other(across_y(y_load))
    top = orb_count - 1
    tell = [(0, 2), (1, 3), (top, top - 2), (top - 1, top - 3)]
    wanted_far = lax.ppermute(tie(wanted_both, [y_load]), "orb", tell).reshape(2, orb_count, occ_dev) > 0
    far_own, far_opp = two_of(wanted_far[0]), two_of(wanted_far[1])
    early = [opp[1], local_other, pick, meta]
    downs[1], ups[1] = tie(downs[1], early), tie(ups[1], early)
    out = None
    for d in range(1, last):
        s_down, s_up = o + 2 * d, o - 2 * d
        first = []
        if d + 1 < last:
            downs.append(hop_down(downs[d], d + 1))
            ups.append(hop_up(ups[d], d + 1))
        else:
            sends_down = z == 1
            source = jnp.where(sends_down, 2 * last + y, y)
            from_set = [1 - sends_down.astype(i32)] * 4
            perm = [(2, 0), (3, 1), (2 * (last - 1), 2 * last), (2 * (last - 1) + 1, 2 * last + 1)]
            over_set = jnp.where(at_end, (z == last).astype(i32), from_set[0])
            end_source = jnp.where(z == 0, s_down, s_up)
            over_pick = [
                jnp.where(at_end, a, b) for a, b in zip(two_for(want_opp, end_source), two_for(far_opp, source))]
            load_over, load_own = copy_sets(
                [over_set] * 2 + from_set[2:], over_pick + two_for(far_own, source), [downs[d], ups[d]], [out], [2, 2])
            over = across_y(load_over)
            far_b = lax.ppermute(over, "orb", perm)
            far_a = lax.ppermute(load_own, "orb", perm)
            first = [load_own]
        if 2 * d <= last:
            place_of = [0, 0, 1, 1]

            def both_ways(table):
                return two_for(table, s_down) + two_for(table, s_up)
        else:
            is_up = (z + d > last).astype(i32)
            place_of = [is_up, is_up]

            def both_ways(table):
                return two_for(table, jnp.where(is_up == 1, s_up, s_down))
        if d == 1:
            theirs = copy_sets(place_of, both_ways(want_opp), [downs[d], ups[d]])
            sets[0] = [opp, with_other(downs[1]), with_other(ups[1]), (stored, local_other)]
            out = pairs_at(0, [theirs], out)
        else:
            theirs, mine = copy_sets(
                place_of * 2, both_ways(want_opp) + both_ways(want), [downs[d], ups[d]], first, [len(place_of)] * 2)
            sets[d - 1] = [with_other(tie(opp, first) if first else opp), with_other(mine)]
            if d + 1 == last:
                sets[d - 1] += [with_other(far_a), with_other(over)]
            out = pairs_at(d - 1, [mine], out)
        opp = across_y(theirs) if d + 1 < last else across_y_inside(theirs)
    sets[last - 1] = [with_other(tie(opp, [out])), with_other(tie(far_b, [out]))]
    return pairs_at(last - 1, [], out)


def solution(mesh):
    in_specs = (
        P(("groups", "orb"), None, "aux"),
        P(("groups", "orb"), None),
        P("groups"),
        P("groups"),
        P(("groups", "orb"), None),
        P(("groups", "orb"), None, None),
    )
    out_specs = P(("groups", "orb", "aux"), None, None)
    return jax.shard_map(
        per_device, mesh=mesh, in_specs=in_specs, out_specs=out_specs, check_vma=False
    )
```

```python
import functools

import jax
import jax.numpy as jnp
from jax import lax
from jax.experimental import pallas as pl
from jax.experimental.pallas import tpu as pltpu
from jax.sharding import PartitionSpec as P

NT = (((1,), (1,)), ((), ()))
VMEM_LIMIT = 63 * 1024 * 1024
EXTRA = 16


def windows(full, kept):
    slack = full - kept
    tile = 256 - slack if 0 <= slack <= 128 else kept
    found = []
    base = 0
    while base < kept:
        rows = min(tile, kept - base)
        found.append((base, rows, rows + slack))
        base += rows
    return found


def pair_kernel(call, wins, n_sets, n_skip, meta_ref, shift_ref, ve1_ref, pick_ref, own_ref, other_ref, *rest):
    sets = [(rest[2 * k], rest[2 * k + 1]) for k in range(n_sets)]
    rest = rest[2 * n_sets + n_skip:]
    (out_ref, first, second, pick, side_a, side_b, e1_buf, out_buf,
     first_sem, second_sem, pick_sem, out_sem) = rest
    pairs_here = out_ref.shape[0]
    kept = out_ref.shape[1]
    half = own_ref.shape[2]
    n_first = first.shape[0]
    lo = meta_ref[0, call]
    hi = meta_ref[0, call + 1]
    base_first = meta_ref[1, 0]

    def first_copies():
        out = []
        for k in range(n_first):
            out.append(pltpu.make_async_copy(
                own_ref.at[base_first + k], first.at[k, :, pl.ds(0, half)], first_sem.at[2 * k]))
            out.append(pltpu.make_async_copy(
                other_ref.at[base_first + k], first.at[k, :, pl.ds(half, half)], first_sem.at[2 * k + 1]))
        return out

    def fetch(i, slot):
        p = meta_ref[2, i]
        which = meta_ref[3, p]
        idx = meta_ref[4, p]
        pltpu.make_async_copy(pick_ref.at[p], pick.at[slot], pick_sem.at[slot]).start()
        for k, (x_own, x_other) in enumerate(sets):
            @pl.when(which == k)
            def _():
                pltpu.make_async_copy(
                    x_own.at[idx], second.at[slot, :, pl.ds(0, half)], second_sem.at[slot, 0]).start()
                pltpu.make_async_copy(
                    x_other.at[idx], second.at[slot, :, pl.ds(half, half)], second_sem.at[slot, 1]).start()

    def await_fetch(slot):
        pltpu.make_async_copy(pick_ref.at[0], pick.at[slot], pick_sem.at[slot]).wait()
        for k in range(2):
            pltpu.make_async_copy(
                sets[0][0].at[0], second.at[slot, :, pl.ds(k * half, half)], second_sem.at[slot, k]).wait()

    def out_copy(p, slot):
        return pltpu.make_async_copy(out_buf.at[slot], out_ref.at[p], out_sem.at[slot])

    @pl.when(hi > lo)
    def _():
        for c in first_copies():
            c.start()
        fetch(lo, lax.rem(lo, 2))
        for c in first_copies():
            c.wait()

    def step(i, carry):
        slot = lax.rem(i, 2)
        p = meta_ref[2, i]
        f = p // (pairs_here // n_first)

        @pl.when(i + 1 < hi)
        def _():
            fetch(i + 1, 1 - slot)

        await_fetch(slot)

        @pl.when(i >= lo + 2)
        def _():
            out_copy(p, slot).wait()

        e2_parts = []
        full = ve1_ref.shape[1]
        for t, (base, rows, span) in enumerate(wins):
            one = pick[slot, 0, base:base + rows, 0:span]
            got = jnp.dot(one, first[f, base:base + span, :], preferred_element_type=jnp.float32)
            side_a[base:base + rows, :] = got.astype(jnp.bfloat16)
            e1_buf[base:base + rows, :] = jnp.dot(
                one, ve1_ref[f, base:base + span, :], preferred_element_type=jnp.float32)
            two = pick[slot, 1, base:base + rows, 0:span]
            got = jnp.dot(two, second[slot, base:base + span, :], preferred_element_type=jnp.float32)
            side_b[base:base + rows, :] = got.astype(jnp.bfloat16)
            ve = second[slot, full:full + EXTRA, 0:span]
            e2_parts.append(
                lax.dot_general(ve, two, NT, preferred_element_type=jnp.float32)[t:t + 1])
        e2 = jnp.concatenate(e2_parts, axis=1)
        shift = shift_ref[p]
        chunk = min(kept, 256)
        for start in range(0, kept, chunk):
            c = lax.dot_general(
                side_a[...], side_b[start:start + chunk, :], NT, preferred_element_type=jnp.float32)
            for col in range(0, chunk, 128):
                den = e1_buf[...] + e2[:, start + col:start + col + 128] - shift
                inv = pl.reciprocal(den, approx=True)
                neg = inv * (den * inv - 2.0)
                out_buf[slot, :, start + col:start + col + 128] = (
                    c[:, col:col + 128] * neg).astype(jnp.bfloat16)
        out_copy(p, slot).start()
        return carry

    lax.fori_loop(lo, hi, step, 0)

    @pl.when(hi - lo >= 2)
    def _():
        out_copy(0, lax.rem(hi, 2)).wait()

    @pl.when(hi > lo)
    def _():
        out_copy(0, lax.rem(hi + 1, 2)).wait()


def run_pairs(call, wins, meta, shift, ve1, pick, own, other, sets, after, prev):
    pairs_here, _, kept, span = pick.shape
    n_first = ve1.shape[0]
    full, half = own.shape[1], own.shape[2]
    any_spec = ANY_SPEC
    smem = pl.BlockSpec(memory_space=pltpu.SMEM)
    vmem = pl.BlockSpec(memory_space=pltpu.VMEM)
    operands = [meta, shift, ve1, pick, own, other]
    for pair in sets:
        operands += list(pair)
    operands += after
    in_specs = [smem, smem, vmem] + [any_spec] * (len(operands) - 3)
    aliases = {}
    if prev is not None:
        aliases = {len(operands): 0}
        operands.append(prev)
        in_specs.append(any_spec)
    bf = jnp.bfloat16
    return pl.pallas_call(
        functools.partial(pair_kernel, call, wins, len(sets), len(after) + (prev is not None)),
        out_shape=jax.ShapeDtypeStruct((pairs_here, kept, kept), bf),
        in_specs=in_specs,
        out_specs=any_spec,
        scratch_shapes=[
            pltpu.VMEM((n_first, full, 2 * half), bf),
            pltpu.VMEM((2, full, 2 * half), bf),
            pltpu.VMEM((2, 2, kept, span), bf),
            pltpu.VMEM((kept, 2 * half), bf),
            pltpu.VMEM((kept, 2 * half), bf),
            pltpu.VMEM((kept, 128), jnp.float32),
            pltpu.VMEM((2, kept, kept), bf),
            pltpu.SemaphoreType.DMA((2 * n_first,)),
            pltpu.SemaphoreType.DMA((2, 2)),
            pltpu.SemaphoreType.DMA((2,)),
            pltpu.SemaphoreType.DMA((2,)),
        ],
        input_output_aliases=aliases,
        compiler_params=pltpu.CompilerParams(vmem_limit_bytes=VMEM_LIMIT),
        cost_estimate=pl.CostEstimate(flops=0, bytes_accessed=0, transcendentals=0),
        name=f"pairs_{call}",
    )(*operands)


def halves(rows):
    cut = rows // 32 * 16
    return [(0, cut), (cut, rows - cut)]


def set_kernel(n_arrays, n_skip, sizes, table_ref, *rest):
    arrays = rest[:n_arrays]
    outs = rest[n_arrays + n_skip:-3]
    held, in_sems, out_sems = rest[-3:]
    places = [(o, k) for o, size in zip(outs, sizes) for k in range(size)]
    cuts = [pl.ds(start, rows) for start, rows in halves(held.shape[1])]
    for j in range(len(places)):
        for k, a in enumerate(arrays):
            @pl.when(table_ref[0, j] == k)
            def _():
                for c, cut in enumerate(cuts):
                    pltpu.make_async_copy(a.at[table_ref[1, j], cut], held.at[j, cut], in_sems.at[j, c]).start()
    for j, (o, k) in enumerate(places):
        for c, cut in enumerate(cuts):
            pltpu.make_async_copy(arrays[0].at[0, cut], held.at[j, cut], in_sems.at[j, c]).wait()
            pltpu.make_async_copy(held.at[j, cut], o.at[k, cut], out_sems.at[j, c]).start()
    for j, (o, k) in enumerate(places):
        for c, cut in enumerate(cuts):
            pltpu.make_async_copy(held.at[j, cut], o.at[k, cut], out_sems.at[j, c]).wait()


ANY_SPEC = pl.BlockSpec(memory_space=pl.ANY)


def copy_sets(which, index, arrays, after=(), sizes=None):
    n = len(index)
    sizes = sizes or [n]
    table = jnp.stack([jnp.stack([jnp.asarray(w, jnp.int32) for w in which]), jnp.stack(index)])
    block = arrays[0].shape[1:]
    outs = pl.pallas_call(
        functools.partial(set_kernel, len(arrays), len(after), sizes),
        out_shape=[jax.ShapeDtypeStruct((size,) + block, arrays[0].dtype) for size in sizes],
        in_specs=[pl.BlockSpec(memory_space=pltpu.SMEM)] + [ANY_SPEC] * (len(arrays) + len(after)),
        out_specs=[ANY_SPEC] * len(sizes),
        scratch_shapes=[
            pltpu.VMEM((n,) + block, arrays[0].dtype),
            pltpu.SemaphoreType.DMA((n, 2)),
            pltpu.SemaphoreType.DMA((n, 2))],
        cost_estimate=pl.CostEstimate(flops=0, bytes_accessed=0, transcendentals=0),
        compiler_params=pltpu.CompilerParams(vmem_limit_bytes=VMEM_LIMIT),
        name="copy_sets",
    )(table, *arrays, *after)
    return outs if len(sizes) > 1 else outs[0]


def extend_kernel(wins, blocks_ref, energy_ref, out_ref, held, in_sems, out_sems):
    count, full, half = blocks_ref.shape
    cuts = halves(full)

    def arrive(k, c):
        rows = pl.ds(*cuts[c])
        return pltpu.make_async_copy(blocks_ref.at[k, rows], held.at[k, rows], in_sems.at[k, c])

    def leave(k, c):
        rows = pl.ds(cuts[c][0], cuts[c][1] + c * EXTRA)
        return pltpu.make_async_copy(held.at[k, rows], out_ref.at[k, rows], out_sems.at[k, c])

    for k in range(count):
        for c in range(2):
            arrive(k, c).start()
    energy = energy_ref[...].astype(jnp.float32)
    span = max(sp for _, _, sp in wins)
    row = lax.broadcasted_iota(jnp.int32, (EXTRA, span), 0)
    for k in range(count):
        held[k, full:, :] = jnp.zeros((EXTRA, half), held.dtype)
        rows = jnp.zeros((EXTRA, span), jnp.float32)
        for t, (base, _, sp) in enumerate(wins):
            piece = energy[k:k + 1, base:base + sp]
            if sp < span:
                piece = jnp.concatenate([piece, jnp.zeros((1, span - sp), jnp.float32)], axis=1)
            rows = jnp.where(row == t, jnp.broadcast_to(piece, (EXTRA, span)), rows)
        held[k, full:, 0:span] = rows.astype(held.dtype)
    for k in range(count):
        for c in range(2):
            arrive(k, c).wait()
            leave(k, c).start()
    for k in range(count):
        for c in range(2):
            leave(k, c).wait()


def extend(blocks, energy, wins):
    count, full, half = blocks.shape
    shape = (count, full + EXTRA, half)
    return pl.pallas_call(
        functools.partial(extend_kernel, wins),
        out_shape=jax.ShapeDtypeStruct(shape, blocks.dtype),
        in_specs=[ANY_SPEC, pl.BlockSpec(memory_space=pltpu.VMEM)],
        out_specs=ANY_SPEC,
        scratch_shapes=[
            pltpu.VMEM(shape, blocks.dtype), pltpu.SemaphoreType.DMA((count, 2)), pltpu.SemaphoreType.DMA((count, 2))],
        compiler_params=pltpu.CompilerParams(vmem_limit_bytes=VMEM_LIMIT),
        name="extend",
    )(blocks, energy)


def tie(x, deps):
    return pl.pallas_call(
        lambda *refs: None,
        out_shape=jax.ShapeDtypeStruct(x.shape, x.dtype),
        in_specs=[ANY_SPEC] * (1 + len(deps)),
        out_specs=ANY_SPEC,
        input_output_aliases={0: 0},
        compiler_params=pltpu.CompilerParams(vmem_limit_bytes=VMEM_LIMIT),
        cost_estimate=pl.CostEstimate(flops=0, bytes_accessed=0, transcendentals=0),
        name="tie",
    )(x, *deps)


def per_device(blocks, virt_energy, occ_energy, owner_slot, pairs, domains):
    orb_count = lax.axis_size("orb")
    aux_count = lax.axis_size("aux")
    occ_dev, full, half = blocks.shape
    pair_dev = pairs.shape[0]
    kept = domains.shape[2]
    own_rows = pair_dev // aux_count
    n_first = occ_dev // aux_count
    core = lax.axis_index("aux")
    o = lax.axis_index("orb")
    z, y = o // 2, o % 2
    chain = orb_count // 2
    last = chain - 1
    n_slots = orb_count * occ_dev
    i32 = jnp.int32
    wins = windows(full, kept)

    swap_aux = [(0, 1), (1, 0)]
    swap_y = [(k, k ^ 1) for k in range(orb_count)]

    def across_y(a):
        return lax.ppermute(a, "orb", swap_y)

    def across_y_inside(a):
        return lax.ppermute(a, "orb", [pair for pair in swap_y if 0 < pair[0] // 2 < last])

    def across_aux(a):
        return lax.ppermute(a, "aux", swap_aux)

    def hop_down(a, d):
        return lax.ppermute(a, "orb", [(k, k - 2) for k in range(2, orb_count) if k // 2 <= chain - d])

    def hop_up(a, d):
        return lax.ppermute(a, "orb", [(k, k + 2) for k in range(orb_count - 2) if k // 2 >= d - 1])

    stored = extend(blocks, virt_energy, wins)

    downs, ups = [stored, hop_down(stored, 1)], [stored, hop_up(stored, 1)]
    local_other = across_aux(stored)

    orbitals = jnp.arange(owner_slot.shape[0], dtype=i32)
    hit_second = pairs[:, 1][:, None] == orbitals[None, :]
    slot_second = jnp.sum(jnp.where(hit_second, owner_slot[None, :], 0), axis=1)
    slots = jnp.arange(n_slots, dtype=i32)
    wanted_flat = jnp.any(slot_second[:, None] == slots[None, :], axis=0).astype(i32)
    wanted_flat = tie(wanted_flat, [stored])
    wanted = wanted_flat.reshape(orb_count, occ_dev) > 0
    wanted_both = jnp.stack([wanted_flat, across_y(wanted_flat)])
    wanted_opp = wanted_both[1].reshape(orb_count, occ_dev) > 0
    local = jnp.arange(occ_dev, dtype=i32)[None, :]

    def two_of(table):
        return jnp.min(jnp.where(table, local, occ_dev - 1), axis=1), jnp.max(jnp.where(table, local, 0), axis=1)

    want, want_opp = two_of(wanted), two_of(wanted_opp)

    first_row = core * own_rows
    own_second = lax.dynamic_slice_in_dim(slot_second, first_row, own_rows, 0)
    own_pairs = lax.dynamic_slice_in_dim(pairs, first_row, own_rows, 0)
    src = own_second // occ_dev
    part = own_second % occ_dev
    rank = jnp.any(
        (slot_second[None, :] // occ_dev == src[:, None]) & (slot_second[None, :] < own_second[:, None]),
        axis=1).astype(i32)
    src_z, src_y = src // 2, src % 2
    dist = jnp.abs(src_z - z)
    is_opp = (src_y != y).astype(i32)
    from_up = src_z < z
    both = 2 * dist <= chain - 1
    is_far = dist == last
    at_hand = (dist <= 1) & (is_opp == 0)
    idx = jnp.where(at_hand, part, rank + jnp.where(both & from_up, 2, 0))
    which_col = jnp.where(dist == 0, 3, jnp.where((dist == 1) & from_up, 2, jnp.where(is_far, 2, 1)))
    at_end = (z == 0) | (z == last)
    is_early = at_end & (dist == last - 1)
    which = jnp.where(is_opp == 1, jnp.where(is_early, 3, is_far.astype(i32)), which_col)
    stage_col = jnp.where(is_far, last - 2, jnp.maximum(dist - 1, 0))
    stage = jnp.where(is_opp == 1, jnp.minimum(dist, last - 1) - is_early.astype(i32), stage_col)
    rows = jnp.arange(own_rows, dtype=i32)
    before = (stage[None, :] < stage[:, None]) | ((stage[None, :] == stage[:, None]) & (rows[None, :] < rows[:, None]))
    place = jnp.sum(before.astype(i32), axis=1)
    order = jnp.sum(jnp.where(place[None, :] == rows[:, None], rows[None, :], 0), axis=1)
    bounds = jnp.sum((stage[None, :] < jnp.arange(chain + 1, dtype=i32)[:, None]).astype(i32), axis=1)
    width = max(own_rows, chain + 1)

    def padded(v):
        v = v.reshape(-1)
        return jnp.pad(v, (0, width - v.shape[0]))

    meta = jnp.stack([padded(bounds), padded(core * n_first), padded(order), padded(which), padded(idx)])

    def occ(col):
        hit = own_pairs[:, col][:, None] == orbitals[None, :]
        return jnp.sum(jnp.where(hit, occ_energy[None, :], 0.0), axis=1)

    shift = occ(0) + occ(1)
    ve1 = lax.dynamic_slice_in_dim(virt_energy, core * n_first, n_first, 0)
    ve1 = jnp.broadcast_to(ve1[:, :, None], (n_first, full, 128))

    dom = lax.dynamic_slice_in_dim(domains, first_row, own_rows, 0)
    base = jnp.concatenate([jnp.full((r,), b, i32) for b, r, _ in wins])
    span = max(sp for _, _, sp in wins)
    pick = ((dom - base)[..., None] == jnp.arange(span, dtype=i32)).astype(jnp.bfloat16)

    def idx_of(table, source):
        return lax.dynamic_index_in_dim(table, jnp.clip(source, 0, orb_count - 1), 0, keepdims=False)

    def two_for(table, source):
        return [idx_of(table[0], source), idx_of(table[1], source)]

    sets = {}

    def pairs_at(d, after, prev):
        return run_pairs(d, wins, meta, shift, ve1, pick, stored, local_other, sets[d], after, prev)

    def across_aux_at_ends(a):
        ends = [k for k in range(orb_count) if k // 2 in (0, last)]
        return lax.ppermute(a, ("orb", "aux"), [(2 * k + c, 2 * k + 1 - c) for k in ends for c in range(2)])

    def with_other(a):
        return a, across_aux(a)

    y_load = copy_sets([0, 0], two_for(want_opp, o), [stored])
    opp = with_other(across_y(y_load))
    top = orb_count - 1
    tell = [(0, 2), (1, 3), (top, top - 2), (top - 1, top - 3)]
    wanted_far = lax.ppermute(tie(wanted_both, [y_load]), "orb", tell).reshape(2, orb_count, occ_dev) > 0
    far_own, far_opp = two_of(wanted_far[0]), two_of(wanted_far[1])
    early = [opp[1], local_other, pick, meta]
    downs[1], ups[1] = tie(downs[1], early), tie(ups[1], early)
    out = None
    for d in range(1, last):
        s_down, s_up = o + 2 * d, o - 2 * d
        first = []
        if d + 1 < last:
            downs.append(hop_down(downs[d], d + 1))
            ups.append(hop_up(ups[d], d + 1))
        else:
            sends_down = z == 1
            source = jnp.where(sends_down, 2 * last + y, y)
            from_set = [1 - sends_down.astype(i32)] * 4
            perm = [(2, 0), (3, 1), (2 * (last - 1), 2 * last), (2 * (last - 1) + 1, 2 * last + 1)]
            over_set = jnp.where(at_end, (z == last).astype(i32), from_set[0])
            end_source = jnp.where(z == 0, s_down, s_up)
            over_pick = [
                jnp.where(at_end, a, b) for a, b in zip(two_for(want_opp, end_source), two_for(far_opp, source))]
            load_over, load_own = copy_sets(
                [over_set] * 2 + from_set[2:], over_pick + two_for(far_own, source), [downs[d], ups[d]], [out], [2, 2])
            over = across_y(load_over)
            far_b = lax.ppermute(over, "orb", perm)
            far_a = lax.ppermute(load_own, "orb", perm)
            first = [load_own]
        if 2 * d <= last:
            place_of = [0, 0, 1, 1]

            def both_ways(table):
                return two_for(table, s_down) + two_for(table, s_up)
        else:
            is_up = (z + d > last).astype(i32)
            place_of = [is_up, is_up]

            def both_ways(table):
                return two_for(table, jnp.where(is_up == 1, s_up, s_down))
        if d == 1:
            theirs = copy_sets(place_of, both_ways(want_opp), [downs[d], ups[d]])
            sets[0] = [opp, with_other(downs[1]), with_other(ups[1]), (stored, local_other)]
            out = pairs_at(0, [theirs], out)
        else:
            theirs, mine = copy_sets(
                place_of * 2, both_ways(want_opp) + both_ways(want), [downs[d], ups[d]], first, [len(place_of)] * 2)
            sets[d - 1] = [with_other(tie(opp, first) if first else opp), with_other(mine)]
            if d + 1 == last:
                sets[d - 1] += [with_other(far_a), (over, across_aux_at_ends(over))]
            out = pairs_at(d - 1, [mine], out)
        opp = across_y(theirs) if d + 1 < last else across_y_inside(theirs)
    sets[last - 1] = [with_other(tie(opp, [out])), with_other(tie(far_b, [out]))]
    return pairs_at(last - 1, [], out)


def solution(mesh):
    in_specs = (
        P(("groups", "orb"), None, "aux"),
        P(("groups", "orb"), None),
        P("groups"),
        P("groups"),
        P(("groups", "orb"), None),
        P(("groups", "orb"), None, None),
    )
    out_specs = P(("groups", "orb", "aux"), None, None)
    return jax.shard_map(
        per_device, mesh=mesh, in_specs=in_specs, out_specs=out_specs, check_vma=False
    )
```
